32 devices in a mesh: batch: 8 (over y, x, core), height: 4 (over z).
Axes of the slice: x: 2, y: 2, z: 4, core: 2. Of those that a mesh axis runs over, the one named last changes fastest.
Arguments:
- images: bfloat16 [192, 32, 32, 1024], P('batch', 'height'), may hold values from -8 to 8
- w_first: bfloat16 [1024, 1024], replicated, may hold values from -0.1875 to 0.1875
- gain_first: float32 [1024], replicated, may hold values from 0.25 to 1.75
- shift_first: float32 [1024], replicated, may hold values from -3 to 3
- w_mid: bfloat16 [3, 3, 32, 1024], replicated, may hold values from -0.375 to 0.375
- gain_mid: float32 [1024], replicated, may hold values from 0.25 to 1.75
- shift_mid: float32 [1024], replicated, may hold values from -3 to 3
- w_last: bfloat16 [1024, 2048], replicated, may hold values from -0.1875 to 0.1875
- gain_last: float32 [2048], replicated, may hold values from 0.25 to 1.75
- shift_last: float32 [2048], replicated, may hold values from -3 to 3
- w_side: bfloat16 [1024, 2048], replicated, may hold values from -0.1875 to 0.1875
- gain_side: float32 [2048], replicated, may hold values from 0.25 to 1.75
- shift_side: float32 [2048], replicated, may hold values from -3 to 3
- cotangent: bfloat16 [192, 16, 16, 2048], P('batch', 'height'), may hold values from -6 to 6
Outputs:
- output: bfloat16 [192, 16, 16, 2048], P('batch', 'height')
- grad_images: bfloat16 [192, 32, 32, 1024], P('batch', 'height')
- grad_first: float32 [1024, 1024], replicated
- grad_gain_first: float32 [1024], replicated
- grad_shift_first: float32 [1024], replicated
- grad_mid: float32 [3, 3, 32, 1024], replicated
- grad_gain_mid: float32 [1024], replicated
- grad_shift_mid: float32 [1024], replicated
- grad_last: float32 [1024, 2048], replicated
- grad_gain_last: float32 [2048], replicated
- grad_shift_last: float32 [2048], replicated
- grad_side: float32 [1024, 2048], replicated
- grad_gain_side: float32 [2048], replicated
- grad_shift_side: float32 [2048], replicated
The draws below stay inside these ranges and needn't reach their ends.
All inputs are finite; a program needn't handle non-finite values.
Results may differ from the reference program's by a relative error of at most 0.0084.
Values may be sent and summed in bfloat16 or wider, within the bound.
A program may use at most 704 MiB of HBM per device.

```python
import math
import jax
import jax.numpy as jnp
from jax import lax

C_IN = 1024
MID = 1024
C_OUT = 2048
GROUPS = 32
H_IN = 32
W_IN = 32
GW = 32
BATCH = 192


def draw_images(key, part):
    first_key = jax.random.fold_in(key, 0)
    image_rank = jnp.arange(BATCH, dtype=jnp.float32) / max(BATCH - 1, 1)
    row_rank = jnp.arange(H_IN, dtype=jnp.float32) / max(H_IN - 1, 1)
    scales = (0.6 * jnp.exp(math.log(3.0) * image_rank))[:, None, None, None] * (0.8 + 0.8 * row_rank)[None, :, None, None]
    values = jax.random.normal(first_key, (BATCH, H_IN, W_IN, C_IN), jnp.float32) * scales
    return jnp.clip(values, -8.0, 8.0).astype(jnp.bfloat16)


def levels(own_key, dims, shards, least, high):
    def one(dim, blocks):
        heights = jax.random.uniform(jax.random.fold_in(jax.random.fold_in(own_key, 6), dim), (blocks,), jnp.float32, least / len(shards), high / len(shards))
        return jnp.repeat(jnp.exp(heights), dims[dim] // blocks).reshape((-1,) + (1,) * (len(dims) - dim - 1))

    loudness = one(*shards[0])
    for cut in shards[1:]:
        loudness = loudness * one(*cut)
    return loudness


def normal_values(rng, dims, deviation, most, cuts=(), kind=jnp.bfloat16):
    drawn = deviation * jax.random.normal(rng, dims, jnp.float32)
    if cuts:
        drawn = drawn * levels(rng, dims, cuts, -0.22, 0.18)
    return jnp.clip(drawn, -most, most).astype(kind)


def setup_inputs(seed: int = 0) -> dict:
    arg_keys = jax.random.split(jax.random.key(seed), 15)
    return {
        "images": draw_images(jax.random.fold_in(arg_keys[14], 71), 0),
        "w_first": normal_values(arg_keys[1], (C_IN, MID), C_IN ** -0.5, 0.1875),
        "gain_first": jnp.clip(1.0 + 0.15 * jax.random.normal(arg_keys[2], (MID,), jnp.float32), 0.25, 1.75),
        "shift_first": normal_values(arg_keys[3], (MID,), 0.5, 3.0, (), jnp.float32),
        "w_mid": normal_values(arg_keys[4], (3, 3, GW, MID), (9 * GW) ** -0.5, 0.375),
        "gain_mid": jnp.clip(1.0 + 0.15 * jax.random.normal(arg_keys[5], (MID,), jnp.float32), 0.25, 1.75),
        "shift_mid": normal_values(arg_keys[6], (MID,), 0.5, 3.0, (), jnp.float32),
        "w_last": normal_values(arg_keys[7], (MID, C_OUT), MID ** -0.5, 0.1875),
        "gain_last": jnp.clip(1.0 + 0.15 * jax.random.normal(arg_keys[8], (C_OUT,), jnp.float32), 0.25, 1.75),
        "shift_last": normal_values(arg_keys[9], (C_OUT,), 0.5, 3.0, (), jnp.float32),
        "w_side": normal_values(arg_keys[10], (C_IN, C_OUT), C_IN ** -0.5, 0.1875),
        "gain_side": jnp.clip(1.0 + 0.15 * jax.random.normal(arg_keys[11], (C_OUT,), jnp.float32), 0.25, 1.75),
        "shift_side": normal_values(arg_keys[12], (C_OUT,), 0.5, 3.0, (), jnp.float32),
        "cotangent": normal_values(arg_keys[13], (BATCH, H_IN // 2, W_IN // 2, C_OUT), 1.0, 6.0, ((0, 8), (1, 4))),
    }


EPSILON = 1e-05
PRECISE = lax.Precision.HIGHEST

@jax.custom_vjp
def low(v):
    return lax.optimization_barrier(v.astype(jnp.bfloat16)).astype(jnp.float32)

@jax.custom_vjp
def low_back(v):
    return v

def low_keep(v):
    return (low(v), None)

def low_pass(kept, grad):
    return (grad,)

def back_keep(v):
    return (v, None)

def back_low(kept, grad):
    return (low(grad),)
low.defvjp(low_keep, low_pass)
low_back.defvjp(back_keep, back_low)

def batch_norm(values, gain_vec, shift_vec):
    average = lax.optimization_barrier(jnp.mean(values, axis=(0, 1, 2)))
    meansq = lax.optimization_barrier(jnp.mean(values * values, axis=(0, 1, 2)))
    inverse = lax.rsqrt(meansq - average * average + EPSILON)
    return gain_vec * (values - average) * inverse + shift_vec

def grouped(active, kernel):
    img_total = active.shape[0]
    rows_out = active.shape[1] // 2
    cols_out = active.shape[2] // 2
    padded = jnp.pad(active, ((0, 0), (1, 1), (1, 1), (0, 0)))
    result = jnp.zeros((img_total, rows_out, cols_out, GROUPS, GW), jnp.float32)
    for tap_row in range(3):
        for tap_col in range(3):
            window = padded[:, tap_row:tap_row + 2 * rows_out:2, tap_col:tap_col + 2 * cols_out:2, :]
            window = window.reshape(img_total, rows_out, cols_out, GROUPS, GW)
            weights = kernel[tap_row, tap_col].reshape(GW, GROUPS, GW)
            result = result + jnp.einsum('bhwgc,cgo->bhwgo', window, weights, precision=PRECISE)
    return result.reshape(img_total, rows_out, cols_out, MID)

def forward(image_f, first_w, first_gain, first_shift, mid_w, mid_gain, mid_shift, last_w, last_gain, last_shift, side_w, side_gain, side_shift):
    first_pre = low_back(jnp.einsum('bhwc,cm->bhwm', image_f, first_w, precision=PRECISE))
    first_act = low(jax.nn.silu(batch_norm(first_pre, first_gain, first_shift)))
    mid_pre = low_back(grouped(first_act, mid_w))
    mid_act = low(jax.nn.silu(batch_norm(mid_pre, mid_gain, mid_shift)))
    last_pre = low_back(jnp.einsum('bhwm,mo->bhwo', mid_act, last_w, precision=PRECISE))
    side_in = image_f[:, ::2, ::2, :]
    side_pre = low_back(jnp.einsum('bhwc,co->bhwo', side_in, side_w, precision=PRECISE))
    summed = batch_norm(last_pre, last_gain, last_shift) + batch_norm(side_pre, side_gain, side_shift)
    return jax.nn.silu(summed)

def reference(images, w_first, gain_first, shift_first, w_mid, gain_mid, shift_mid, w_last, gain_last, shift_last, w_side, gain_side, shift_side, cotangent):
    inputs = [images, w_first, gain_first, shift_first, w_mid, gain_mid, shift_mid, w_last, gain_last, shift_last, w_side, gain_side, shift_side]
    inputs = [item.astype(jnp.float32) for item in inputs]
    result, pullback = jax.vjp(forward, *inputs)
    gradients = pullback(cotangent.astype(jnp.float32).astype(result.dtype))
    return (result.astype(jnp.bfloat16), gradients[0].astype(jnp.bfloat16), gradients[1].astype(jnp.float32), gradients[2].astype(jnp.float32), gradients[3].astype(jnp.float32), gradients[4].astype(jnp.float32), gradients[5].astype(jnp.float32), gradients[6].astype(jnp.float32), gradients[7].astype(jnp.float32), gradients[8].astype(jnp.float32), gradients[9].astype(jnp.float32), gradients[10].astype(jnp.float32), gradients[11].astype(jnp.float32), gradients[12].astype(jnp.float32))
```

```python
import functools

import jax
import jax.numpy as jnp
from jax import lax
from jax.experimental import pallas as pl
from jax.experimental.pallas import tpu as pltpu
from jax.sharding import PartitionSpec as P

EPSILON = 1e-05
LANES = 128
CHUNK = 256
BF16 = jnp.bfloat16
F32 = jnp.float32
MIB = 1 << 20


def dot(a, b):
    return jnp.dot(a, b, preferred_element_type=F32)


def dot_nt(a, b):
    return lax.dot_general(a, b, (((1,), (1,)), ((), ())), preferred_element_type=F32)


def dot_tn(a, b):
    return lax.dot_general(a, b, (((0,), (0,)), ((), ())), preferred_element_type=F32)


def fold(values):
    rows, cols = values.shape
    return jnp.sum(values.reshape(rows // 8, 8, cols), axis=0)


def put_row(ref, first, row):
    for k in range(row.shape[1] // LANES):
        ref[first + k : first + k + 1, :] = row[:, k * LANES : (k + 1) * LANES]


def get_row(values, first, width):
    count = width // LANES
    return jnp.concatenate([values[first + k : first + k + 1, :] for k in range(count)], axis=1)


def sums_out(ref, *partials):
    first = 0
    for part in partials:
        row = jnp.sum(part, axis=0, keepdims=True)
        put_row(ref, first, row)
        first += row.shape[1] // LANES


def whole(shape):
    return pl.BlockSpec(shape, lambda *_: (0,) * len(shape), pipeline_mode=pl.Buffered(1))


def rows_spec(rows, cols):
    return pl.BlockSpec((rows, cols), lambda i: (i, 0))


def call(body, name, grid, in_specs, out_specs, out_shape, scratch=(), flops=0, moved=0, vmem=56):
    return pl.pallas_call(
        body,
        name=name,
        grid=grid,
        in_specs=in_specs,
        out_specs=out_specs,
        out_shape=out_shape,
        scratch_shapes=list(scratch),
        compiler_params=pltpu.CompilerParams(vmem_limit_bytes=vmem * MIB),
        cost_estimate=pl.CostEstimate(flops=flops, bytes_accessed=moved, transcendentals=0),
    )


def shape(dims, kind=F32):
    return jax.ShapeDtypeStruct(dims, kind)


def exchange_body(epilogue, outs, in_ref, *rest):
    n_par = len(rest) - outs - 6
    params = rest[:n_par]
    out_refs = rest[n_par : n_par + outs]
    got_b, got_h, send_b, recv_b, send_h, recv_h = rest[n_par + outs :]
    size_b, size_h = got_b.shape[0], got_h.shape[0]
    me_b, me_h = lax.axis_index("batch"), lax.axis_index("height")
    barrier = pltpu.get_barrier_semaphore()
    peers = [(lax.rem(me_b + k, size_b), me_h) for k in range(1, size_b)]
    peers_h = [(me_b, lax.rem(me_h + k, size_h)) for k in range(1, size_h)]
    for peer in peers + peers_h:
        pl.semaphore_signal(barrier, inc=1, device_id=peer, device_id_type=pl.DeviceIdType.MESH)
    pl.semaphore_wait(barrier, len(peers) + len(peers_h))

    def spread(src, got, me, targets, size, send, recv):
        copies = []
        for k, peer in enumerate(targets):
            copy = pltpu.make_async_remote_copy(
                src_ref=src,
                dst_ref=got.at[me],
                send_sem=send.at[k],
                recv_sem=recv.at[me],
                device_id=peer,
                device_id_type=pl.DeviceIdType.MESH,
            )
            copy.start()
            copies.append(copy)
        for k, peer in enumerate(targets):
            other = lax.rem(me + (size - 1 - k), size)
            pltpu.make_async_remote_copy(
                src_ref=src,
                dst_ref=got.at[other],
                send_sem=send.at[k],
                recv_sem=recv.at[other],
                device_id=peer,
                device_id_type=pl.DeviceIdType.MESH,
            ).wait_recv()
        total = got[0]
        for k in range(1, size):
            total = total + got[k]
        return total, copies

    got_b[me_b] = in_ref[...]
    part, copies_b = spread(in_ref, got_b, me_b, peers, size_b, send_b, recv_b)
    got_h[me_h] = part
    total, copies_h = spread(got_h.at[me_h], got_h, me_h, peers_h, size_h, send_h, recv_h)
    epilogue(total, params, out_refs)
    for copy in copies_b + copies_h:
        copy.wait_send()


def exchange(sums, params, epilogue, out_shape, ident):
    rows = sums.shape[0]
    size_b, size_h = lax.axis_size("batch"), lax.axis_size("height")
    vmem = pl.BlockSpec(memory_space=pltpu.VMEM)
    return pl.pallas_call(
        functools.partial(exchange_body, epilogue, len(out_shape)),
        name="exchange_%d" % ident,
        in_specs=[vmem] * (1 + len(params)),
        out_specs=[vmem] * len(out_shape),
        out_shape=out_shape,
        scratch_shapes=[
            pltpu.VMEM((size_b, rows, LANES), F32),
            pltpu.VMEM((size_h, rows, LANES), F32),
            pltpu.SemaphoreType.DMA((size_b - 1,)),
            pltpu.SemaphoreType.DMA((size_b,)),
            pltpu.SemaphoreType.DMA((size_h - 1,)),
            pltpu.SemaphoreType.DMA((size_h,)),
        ],
        compiler_params=pltpu.CompilerParams(collective_id=ident, has_side_effects=True),
        cost_estimate=pl.CostEstimate(flops=1000, bytes_accessed=100000, transcendentals=0),
    )(sums, *params)


def norm_terms(total, first, width, cells):
    average = get_row(total, first, width) * (1.0 / cells)
    meansq = get_row(total, first + width // LANES, width) * (1.0 / cells)
    inverse = lax.rsqrt(meansq - average * average + EPSILON)
    return inverse, -average * inverse


def fill(ref, rows):
    for k, row in enumerate(rows):
        ref[k : k + 1, :] = row
    ref[len(rows) :, :] = jnp.zeros((8 - len(rows), ref.shape[1]), F32)


def act_rows(inverse, offset, gain, shift):
    return [
        inverse,
        offset,
        0.5 * gain,
        0.5 * shift,
        0.5 * gain * inverse,
        0.5 * (shift + gain * offset),
    ]


def first_totals(cells_in, cells_out, width, wide, total, params, outs):
    gain, shift = params[0][0:1, :], params[0][1:2, :]
    fill(outs[0], act_rows(*norm_terms(total, 0, width, cells_in), gain, shift))
    fill(outs[1], list(norm_terms(total, 2 * width // LANES, wide, cells_out)))


def mid_totals(cells_out, width, total, params, outs):
    gain, shift = params[0][2:3, :], params[0][3:4, :]
    fill(outs[0], act_rows(*norm_terms(total, 0, width, cells_out), gain, shift))


def last_totals(cells_out, wide, total, params, outs):
    wides, side = params
    inverse, offset = norm_terms(total, 0, wide, cells_out)
    fill(
        outs[0],
        [
            inverse,
            offset,
            side[0:1, :],
            side[1:2, :],
            0.5 * wides[0:1, :],
            0.5 * wides[2:3, :],
            0.5 * (wides[1:2, :] + wides[3:4, :]),
        ],
    )


def back_rows(gain, inverse, total_up, cross, cells):
    scale = gain * inverse
    return [0.5 * scale, -scale * total_up * (1.0 / cells), -scale * cross * (1.0 / cells)]


def out_totals(cells_out, wide, total, params, outs):
    coef = params[0]
    step = wide // LANES
    total_up, last_cross, side_cross = [
        0.5 * get_row(total, k * step, wide) for k in range(3)
    ]
    fill(
        outs[0],
        back_rows(2.0 * coef[4:5, :], coef[0:1, :], total_up, last_cross, cells_out)
        + back_rows(2.0 * coef[5:6, :], coef[2:3, :], total_up, side_cross, cells_out),
    )
    fill(outs[1], [total_up, last_cross, side_cross])


def inner_totals(cells, width, total, params, outs):
    coef = params[0]
    total_up = 0.5 * get_row(total, 0, width)
    cross = 0.5 * get_row(total, width // LANES, width)
    fill(outs[0], back_rows(2.0 * coef[2:3, :], coef[0:1, :], total_up, cross, cells))
    fill(outs[1], [total_up, cross])


def half_silu(half):
    return half + half * jnp.tanh(half)


def slope_twice(half, th):
    return (1.0 + th) * (1.0 + half * (1.0 - th))


def first_body(per, px, q, img, perm, w1, ws, xp, pre, side, stat, acc, acc_s):
    step = pl.program_id(0)
    mid, wide = w1.shape[1], ws.shape[1]

    @pl.when(step == 0)
    def _():
        acc[...] = jnp.zeros_like(acc)
        acc_s[...] = jnp.zeros_like(acc_s)

    for k in range(per):
        flat = img[k].reshape(px, img.shape[3])
        moved = dot(perm[...], flat).astype(BF16)
        xp[k * px : (k + 1) * px, :] = moved
        for c in range(0, mid, CHUNK):
            cols = slice(c, c + CHUNK)
            part = dot(moved, w1[:, cols])
            pre[k * px : (k + 1) * px, cols] = part
            acc[0:8, cols] += fold(part)
            acc[8:16, cols] += fold(part * part)
    even = jnp.concatenate([xp[k * px : k * px + q, :] for k in range(per)], axis=0)
    for c in range(0, wide, CHUNK):
        cols = slice(c, c + CHUNK)
        part = dot(even, ws[:, cols])
        side[:, cols] = part
        acc_s[0:8, cols] += fold(part)
        acc_s[8:16, cols] += fold(part * part)

    @pl.when(step == pl.num_programs(0) - 1)
    def _():
        sums_out(stat, acc[0:8, :], acc[8:16, :], acc_s[0:8, :], acc_s[8:16, :])


def conv_body(per, px, q, pre, halo, flag, w1, perm, coef, wbd, mid, stat, a00, a01, a10, a11, acc):
    step = pl.program_id(0)
    width = w1.shape[1]

    @pl.when(step == 0)
    def _():
        acc[...] = jnp.zeros_like(acc)

    scale, offset = coef[4:5, :], coef[5:6, :]
    flat = halo[...].reshape(per * 32, halo.shape[2])
    rim = dot(dot(perm[...], flat).astype(BF16), w1[...])
    rim = (half_silu(rim * scale + offset) * flag[0]).astype(BF16)
    rim = rim.reshape(per, 2, 16, width)
    a10[:, 0:16, :] = rim[:, 0]
    a11[:, 0:16, :] = rim[:, 1]
    for plane, ref, top in ((0, a00, 0), (1, a01, 0), (2, a10, 16), (3, a11, 16)):
        half = pre[:, plane] * scale[None] + offset[None]
        ref[:, top : top + q, :] = half_silu(half).astype(BF16)
    rows = per * q
    first_col = lax.broadcasted_iota(jnp.int32, (rows, CHUNK), 0) % 16 == 0
    for c in range(0, width, CHUNK):
        cols = slice(c, c + CHUNK)

        def tap(ref, top, row, col):
            return dot(ref[:, top : top + q, cols].reshape(rows, CHUNK), wbd[row * 3 + col, :, cols])

        straight = (
            tap(a00, 0, 1, 1)
            + tap(a01, 0, 1, 2)
            + tap(a10, 16, 2, 1)
            + tap(a11, 16, 2, 2)
            + tap(a10, 0, 0, 1)
            + tap(a11, 0, 0, 2)
        )
        moved = tap(a01, 0, 1, 0) + tap(a11, 16, 2, 0) + tap(a11, 0, 0, 0)
        part = straight + jnp.where(first_col, 0.0, pltpu.roll(moved, 1, 0))
        mid[:, cols] = part
        acc[0:8, cols] += fold(part)
        acc[8:16, cols] += fold(part * part)

    @pl.when(step == pl.num_programs(0) - 1)
    def _():
        sums_out(stat, acc[0:8, :], acc[8:16, :])


def last_body(mid, coef, w, act, pre, stat, acc):
    step = pl.program_id(0)

    @pl.when(step == 0)
    def _():
        acc[...] = jnp.zeros_like(acc)

    half = mid[...] * coef[4:5, :] + coef[5:6, :]
    act[...] = half_silu(half).astype(BF16)
    for c in range(0, w.shape[1], CHUNK):
        cols = slice(c, c + CHUNK)
        part = dot(act[...], w[:, cols])
        pre[:, cols] = part
        acc[0:8, cols] += fold(part)
        acc[8:16, cols] += fold(part * part)

    @pl.when(step == pl.num_programs(0) - 1)
    def _():
        sums_out(stat, acc[0:8, :], acc[8:16, :])


def out_parts(last, side, cot, coef, cols):
    last_normed = last[:, cols] * coef[0:1, cols] + coef[1:2, cols]
    side_normed = side[:, cols] * coef[2:3, cols] + coef[3:4, cols]
    half = last_normed * coef[4:5, cols] + side_normed * coef[5:6, cols] + coef[6:7, cols]
    th = jnp.tanh(half)
    up = cot[:, cols].astype(F32) * slope_twice(half, th)
    return last_normed, side_normed, half, th, up


def out_body(last, side, cot, coef, out, stat, acc):
    step = pl.program_id(0)

    @pl.when(step == 0)
    def _():
        acc[...] = jnp.zeros_like(acc)

    for c in range(0, last.shape[1], CHUNK):
        cols = slice(c, c + CHUNK)
        last_normed, side_normed, half, th, up = out_parts(last, side, cot, coef, cols)
        out[:, cols] = (half + half * th).astype(BF16)
        acc[0:8, cols] += fold(up)
        acc[8:16, cols] += fold(up * last_normed)
        acc[16:24, cols] += fold(up * side_normed)

    @pl.when(step == pl.num_programs(0) - 1)
    def _():
        sums_out(stat, acc[0:8, :], acc[8:16, :], acc[16:24, :])


def tail_body(per, q, last, side, cot, coef, back, act, even, lg, sg, g_last, g_side, acc_l, acc_s):
    step = pl.program_id(0)

    @pl.when(step == 0)
    def _():
        acc_l[...] = jnp.zeros_like(acc_l)
        acc_s[...] = jnp.zeros_like(acc_s)

    flat = even[...].reshape(per * q, even.shape[3])
    for c in range(0, last.shape[1], CHUNK):
        cols = slice(c, c + CHUNK)
        last_normed, side_normed, _, _, up = out_parts(last, side, cot, coef, cols)
        down = (up * back[0:1, cols] + back[1:2, cols] + last_normed * back[2:3, cols]).astype(BF16)
        lg[:, cols] = down
        acc_l[:, cols] += dot_tn(act[...], down)
        down = (up * back[3:4, cols] + back[4:5, cols] + side_normed * back[5:6, cols]).astype(BF16)
        sg[:, cols] = down
        acc_s[:, cols] += dot_tn(flat, down)

    @pl.when(step == pl.num_programs(0) - 1)
    def _():
        g_last[...] = acc_l[...].astype(BF16)
        g_side[...] = acc_s[...].astype(BF16)


def mid_back_body(lg, sg, wl, ws, mid, coef, up, side_back, stat, acc):
    step = pl.program_id(0)

    @pl.when(step == 0)
    def _():
        acc[...] = jnp.zeros_like(acc)

    for c in range(0, mid.shape[1], CHUNK):
        cols = slice(c, c + CHUNK)
        part = dot_nt(lg[...], wl[cols, :])
        normed = mid[:, cols] * coef[0:1, cols] + coef[1:2, cols]
        half = normed * coef[2:3, cols] + coef[3:4, cols]
        part = part * slope_twice(half, jnp.tanh(half))
        up[:, cols] = part
        acc[0:8, cols] += fold(part)
        acc[8:16, cols] += fold(part * normed)
        side_back[:, cols] = dot_nt(sg[...], ws[cols, :])

    @pl.when(step == pl.num_programs(0) - 1)
    def _():
        sums_out(stat, acc[0:8, :], acc[8:16, :])


def conv_back_body(
    per, px, q, mup, mid, halo, pre, coef2, back, coef, wbd, up, g_mid, stat, mg, mgs, acc, acc_g
):
    step = pl.program_id(0)
    width = mid.shape[1]
    rows = per * q

    @pl.when(step == 0)
    def _():
        acc[...] = jnp.zeros_like(acc)
        acc_g[...] = jnp.zeros_like(acc_g)

    ext = q + 16
    last_col = lax.broadcasted_iota(jnp.int32, (rows, CHUNK), 0) % 16 == 15
    last_rim = lax.broadcasted_iota(jnp.int32, (per * 16, CHUNK), 0) % 16 == 15
    for c in range(0, width, CHUNK):
        cols = slice(c, c + CHUNK)
        normed = mid[:, cols] * coef2[0:1, cols] + coef2[1:2, cols]
        grad = (mup[:, cols] * back[0:1, cols] + back[1:2, cols] + normed * back[2:3, cols]).astype(BF16)
        mg[:, 0:q, cols] = grad.reshape(per, q, CHUNK)
        grad = pltpu.roll(grad.astype(F32), rows - 1, 0)
        mgs[:, 0:q, cols] = jnp.where(last_col, 0.0, grad).astype(BF16).reshape(per, q, CHUNK)
        rim = halo[:, :, cols]
        mg[:, q:ext, cols] = rim
        rim = pltpu.roll(rim.reshape(per * 16, CHUNK).astype(F32), per * 16 - 1, 0)
        mgs[:, q:ext, cols] = jnp.where(last_rim, 0.0, rim).astype(BF16).reshape(per, 16, CHUNK)
        views = [ref[:, top : top + q, cols].reshape(rows, CHUNK) for top in (0, 16) for ref in (mg, mgs)]
        plans = (
            (0, ((1, 1, 0),)),
            (1, ((1, 2, 0), (1, 0, 1))),
            (2, ((2, 1, 0), (0, 1, 2))),
            (3, ((2, 2, 0), (2, 0, 1), (0, 2, 2), (0, 0, 3))),
        )
        for plane, taps in plans:
            total = None
            for row, col, view in taps:
                part = dot_nt(views[view], wbd[row * 3 + col, :, cols])
                total = part if total is None else total + part
            normed = pre[:, plane, :, cols].reshape(rows, CHUNK) * coef[0:1, cols] + coef[1:2, cols]
            half = normed * coef[2:3, cols] + coef[3:4, cols]
            th = jnp.tanh(half)
            act = (half + half * th).astype(BF16)
            total = total * slope_twice(half, th)
            up[:, plane, :, cols] = total.reshape(per, q, CHUNK)
            acc[0:8, cols] += fold(total)
            acc[8:16, cols] += fold(total * normed)
            for row, col, view in taps:
                acc_g[row * 3 + col, :, cols] += dot_tn(act, views[view])

    @pl.when(step == pl.num_programs(0) - 1)
    def _():
        sums_out(stat, acc[0:8, :], acc[8:16, :])
        group = (lax.broadcasted_iota(jnp.int32, (32, width), 1) % CHUNK) // 32
        for tap in range(9):
            total = jnp.zeros((32, width), F32)
            for g in range(CHUNK // 32):
                total = total + jnp.where(group == g, acc_g[tap, g * 32 : (g + 1) * 32, :], 0.0)
            g_mid[tap] = total.astype(BF16)


def first_back_body(up, pre, coef, back, xp, fg, g_first, acc):
    step = pl.program_id(0)

    @pl.when(step == 0)
    def _():
        acc[...] = jnp.zeros_like(acc)

    for c in range(0, up.shape[1], CHUNK):
        cols = slice(c, c + CHUNK)
        normed = pre[:, cols] * coef[0:1, cols] + coef[1:2, cols]
        down = (up[:, cols] * back[0:1, cols] + back[1:2, cols] + normed * back[2:3, cols]).astype(BF16)
        fg[:, cols] = down
        acc[:, cols] += dot_tn(xp[...], down)

    @pl.when(step == pl.num_programs(0) - 1)
    def _():
        g_first[...] = acc[...].astype(BF16)


def image_back_body(per, px, q, fg, w1, side_back, perm, out):
    cin = w1.shape[0]
    for k in range(per):
        for c in range(0, cin, CHUNK):
            cols = slice(c, c + CHUNK)
            part = dot_nt(fg[k * px : (k + 1) * px, :], w1[cols, :])
            even = part[0:q] + side_back[k * q : (k + 1) * q, cols]
            part = jnp.concatenate([even, part[q:]], axis=0).astype(BF16)
            part = dot_tn(perm[...], part).astype(BF16)
            out[k, :, :, cols] = part.reshape(out.shape[1], out.shape[2], CHUNK)


def flip(axis, bit):
    return [(i, i ^ (1 << bit)) for i in range(lax.axis_size(axis))]


def halve(part, axis, bit):
    mine = (lax.axis_index(axis) >> bit) & 1
    half = part.shape[0] // 2
    send = lax.dynamic_slice_in_dim(part, (1 - mine) * half, half, 0)
    got = lax.ppermute(send, axis, flip(axis, bit))
    keep = lax.dynamic_slice_in_dim(part, mine * half, half, 0)
    return (keep.astype(F32) + got.astype(F32)).astype(BF16)


def double(part, axis, bit):
    mine = (lax.axis_index(axis) >> bit) & 1
    got = lax.ppermute(part, axis, flip(axis, bit))
    return jnp.concatenate([jnp.where(mine == 1, got, part), jnp.where(mine == 1, part, got)], axis=0)


def orders():
    bits_b = lax.axis_size("batch").bit_length() - 1
    bits_h = lax.axis_size("height").bit_length() - 1
    near = [("batch", 0)]
    across = [("batch", k) for k in range(1, bits_b)]
    half = len(across) // 2
    x_bits, y_bits = across[:half], across[half:]
    z_bits = [("height", k) for k in range(bits_h)]
    return [near + x_bits + y_bits + z_bits, near + y_bits + z_bits + x_bits, near + z_bits + x_bits + y_bits]


def sum_all(parts):
    totals = []
    for part, order in zip(parts, orders()):
        for axis, bit in order:
            part = halve(part, axis, bit)
        for axis, bit in reversed(order):
            part = double(part, axis, bit)
        totals.append(part)
    return totals


def split_sum(rows_2d):
    count = rows_2d.shape[0]
    unit = lax.axis_size("batch") * lax.axis_size("height") * 16
    cuts = [0]
    for k in range(3):
        cuts.append(min(count, cuts[-1] + -(-(count - cuts[-1]) // ((3 - k) * unit)) * unit))
    parts = [rows_2d[a:b] for a, b in zip(cuts, cuts[1:]) if b > a]
    return jnp.concatenate(sum_all(parts), axis=0)


def per_device(
    images,
    w_first,
    gain_first,
    shift_first,
    w_mid,
    gain_mid,
    shift_mid,
    w_last,
    gain_last,
    shift_last,
    w_side,
    gain_side,
    shift_side,
    cotangent,
):
    n, rows_in, cols_in, cin = images.shape
    mid = w_first.shape[1]
    wide = w_last.shape[1]
    gw = w_mid.shape[2]
    rows_out, cols_out = rows_in // 2, cols_in // 2
    px, q = rows_in * cols_in, rows_out * cols_out
    devices = lax.axis_size("batch") * lax.axis_size("height")
    cells_in = float(n * px * devices)
    cells_out = float(n * q * devices)
    size_h = lax.axis_size("height")
    per = 4
    steps = n // per
    rows = per * q

    halo_x = lax.ppermute(images[:, rows_in - 1], "height", [(i, i + 1) for i in range(size_h - 1)])

    narrow = jnp.stack([gain_first, shift_first, gain_mid, shift_mid] + [jnp.zeros_like(gain_mid)] * 4)
    wides = jnp.stack([gain_last, shift_last, gain_side, shift_side] + [jnp.zeros_like(gain_last)] * 4)
    flag = (lax.axis_index("height") > 0).astype(F32).reshape(1)
    tiled = jnp.tile(w_mid.reshape(9, 1, gw, mid), (1, CHUNK // gw, 1, 1))
    same = (
        lax.broadcasted_iota(jnp.int32, (CHUNK // gw, gw, mid), 0)
        == (lax.broadcasted_iota(jnp.int32, (CHUNK // gw, gw, mid), 2) % CHUNK) // gw
    )
    wbd = jnp.where(same[None], tiled, 0).reshape(9, CHUNK, mid).astype(BF16)

    place = lax.broadcasted_iota(jnp.int32, (px, px), 0)
    plane, i, j = place // q, (place % q) // cols_out, place % cols_out
    source = (2 * i + plane // 2) * cols_in + 2 * j + plane % 2
    perm = (source == lax.broadcasted_iota(jnp.int32, (px, px), 1)).astype(BF16)
    size_p = per * cols_in
    place = lax.broadcasted_iota(jnp.int32, (size_p, size_p), 0)
    source = (place // cols_in) * cols_in + 2 * (place % cols_out) + (place % cols_in) // cols_out
    perm_rim = (source == lax.broadcasted_iota(jnp.int32, (size_p, size_p), 1)).astype(BF16)

    xp, pre, side_pre, stat = call(
        functools.partial(first_body, per, px, q),
        "first_product",
        (steps,),
        [
            pl.BlockSpec((per, rows_in, cols_in, cin), lambda s: (s, 0, 0, 0)),
            whole((px, px)),
            whole((cin, mid)),
            whole((cin, wide)),
        ],
        [
            rows_spec(per * px, cin),
            rows_spec(per * px, mid),
            rows_spec(rows, wide),
            whole((2 * (mid + wide) // LANES, LANES)),
        ],
        [
            shape((n * px, cin), BF16),
            shape((n * px, mid)),
            shape((n * q, wide)),
            shape((2 * (mid + wide) // LANES, LANES)),
        ],
        [pltpu.VMEM((16, mid), F32), pltpu.VMEM((16, wide), F32)],
        flops=2 * n * (px * cin * (mid + px) + q * cin * wide),
        moved=n * px * cin * 8 + n * q * wide * 4 + cin * (mid + wide) * 2,
    )(images, perm, w_first, w_side)
    coef1, side_coef = exchange(
        stat,
        [narrow],
        functools.partial(first_totals, cells_in, cells_out, mid, wide),
        [shape((8, mid)), shape((8, wide))],
        0,
    )

    pre_planes = pre.reshape(n, 4, q, mid)
    planes_spec = pl.BlockSpec((per, 4, q, mid), lambda s: (s, 0, 0, 0))
    mid_pre, stat = call(
        functools.partial(conv_body, per, px, q),
        "grouped_conv",
        (steps,),
        [
            planes_spec,
            pl.BlockSpec((per, cols_in, cin), lambda s: (s, 0, 0)),
            pl.BlockSpec(memory_space=pltpu.SMEM),
            whole((cin, mid)),
            whole((size_p, size_p)),
            whole((8, mid)),
            whole((9, CHUNK, mid)),
        ],
        [rows_spec(rows, mid), whole((2 * mid // LANES, LANES))],
        [shape((n * q, mid)), shape((2 * mid // LANES, LANES))],
        [
            pltpu.VMEM((per, q, mid), BF16),
            pltpu.VMEM((per, q, mid), BF16),
            pltpu.VMEM((per, q + 16, mid), BF16),
            pltpu.VMEM((per, q + 16, mid), BF16),
            pltpu.VMEM((16, mid), F32),
        ],
        flops=2 * n * q * mid * CHUNK * 9 + 2 * n * cols_in * cin * mid,
        moved=n * px * mid * 4 + n * q * mid * 4,
    )(pre_planes, halo_x, flag, w_first, perm_rim, coef1, wbd)
    (coef2,) = exchange(
        stat, [narrow], functools.partial(mid_totals, cells_out, mid), [shape((8, mid))], 1
    )

    mid_act, last_pre, stat = call(
        last_body,
        "last_product",
        (steps,),
        [rows_spec(rows, mid), whole((8, mid)), whole((mid, wide))],
        [rows_spec(rows, mid), rows_spec(rows, wide), whole((2 * wide // LANES, LANES))],
        [shape((n * q, mid), BF16), shape((n * q, wide)), shape((2 * wide // LANES, LANES))],
        [pltpu.VMEM((16, wide), F32)],
        flops=2 * n * q * mid * wide,
        moved=n * q * (mid * 6 + wide * 4),
    )(mid_pre, coef2, w_last)
    (coef3,) = exchange(
        stat,
        [wides, side_coef],
        functools.partial(last_totals, cells_out, wide),
        [shape((8, wide))],
        2,
    )

    cot = cotangent.reshape(n * q, wide)
    output, stat = call(
        out_body,
        "output",
        (steps,),
        [rows_spec(rows, wide), rows_spec(rows, wide), rows_spec(rows, wide), whole((8, wide))],
        [rows_spec(rows, wide), whole((3 * wide // LANES, LANES))],
        [shape((n * q, wide), BF16), shape((3 * wide // LANES, LANES))],
        [pltpu.VMEM((24, wide), F32)],
        flops=30 * n * q * wide,
        moved=n * q * wide * 12,
    )(last_pre, side_pre, cot, coef3)
    coef4, wide_grads = exchange(
        stat,
        [coef3],
        functools.partial(out_totals, cells_out, wide),
        [shape((8, wide)), shape((8, wide))],
        3,
    )

    xp_planes = xp.reshape(n, 4, q, cin)
    last_grad, side_grad, g_last, g_side = call(
        functools.partial(tail_body, per, q),
        "last_gradients",
        (steps,),
        [
            rows_spec(rows, wide),
            rows_spec(rows, wide),
            rows_spec(rows, wide),
            whole((8, wide)),
            whole((8, wide)),
            rows_spec(rows, mid),
            pl.BlockSpec((per, 1, q, cin), lambda s: (s, 0, 0, 0)),
        ],
        [rows_spec(rows, wide), rows_spec(rows, wide), whole((mid, wide)), whole((cin, wide))],
        [
            shape((n * q, wide), BF16),
            shape((n * q, wide), BF16),
            shape((mid, wide), BF16),
            shape((cin, wide), BF16),
        ],
        [pltpu.VMEM((mid, wide), F32), pltpu.VMEM((cin, wide), F32)],
        flops=4 * n * q * mid * wide,
        moved=n * q * (wide * 14 + mid * 4) + (mid + cin) * wide * 2,
        vmem=60,
    )(last_pre, side_pre, cot, coef3, coef4, mid_act, xp_planes)
    half = wide // 2
    tail_sum = split_sum(
        jnp.concatenate([g_last[:, :half], g_last[:, half:], g_side[:, :half], g_side[:, half:]], axis=0)
    )
    g_last = jnp.concatenate([tail_sum[:mid], tail_sum[mid : 2 * mid]], axis=1).astype(F32)
    g_side = jnp.concatenate([tail_sum[2 * mid : 2 * mid + cin], tail_sum[2 * mid + cin :]], axis=1).astype(F32)

    mid_up, side_back, stat = call(
        mid_back_body,
        "mid_back",
        (steps,),
        [
            rows_spec(rows, wide),
            rows_spec(rows, wide),
            whole((mid, wide)),
            whole((cin, wide)),
            rows_spec(rows, mid),
            whole((8, mid)),
        ],
        [rows_spec(rows, mid), rows_spec(rows, cin), whole((2 * mid // LANES, LANES))],
        [shape((n * q, mid)), shape((n * q, cin)), shape((2 * mid // LANES, LANES))],
        [pltpu.VMEM((16, mid), F32)],
        flops=4 * n * q * mid * wide,
        moved=n * q * (wide * 4 + mid * 12) + (mid + cin) * wide * 2,
    )(last_grad, side_grad, w_last, w_side, mid_pre, coef2)
    coef5, mid_grads = exchange(
        stat,
        [coef2],
        functools.partial(inner_totals, cells_out, mid),
        [shape((8, mid)), shape((8, mid))],
        4,
    )

    def top(values):
        return values.reshape(n, q, mid)[:, :cols_out]

    rim = top(mid_pre) * coef2[0] + coef2[1]
    rim = (top(mid_up) * coef5[0] + coef5[1] + rim * coef5[2]).astype(BF16)
    rim = lax.ppermute(rim, "height", [(i + 1, i) for i in range(size_h - 1)])
    first_up, g_mid, stat = call(
        functools.partial(conv_back_body, per, px, q),
        "grouped_conv_back",
        (steps,),
        [
            rows_spec(rows, mid),
            rows_spec(rows, mid),
            pl.BlockSpec((per, cols_out, mid), lambda s: (s, 0, 0)),
            planes_spec,
            whole((8, mid)),
            whole((8, mid)),
            whole((8, mid)),
            whole((9, CHUNK, mid)),
        ],
        [planes_spec, whole((9, gw, mid)), whole((2 * mid // LANES, LANES))],
        [shape((n, 4, q, mid)), shape((9, gw, mid), BF16), shape((2 * mid // LANES, LANES))],
        [
            pltpu.VMEM((per, q + 16, mid), BF16),
            pltpu.VMEM((per, q + 16, mid), BF16),
            pltpu.VMEM((16, mid), F32),
            pltpu.VMEM((9, CHUNK, mid), F32),
        ],
        flops=4 * n * q * mid * CHUNK * 9,
        moved=n * q * mid * 8 + n * px * mid * 8,
        vmem=60,
    )(mid_up, mid_pre, rim, pre_planes, coef2, coef5, coef1, wbd)
    coef6, first_grads = exchange(
        stat,
        [coef1],
        functools.partial(inner_totals, cells_in, mid),
        [shape((8, mid)), shape((8, mid))],
        5,
    )

    first_grad, g_first = call(
        first_back_body,
        "first_gradient",
        (steps,),
        [
            rows_spec(per * px, mid),
            rows_spec(per * px, mid),
            whole((8, mid)),
            whole((8, mid)),
            rows_spec(per * px, cin),
        ],
        [rows_spec(per * px, mid), whole((cin, mid))],
        [shape((n * px, mid), BF16), shape((cin, mid), BF16)],
        [pltpu.VMEM((cin, mid), F32)],
        flops=2 * n * px * mid * cin,
        moved=n * px * (mid * 10 + cin * 2),
    )(first_up.reshape(n * px, mid), pre, coef1, coef6, xp)
    head = jnp.concatenate([g_first, g_mid.reshape(9 * gw, mid)], axis=0)
    unit = devices * 16
    lack = -head.shape[0] % unit
    head_sum = split_sum(jnp.pad(head, ((0, lack), (0, 0))))

    grad_images = call(
        functools.partial(image_back_body, per, px, q),
        "image_gradient",
        (steps,),
        [
            rows_spec(per * px, mid),
            whole((cin, mid)),
            rows_spec(rows, cin),
            whole((px, px)),
        ],
        pl.BlockSpec((per, rows_in, cols_in, cin), lambda s: (s, 0, 0, 0)),
        shape((n, rows_in, cols_in, cin), BF16),
        flops=2 * n * px * cin * (mid + px),
        moved=n * px * (mid * 2 + cin * 2) + n * q * cin * 4,
    )(first_grad, w_first, side_back, perm)

    return (
        output.reshape(n, rows_out, cols_out, wide),
        grad_images,
        head_sum[:cin].astype(F32),
        first_grads[1],
        first_grads[0],
        head_sum[cin : cin + 9 * gw].reshape(3, 3, gw, mid).astype(F32),
        mid_grads[1],
        mid_grads[0],
        g_last,
        wide_grads[1],
        wide_grads[0],
        g_side,
        wide_grads[2],
        wide_grads[0],
    )


def solution(mesh):
    split = P("batch", "height", None, None)
    in_specs = (split,) + (P(),) * 12 + (split,)
    out_specs = (split, split) + (P(),) * 12
    return jax.shard_map(
        per_device, mesh=mesh, in_specs=in_specs, out_specs=out_specs, check_vma=False
    )
```

```python
import functools

import jax
import jax.numpy as jnp
from jax import lax
from jax.experimental import pallas as pl
from jax.experimental.pallas import tpu as pltpu
from jax.sharding import PartitionSpec as P

EPSILON = 1e-05
LANES = 128
CHUNK = 256
BF16 = jnp.bfloat16
F32 = jnp.float32
MIB = 1 << 20


def dot(a, b):
    return jnp.dot(a, b, preferred_element_type=F32)


def dot_nt(a, b):
    return lax.dot_general(a, b, (((1,), (1,)), ((), ())), preferred_element_type=F32)


def dot_tn(a, b):
    return lax.dot_general(a, b, (((0,), (0,)), ((), ())), preferred_element_type=F32)


def fold(values):
    rows, cols = values.shape
    return jnp.sum(values.reshape(rows // 8, 8, cols), axis=0)


def put_row(ref, first, row):
    for k in range(row.shape[1] // LANES):
        ref[first + k : first + k + 1, :] = row[:, k * LANES : (k + 1) * LANES]


def get_row(values, first, width):
    count = width // LANES
    return jnp.concatenate([values[first + k : first + k + 1, :] for k in range(count)], axis=1)


def sums_out(ref, *partials):
    first = 0
    for part in partials:
        row = jnp.sum(part, axis=0, keepdims=True)
        put_row(ref, first, row)
        first += row.shape[1] // LANES


def whole(shape):
    return pl.BlockSpec(shape, lambda *_: (0,) * len(shape), pipeline_mode=pl.Buffered(1))


def rows_spec(rows, cols):
    return pl.BlockSpec((rows, cols), lambda i: (i, 0))


def call(
    body, name, grid, in_specs, out_specs, out_shape, scratch=(), flops=0, moved=0, vmem=56, ident=None
):
    return pl.pallas_call(
        body,
        name=name,
        grid=grid,
        in_specs=in_specs,
        out_specs=out_specs,
        out_shape=out_shape,
        scratch_shapes=list(scratch),
        compiler_params=pltpu.CompilerParams(
            vmem_limit_bytes=vmem * MIB, collective_id=ident, has_side_effects=ident is not None
        ),
        cost_estimate=pl.CostEstimate(flops=flops, bytes_accessed=moved, transcendentals=0),
    )


def shape(dims, kind=F32):
    return jax.ShapeDtypeStruct(dims, kind)


def exchange_body(epilogue, outs, in_ref, *rest):
    n_par = len(rest) - outs - 6
    params = rest[:n_par]
    out_refs = rest[n_par : n_par + outs]
    got_b, got_h, send_b, recv_b, send_h, recv_h = rest[n_par + outs :]
    size_b, size_h = got_b.shape[0], got_h.shape[0]
    me_b, me_h = lax.axis_index("batch"), lax.axis_index("height")
    barrier = pltpu.get_barrier_semaphore()
    peers = [(lax.rem(me_b + k, size_b), me_h) for k in range(1, size_b)]
    peers_h = [(me_b, lax.rem(me_h + k, size_h)) for k in range(1, size_h)]
    for peer in peers + peers_h:
        pl.semaphore_signal(barrier, inc=1, device_id=peer, device_id_type=pl.DeviceIdType.MESH)
    pl.semaphore_wait(barrier, len(peers) + len(peers_h))

    def spread(src, got, me, targets, size, send, recv):
        copies = []
        for k, peer in enumerate(targets):
            copy = pltpu.make_async_remote_copy(
                src_ref=src,
                dst_ref=got.at[me],
                send_sem=send.at[k],
                recv_sem=recv.at[me],
                device_id=peer,
                device_id_type=pl.DeviceIdType.MESH,
            )
            copy.start()
            copies.append(copy)
        for k, peer in enumerate(targets):
            other = lax.rem(me + (size - 1 - k), size)
            pltpu.make_async_remote_copy(
                src_ref=src,
                dst_ref=got.at[other],
                send_sem=send.at[k],
                recv_sem=recv.at[other],
                device_id=peer,
                device_id_type=pl.DeviceIdType.MESH,
            ).wait_recv()
        total = got[0]
        for k in range(1, size):
            total = total + got[k]
        return total, copies

    got_b[me_b] = in_ref[...]
    part, copies_b = spread(in_ref, got_b, me_b, peers, size_b, send_b, recv_b)
    got_h[me_h] = part
    total, copies_h = spread(got_h.at[me_h], got_h, me_h, peers_h, size_h, send_h, recv_h)
    epilogue(total, params, out_refs)
    for copy in copies_b + copies_h:
        copy.wait_send()


def exchange(sums, params, epilogue, out_shape, ident):
    rows = sums.shape[0]
    size_b, size_h = lax.axis_size("batch"), lax.axis_size("height")
    vmem = pl.BlockSpec(memory_space=pltpu.VMEM)
    return pl.pallas_call(
        functools.partial(exchange_body, epilogue, len(out_shape)),
        name="exchange_%d" % ident,
        in_specs=[vmem] * (1 + len(params)),
        out_specs=[vmem] * len(out_shape),
        out_shape=out_shape,
        scratch_shapes=[
            pltpu.VMEM((size_b, rows, LANES), F32),
            pltpu.VMEM((size_h, rows, LANES), F32),
            pltpu.SemaphoreType.DMA((size_b - 1,)),
            pltpu.SemaphoreType.DMA((size_b,)),
            pltpu.SemaphoreType.DMA((size_h - 1,)),
            pltpu.SemaphoreType.DMA((size_h,)),
        ],
        compiler_params=pltpu.CompilerParams(collective_id=ident, has_side_effects=True),
        cost_estimate=pl.CostEstimate(flops=1000, bytes_accessed=100000, transcendentals=0),
    )(sums, *params)


def norm_terms(total, first, width, cells):
    average = get_row(total, first, width) * (1.0 / cells)
    meansq = get_row(total, first + width // LANES, width) * (1.0 / cells)
    inverse = lax.rsqrt(meansq - average * average + EPSILON)
    return inverse, -average * inverse


def fill(ref, rows):
    for k, row in enumerate(rows):
        ref[k : k + 1, :] = row
    ref[len(rows) :, :] = jnp.zeros((8 - len(rows), ref.shape[1]), F32)


def act_rows(inverse, offset, gain, shift):
    return [
        inverse,
        offset,
        0.5 * gain,
        0.5 * shift,
        0.5 * gain * inverse,
        0.5 * (shift + gain * offset),
    ]


def first_totals(cells_in, cells_out, width, wide, total, params, outs):
    gain, shift = params[0][0:1, :], params[0][1:2, :]
    fill(outs[0], act_rows(*norm_terms(total, 0, width, cells_in), gain, shift))
    fill(outs[1], list(norm_terms(total, 2 * width // LANES, wide, cells_out)))


def mid_totals(cells_out, width, total, params, outs):
    gain, shift = params[0][2:3, :], params[0][3:4, :]
    fill(outs[0], act_rows(*norm_terms(total, 0, width, cells_out), gain, shift))


def last_totals(cells_out, wide, total, params, outs):
    wides, side = params
    inverse, offset = norm_terms(total, 0, wide, cells_out)
    fill(
        outs[0],
        [
            inverse,
            offset,
            side[0:1, :],
            side[1:2, :],
            0.5 * wides[0:1, :],
            0.5 * wides[2:3, :],
            0.5 * (wides[1:2, :] + wides[3:4, :]),
        ],
    )


def back_rows(gain, inverse, total_up, cross, cells):
    scale = gain * inverse
    return [0.5 * scale, -scale * total_up * (1.0 / cells), -scale * cross * (1.0 / cells)]


def out_totals(cells_out, wide, total, params, outs):
    coef = params[0]
    step = wide // LANES
    total_up, last_cross, side_cross = [
        0.5 * get_row(total, k * step, wide) for k in range(3)
    ]
    fill(
        outs[0],
        back_rows(2.0 * coef[4:5, :], coef[0:1, :], total_up, last_cross, cells_out)
        + back_rows(2.0 * coef[5:6, :], coef[2:3, :], total_up, side_cross, cells_out),
    )
    fill(outs[1], [total_up, last_cross, side_cross])


def inner_totals(cells, width, total, params, outs):
    coef = params[0]
    total_up = 0.5 * get_row(total, 0, width)
    cross = 0.5 * get_row(total, width // LANES, width)
    fill(outs[0], back_rows(2.0 * coef[2:3, :], coef[0:1, :], total_up, cross, cells))
    fill(outs[1], [total_up, cross])


def half_silu(half):
    return half + half * jnp.tanh(half)


def slope_twice(half, th):
    return (1.0 + th) * (1.0 + half * (1.0 - th))


def to_neighbour(copies, moves_up, what):
    height, size = lax.axis_index("height"), lax.axis_size("height")
    sends = height > 0 if moves_up else height < size - 1
    gets = height < size - 1 if moves_up else height > 0
    if what == "start":
        pl.when(sends)(lambda: run(copies, "start"))
    else:
        pl.when(sends)(lambda: run(copies, "wait_send"))
        pl.when(gets)(lambda: run(copies, "wait_recv"))


def first_body(
    per, px, q, img, perm, w1, ws, images, xp, pre, side, stat, halo, acc, acc_s, send, recv
):
    step = pl.program_id(0)
    mid, wide = w1.shape[1], ws.shape[1]
    below = images.at[:, images.shape[1] - 1]
    row = remote(below, halo, send, recv, upper_lower()[0])

    @pl.when(step == 0)
    def _():
        greet(upper_lower())
        to_neighbour([row], False, "start")

    @pl.when(step == 0)
    def _():
        acc[...] = jnp.zeros_like(acc)
        acc_s[...] = jnp.zeros_like(acc_s)

    for k in range(per):
        flat = img[k].reshape(px, img.shape[3])
        moved = dot(perm[...], flat).astype(BF16)
        xp[k * px : (k + 1) * px, :] = moved
        for c in range(0, mid, CHUNK):
            cols = slice(c, c + CHUNK)
            part = dot(moved, w1[:, cols])
            pre[k * px : (k + 1) * px, cols] = part
            acc[0:8, cols] += fold(part)
            acc[8:16, cols] += fold(part * part)
    even = jnp.concatenate([xp[k * px : k * px + q, :] for k in range(per)], axis=0)
    for c in range(0, wide, CHUNK):
        cols = slice(c, c + CHUNK)
        part = dot(even, ws[:, cols])
        side[:, cols] = part
        acc_s[0:8, cols] += fold(part)
        acc_s[8:16, cols] += fold(part * part)

    @pl.when(step == pl.num_programs(0) - 1)
    def _():
        sums_out(stat, acc[0:8, :], acc[8:16, :], acc_s[0:8, :], acc_s[8:16, :])
        to_neighbour([row], False, "wait")


def conv_body(per, px, q, pre, halo, flag, w1, perm, coef, wbd, mid, stat, a00, a01, a10, a11, acc):
    step = pl.program_id(0)
    width = w1.shape[1]

    @pl.when(step == 0)
    def _():
        acc[...] = jnp.zeros_like(acc)

    scale, offset = coef[4:5, :], coef[5:6, :]
    flat = halo[...].reshape(per * 32, halo.shape[2])
    rim = dot(dot(perm[...], flat).astype(BF16), w1[...])
    rim = jnp.where(flag[0] > 0, half_silu(rim * scale + offset), 0.0).astype(BF16)
    rim = rim.reshape(per, 2, 16, width)
    a10[:, 0:16, :] = rim[:, 0]
    a11[:, 0:16, :] = rim[:, 1]
    for plane, ref, top in ((0, a00, 0), (1, a01, 0), (2, a10, 16), (3, a11, 16)):
        half = pre[:, plane] * scale[None] + offset[None]
        ref[:, top : top + q, :] = half_silu(half).astype(BF16)
    rows = per * q
    first_col = lax.broadcasted_iota(jnp.int32, (rows, CHUNK), 0) % 16 == 0
    for c in range(0, width, CHUNK):
        cols = slice(c, c + CHUNK)

        def tap(ref, top, row, col):
            return dot(ref[:, top : top + q, cols].reshape(rows, CHUNK), wbd[row * 3 + col, :, cols])

        straight = (
            tap(a00, 0, 1, 1)
            + tap(a01, 0, 1, 2)
            + tap(a10, 16, 2, 1)
            + tap(a11, 16, 2, 2)
            + tap(a10, 0, 0, 1)
            + tap(a11, 0, 0, 2)
        )
        moved = tap(a01, 0, 1, 0) + tap(a11, 16, 2, 0) + tap(a11, 0, 0, 0)
        part = straight + jnp.where(first_col, 0.0, pltpu.roll(moved, 1, 0))
        mid[:, cols] = part
        acc[0:8, cols] += fold(part)
        acc[8:16, cols] += fold(part * part)

    @pl.when(step == pl.num_programs(0) - 1)
    def _():
        sums_out(stat, acc[0:8, :], acc[8:16, :])


def rim_copy(rim, halo, per, step, send, recv):
    images = pl.ds(step * per, per)
    return remote(rim.at[images], halo.at[images], send.at[step], recv.at[step], upper_lower()[1])


def rim_finish(rim, halo, per, send, recv):
    copies = [rim_copy(rim, halo, per, s, send, recv) for s in range(rim.shape[0] // per)]
    to_neighbour(copies, True, "wait")


def last_body(per, q, mid, coef, w, act, pre, stat, halo, acc, rim, send, recv):
    step = pl.program_id(0)
    width = mid.shape[1]

    @pl.when(step == 0)
    def _():
        acc[...] = jnp.zeros_like(acc)
        greet(upper_lower())

    top = mid[...].reshape(per, q, width)[:, 0:16] * coef[0:1, :][None] + coef[1:2, :][None]
    rim[pl.ds(step * per, per)] = top.astype(BF16)
    to_neighbour([rim_copy(rim, halo, per, step, send, recv)], True, "start")
    half = mid[...] * coef[4:5, :] + coef[5:6, :]
    act[...] = half_silu(half).astype(BF16)
    for c in range(0, w.shape[1], CHUNK):
        cols = slice(c, c + CHUNK)
        part = dot(act[...], w[:, cols])
        pre[:, cols] = part
        acc[0:8, cols] += fold(part)
        acc[8:16, cols] += fold(part * part)

    @pl.when(step == pl.num_programs(0) - 1)
    def _():
        sums_out(stat, acc[0:8, :], acc[8:16, :])
        rim_finish(rim, halo, per, send, recv)


def out_parts(last, side, cot, coef, cols):
    last_normed = last[:, cols] * coef[0:1, cols] + coef[1:2, cols]
    side_normed = side[:, cols] * coef[2:3, cols] + coef[3:4, cols]
    half = last_normed * coef[4:5, cols] + side_normed * coef[5:6, cols] + coef[6:7, cols]
    th = jnp.tanh(half)
    up = cot[:, cols].astype(F32) * slope_twice(half, th)
    return last_normed, side_normed, half, th, up


def out_body(last, side, cot, coef, out, stat, acc):
    step = pl.program_id(0)

    @pl.when(step == 0)
    def _():
        acc[...] = jnp.zeros_like(acc)

    for c in range(0, last.shape[1], CHUNK):
        cols = slice(c, c + CHUNK)
        last_normed, side_normed, half, th, up = out_parts(last, side, cot, coef, cols)
        out[:, cols] = (half + half * th).astype(BF16)
        acc[0:8, cols] += fold(up)
        acc[8:16, cols] += fold(up * last_normed)
        acc[16:24, cols] += fold(up * side_normed)

    @pl.when(step == pl.num_programs(0) - 1)
    def _():
        sums_out(stat, acc[0:8, :], acc[8:16, :], acc[16:24, :])


def last_grad_body(last, side, cot, coef, back, act, lg, sg, g_last, acc):
    step = pl.program_id(0)

    @pl.when(step == 0)
    def _():
        acc[...] = jnp.zeros_like(acc)

    for c in range(0, last.shape[1], CHUNK):
        cols = slice(c, c + CHUNK)
        last_normed, side_normed, _, _, up = out_parts(last, side, cot, coef, cols)
        down = (up * back[0:1, cols] + back[1:2, cols] + last_normed * back[2:3, cols]).astype(BF16)
        lg[:, cols] = down
        acc[:, cols] += dot_tn(act[...], down)
        down = (up * back[3:4, cols] + back[4:5, cols] + side_normed * back[5:6, cols]).astype(BF16)
        sg[:, cols] = down

    @pl.when(step == pl.num_programs(0) - 1)
    def _():
        g_last[...] = acc[...].astype(BF16)


def side_grad_body(per, q, sg, even, g_side, acc):
    step = pl.program_id(0)

    @pl.when(step == 0)
    def _():
        acc[...] = jnp.zeros_like(acc)

    flat = even[...].reshape(per * q, even.shape[3])
    for c in range(0, sg.shape[1], CHUNK):
        cols = slice(c, c + CHUNK)
        acc[:, cols] += dot_tn(flat, sg[:, cols])

    @pl.when(step == pl.num_programs(0) - 1)
    def _():
        g_side[...] = acc[...].astype(BF16)


def mid_back_body(per, q, lg, sg, wl, ws, mid, coef, up, side_back, stat, halo, acc, rim, send, recv):
    step = pl.program_id(0)

    @pl.when(step == 0)
    def _():
        acc[...] = jnp.zeros_like(acc)

    for c in range(0, mid.shape[1], CHUNK):
        cols = slice(c, c + CHUNK)
        part = dot_nt(lg[...], wl[cols, :])
        normed = mid[:, cols] * coef[0:1, cols] + coef[1:2, cols]
        half = normed * coef[2:3, cols] + coef[3:4, cols]
        part = part * slope_twice(half, jnp.tanh(half))
        up[:, cols] = part
        rim[pl.ds(step * per, per), :, cols] = part.reshape(per, q, CHUNK)[:, 0:16].astype(BF16)
        acc[0:8, cols] += fold(part)
        acc[8:16, cols] += fold(part * normed)
    to_neighbour([rim_copy(rim, halo, per, step, send, recv)], True, "start")
    for c in range(0, mid.shape[1], CHUNK):
        cols = slice(c, c + CHUNK)
        side_back[:, cols] = dot_nt(sg[...], ws[cols, :])

    @pl.when(step == pl.num_programs(0) - 1)
    def _():
        sums_out(stat, acc[0:8, :], acc[8:16, :])
        rim_finish(rim, halo, per, send, recv)


def conv_back_body(
    per, px, q, mup, mid, rim_up, rim_normed, flag, pre, coef2, back, coef, wbd, up, g_mid, stat, mg, mgs, acc, acc_g
):
    step = pl.program_id(0)
    width = mid.shape[1]
    rows = per * q

    @pl.when(step == 0)
    def _():
        acc[...] = jnp.zeros_like(acc)
        acc_g[...] = jnp.zeros_like(acc_g)

    ext = q + 16
    last_col = lax.broadcasted_iota(jnp.int32, (rows, CHUNK), 0) % 16 == 15
    last_rim = lax.broadcasted_iota(jnp.int32, (per * 16, CHUNK), 0) % 16 == 15
    for c in range(0, width, CHUNK):
        cols = slice(c, c + CHUNK)
        normed = mid[:, cols] * coef2[0:1, cols] + coef2[1:2, cols]
        grad = (mup[:, cols] * back[0:1, cols] + back[1:2, cols] + normed * back[2:3, cols]).astype(BF16)
        mg[:, 0:q, cols] = grad.reshape(per, q, CHUNK)
        grad = pltpu.roll(grad.astype(F32), rows - 1, 0)
        mgs[:, 0:q, cols] = jnp.where(last_col, 0.0, grad).astype(BF16).reshape(per, q, CHUNK)
        rim = rim_up[:, :, cols].astype(F32).reshape(per * 16, CHUNK) * back[0:1, cols] + back[1:2, cols]
        rim = rim + rim_normed[:, :, cols].astype(F32).reshape(per * 16, CHUNK) * back[2:3, cols]
        rim = jnp.where(flag[0] > 0, rim, 0.0).astype(BF16)
        mg[:, q:ext, cols] = rim.reshape(per, 16, CHUNK)
        rim = pltpu.roll(rim.astype(F32), per * 16 - 1, 0)
        mgs[:, q:ext, cols] = jnp.where(last_rim, 0.0, rim).astype(BF16).reshape(per, 16, CHUNK)
        views = [ref[:, top : top + q, cols].reshape(rows, CHUNK) for top in (0, 16) for ref in (mg, mgs)]
        plans = (
            (0, ((1, 1, 0),)),
            (1, ((1, 2, 0), (1, 0, 1))),
            (2, ((2, 1, 0), (0, 1, 2))),
            (3, ((2, 2, 0), (2, 0, 1), (0, 2, 2), (0, 0, 3))),
        )
        for plane, taps in plans:
            total = None
            for row, col, view in taps:
                part = dot_nt(views[view], wbd[row * 3 + col, :, cols])
                total = part if total is None else total + part
            normed = pre[:, plane, :, cols].reshape(rows, CHUNK) * coef[0:1, cols] + coef[1:2, cols]
            half = normed * coef[2:3, cols] + coef[3:4, cols]
            th = jnp.tanh(half)
            act = (half + half * th).astype(BF16)
            total = total * slope_twice(half, th)
            up[:, plane, :, cols] = total.reshape(per, q, CHUNK).astype(BF16)
            acc[0:8, cols] += fold(total)
            acc[8:16, cols] += fold(total * normed)
            for row, col, view in taps:
                acc_g[row * 3 + col, :, cols] += dot_tn(act, views[view])

    @pl.when(step == pl.num_programs(0) - 1)
    def _():
        sums_out(stat, acc[0:8, :], acc[8:16, :])
        group = (lax.broadcasted_iota(jnp.int32, (32, width), 1) % CHUNK) // 32
        for tap in range(9):
            total = jnp.zeros((32, width), F32)
            for g in range(CHUNK // 32):
                total = total + jnp.where(group == g, acc_g[tap, g * 32 : (g + 1) * 32, :], 0.0)
            g_mid[tap] = total.astype(BF16)


def first_back_body(up, pre, coef, back, xp, fg, g_first, acc):
    step = pl.program_id(0)

    @pl.when(step == 0)
    def _():
        acc[...] = jnp.zeros_like(acc)

    for c in range(0, up.shape[1], CHUNK):
        cols = slice(c, c + CHUNK)
        normed = pre[:, cols] * coef[0:1, cols] + coef[1:2, cols]
        down = up[:, cols].astype(F32) * back[0:1, cols] + back[1:2, cols]
        down = (down + normed * back[2:3, cols]).astype(BF16)
        fg[:, cols] = down
        acc[:, cols] += dot_tn(xp[...], down)

    @pl.when(step == pl.num_programs(0) - 1)
    def _():
        g_first[...] = acc[...].astype(BF16)


def image_back_body(per, px, q, fg, w1, side_back, out):
    for k in range(per):
        for c in range(0, w1.shape[0], CHUNK):
            cols = slice(c, c + CHUNK)
            part = dot_nt(fg[k * px : (k + 1) * px, :], w1[cols, :])
            even = part[0:q] + side_back[k * q : (k + 1) * q, cols]
            out[k * px : k * px + q, cols] = even.astype(BF16)
            out[k * px + q : (k + 1) * px, cols] = part[q:].astype(BF16)


def place_body(per, px, planes, perm, out):
    for k in range(per):
        part = dot(perm[...], planes[k * px : (k + 1) * px, :]).astype(BF16)
        out[k] = part.reshape(out.shape[1:])


def digit(axis, bit):
    return lax.rem(lax.div(lax.axis_index(axis), 1 << bit), 2)


def peer(axis, bit):
    batch, height = lax.axis_index("batch"), lax.axis_index("height")
    move = (1 - 2 * digit(axis, bit)) * (1 << bit)
    return (batch + move, height) if axis == "batch" else (batch, height + move)


def orders():
    bits_b = lax.axis_size("batch").bit_length() - 1
    bits_h = lax.axis_size("height").bit_length() - 1
    across = [("batch", k) for k in range(1, bits_b)]
    half = len(across) // 2
    x_bits, y_bits = across[:half], across[half:]
    z_bits = [("height", k) for k in range(bits_h)]
    return [x_bits + y_bits + z_bits, y_bits + x_bits + z_bits]


def stage_count():
    return len(orders()[0])


def lengths(rows):
    kept = [rows]
    for _ in range(stage_count()):
        kept.append(kept[-1] // 2 if kept[-1] % 32 == 0 else kept[-1])
    return kept


def landing(rows):
    return sum(lengths(rows)[1:])


def upper_lower():
    batch, height = lax.axis_index("batch"), lax.axis_index("height")
    size = lax.axis_size("height")
    return [(batch, lax.rem(height + 1, size)), (batch, lax.rem(height + size - 1, size))]


def partners():
    return [peer("batch", 0)] + [peer(axis, bit) for axis, bit in orders()[0]]


def greet(peers):
    barrier = pltpu.get_barrier_semaphore()
    for one in peers:
        pl.semaphore_signal(barrier, inc=1, device_id=one, device_id_type=pl.DeviceIdType.MESH)
    pl.semaphore_wait(barrier, len(peers))


def remote(src, dst, send, recv, target):
    return pltpu.make_async_remote_copy(
        src_ref=src,
        dst_ref=dst,
        send_sem=send,
        recv_sem=recv,
        device_id=target,
        device_id_type=pl.DeviceIdType.MESH,
    )


class Flow:
    def __init__(self, rows, width, own, got, send, recv):
        self.own, self.got, self.send, self.recv = own, got, send, recv
        self.kept = lengths(rows)
        self.orders = orders()
        self.cols = [slice(0, width // 2), slice(width // 2, width)]
        self.low = []
        for order in self.orders:
            low = [0]
            for s, (axis, bit) in enumerate(order):
                move = digit(axis, bit) * self.kept[s + 1] if self.halved(s) else 0
                low.append(low[-1] + move)
            self.low.append(low)

    def halved(self, s):
        return self.kept[s + 1] < self.kept[s]

    def rows(self, first, count):
        return pl.ds(pl.multiple_of(first, 16), count)

    def keep(self, k, s):
        return self.rows(self.low[k][s], self.kept[s])

    def away(self, k, s):
        if not self.halved(s):
            return self.keep(k, s)
        axis, bit = self.orders[k][s]
        return self.rows(self.low[k][s] + (1 - digit(axis, bit)) * self.kept[s + 1], self.kept[s + 1])

    def place(self, s):
        return pl.ds(sum(self.kept[1 : s + 1]), self.kept[s + 1])

    def scatter(self, k, s):
        return remote(
            self.own.at[self.away(k, s), self.cols[k]],
            self.got.at[self.place(s), self.cols[k]],
            self.send.at[0, k, s],
            self.recv.at[0, k, s],
            peer(*self.orders[k][s]),
        )

    def scatter_start(self, s):
        for k in range(2):
            self.scatter(k, s).start()

    def scatter_finish(self, s):
        for k in range(2):
            self.scatter(k, s).wait()
            rows, cols = self.keep(k, s + 1), self.cols[k]
            total = self.own[rows, cols].astype(F32) + self.got[self.place(s), cols].astype(F32)
            self.own[rows, cols] = total.astype(BF16)

    def gather(self, k, s, rows):
        return remote(
            self.own.at[rows, self.cols[k]],
            self.own.at[rows, self.cols[k]],
            self.send.at[1, k, s],
            self.recv.at[1, k, s],
            peer(*self.orders[k][s]),
        )

    def gather_start(self, s):
        for k in range(2):
            if self.halved(s):
                self.gather(k, s, self.keep(k, s + 1)).start()

    def gather_finish(self, s):
        for k in range(2):
            if self.halved(s):
                self.gather(k, s, self.keep(k, s + 1)).wait_send()
                self.gather(k, s, self.away(k, s)).wait_recv()

    def moves(self, s, hbm, sems, out):
        copies = []
        for k in range(2):
            here = self.own.at[self.keep(k, s), self.cols[k]]
            there = hbm.at[self.keep(k, s), self.cols[k]]
            copies.append(pltpu.make_async_copy(*((here, there) if out else (there, here)), sems.at[k]))
        return copies


def run(copies, what):
    for copy in copies:
        getattr(copy, what)()


def own_half(ref):
    half = ref.shape[0] // 2
    return ref.at[pl.ds(pl.multiple_of(lax.axis_index("batch") % 2 * half, 16), half)]


def other_half(ref):
    half = ref.shape[0] // 2
    return ref.at[pl.ds(pl.multiple_of((1 - lax.axis_index("batch") % 2) * half, 16), half)]


def add_into(ref, other, step=64):
    for first in range(0, other.shape[0], step):
        rows = slice(first, min(first + step, other.shape[0]))
        ref[rows, :] = (ref[rows, :].astype(F32) + other[rows, :].astype(F32)).astype(BF16)


def carrying(body, counts, carry):
    def kernel(*refs):
        groups, first = [], 0
        for count in counts:
            groups.append(refs[first : first + count])
            first += count
        ins, c_ins, outs, c_outs, scr = groups
        c_scr = refs[first:]
        step = pl.program_id(0)
        ahead, last = carry(c_ins, c_outs, c_scr)
        for when, action in ahead:
            pl.when(step == when)(action)
        body(*ins, *outs, *scr)
        for action in last:
            pl.when(step == pl.num_programs(0) - 1)(action)

    return kernel


def carry_core(c_ins, c_outs, c_scr):
    (g_last,), (mate_last,), (send, recv) = c_ins, c_outs, c_scr
    copy = remote(other_half(g_last), mate_last, send, recv, peer("batch", 0))

    def start():
        greet([peer("batch", 0)])
        copy.start()

    return [(0, start)], [copy.wait]


def carry_mid(c_ins, c_outs, c_scr):
    g_last, mate_last, g_side = c_ins
    mate_side, state_last = c_outs
    own, got, tmp, local, core, send, recv = c_scr
    flow = Flow(own.shape[0], own.shape[1], own, got, send, recv)
    copy = remote(other_half(g_side), mate_side, core.at[0], core.at[1], peer("batch", 0))
    loads = [
        pltpu.make_async_copy(own_half(g_last), own, local.at[0]),
        pltpu.make_async_copy(mate_last, tmp, local.at[1]),
    ]

    def start():
        run(loads, "start")
        greet(partners() + upper_lower())
        copy.start()

    def first():
        run(loads, "wait")
        add_into(own, tmp)
        flow.scatter_start(0)

    def finish():
        flow.scatter_finish(0)
        dumps = flow.moves(1, state_last, local, True)
        run(dumps, "start")
        copy.wait()
        run(dumps, "wait")

    return [(0, start), (1, first)], [finish]


def carry_conv(c_ins, c_outs, c_scr):
    state_last, g_side, mate_side = c_ins
    shard_last, state_side = c_outs
    own_l, got_l, own_s, got_s, tmp, local, send_l, recv_l, send_s, recv_s = c_scr
    rows, width = own_l.shape
    last = Flow(rows, width, own_l, got_l, send_l, recv_l)
    side = Flow(rows, width, own_s, got_s, send_s, recv_s)
    stages = stage_count()
    loads_l = last.moves(1, state_last, local, False)
    loads_s = [
        pltpu.make_async_copy(own_half(g_side), own_s, local.at[2]),
        pltpu.make_async_copy(mate_side, tmp, local.at[3]),
    ]

    def start():
        run(loads_l + loads_s, "start")
        greet(partners())

    def first():
        run(loads_l, "wait")
        last.scatter_start(1)
        run(loads_s, "wait")
        add_into(own_s, tmp)
        side.scatter_start(0)

    def next_last(s):
        def action():
            last.scatter_finish(s)
            if s + 1 < stages:
                last.scatter_start(s + 1)

        return action

    def next_side():
        side.scatter_finish(0)
        side.scatter_start(1)

    def finish():
        last.scatter_finish(stages - 1)
        side.scatter_finish(1)
        dumps = last.moves(stages, shard_last, local, True)
        dumps += side.moves(2, state_side, local.at[pl.ds(2, 2)], True)
        run(dumps, "start")
        run(dumps, "wait")

    ahead = [(0, start), (1, first)]
    ahead += [(min(2 + s, 5), next_last(s)) for s in range(1, stages - 1)]
    return ahead + [(5, next_side)], [finish]


def carry_first(c_ins, c_outs, c_scr):
    shard_last, state_side = c_ins
    part_last, shard_side = c_outs
    own_l, own_s, got_s, local, send_l, recv_l, send_s, recv_s = c_scr
    rows, width = own_l.shape
    last = Flow(rows, width, own_l, None, send_l, recv_l)
    side = Flow(rows, width, own_s, got_s, send_s, recv_s)
    stages = stage_count()
    loads = last.moves(stages, shard_last, local, False)
    loads += side.moves(2, state_side, local.at[pl.ds(2, 2)], False)

    def start():
        run(loads, "start")
        greet(partners())

    def first():
        run(loads, "wait")
        last.gather_start(stages - 1)
        side.scatter_start(2)

    def following(k):
        def action():
            last.gather_finish(stages - 1 - k)
            if stages - 2 - k >= 2:
                last.gather_start(stages - 2 - k)
            side.scatter_finish(2 + k)
            if 3 + k < stages:
                side.scatter_start(3 + k)

        return action

    def finish():
        dumps = last.moves(2, part_last, local, True)
        dumps += side.moves(stages, shard_side, local.at[pl.ds(2, 2)], True)
        run(dumps, "start")
        run(dumps, "wait")

    between = [following(k) for k in range(stages - 2)]
    ahead = [(0, start), (1, first)] + [(min(3 + k, 5), act) for k, act in enumerate(between[:-1])]
    return ahead, [between[-1], finish]


def carry_image(c_ins, c_outs, c_scr):
    part_last, shard_side, g_first, g_mid = c_ins
    all_last, all_side, all_head = c_outs
    (own_l, own_s, own_h, got_h, tmp_h, full_h, local, core) = c_scr[:8]
    send_l, recv_l, send_s, recv_s, send_h, recv_h = c_scr[8:]
    rows, width = own_l.shape
    last = Flow(rows, width, own_l, None, send_l, recv_l)
    side = Flow(rows, width, own_s, None, send_s, recv_s)
    head = Flow(own_h.shape[0], own_h.shape[1], own_h, got_h, send_h, recv_h)
    done = Flow(own_h.shape[0], own_h.shape[1], full_h, None, send_h, recv_h)
    stages = stage_count()
    mate = peer("batch", 0)
    mine = lax.axis_index("batch") % 2
    wide_h = own_h.shape[1]
    cols = pl.ds(pl.multiple_of(mine * wide_h, LANES), wide_h)
    away = pl.ds(pl.multiple_of((1 - mine) * wide_h, LANES), wide_h)
    cut, end = g_first.shape[0], g_first.shape[0] + g_mid.shape[0]
    loads = last.moves(2, part_last, local, False)
    loads += side.moves(stages, shard_side, local.at[pl.ds(2, 2)], False)
    loads_h = [
        pltpu.make_async_copy(g_first.at[:, cols], own_h.at[0:cut], local.at[4]),
        pltpu.make_async_copy(g_mid.at[:, cols], own_h.at[cut:end], local.at[5]),
    ]
    mates_h = [
        remote(g_first.at[:, away], tmp_h.at[0:cut], core.at[0], core.at[1], mate),
        remote(g_mid.at[:, away], tmp_h.at[cut:end], core.at[2], core.at[3], mate),
    ]

    def ends(flow, array, k):
        return [
            pltpu.make_async_copy(flow.own, own_half(array), local.at[k]),
            remote(flow.own, own_half(array), core.at[4 + 2 * k], core.at[5 + 2 * k], mate),
        ]

    def ends_head():
        return [
            pltpu.make_async_copy(full_h.at[0:end], all_head.at[:, cols], local.at[2]),
            remote(full_h.at[0:end], all_head.at[:, cols], core.at[8], core.at[9], mate),
        ]

    def start():
        run(loads + loads_h, "start")
        own_h[end:, :] = jnp.zeros((own_h.shape[0] - end, wide_h), BF16)
        tmp_h[end:, :] = jnp.zeros((own_h.shape[0] - end, wide_h), BF16)
        greet(partners())
        run(mates_h, "start")

    def first():
        run(loads + loads_h, "wait")
        last.gather_start(1)
        side.gather_start(stages - 1)
        run(mates_h, "wait")
        add_into(own_h, tmp_h)
        head.scatter_start(0)

    def side_next(s):
        def action():
            side.gather_finish(s)
            if s:
                side.gather_start(s - 1)

        return action

    def last_next():
        last.gather_finish(1)
        last.gather_start(0)

    def head_next(s):
        def action():
            head.scatter_finish(s)
            if s + 1 < stages:
                head.scatter_start(s + 1)

        return action

    def head_back(s):
        def action():
            done.gather_finish(s)
            if s:
                done.gather_start(s - 1)

        return action

    def turn():
        for k in range(2):
            rows_k = head.keep(k, stages)
            full_h[rows_k, head.cols[k]] = own_h[rows_k, head.cols[k]]
        done.gather_start(stages - 1)

    def last_end():
        last.gather_finish(0)
        run(ends(last, all_last, 0), "start")

    def side_end():
        run(ends(side, all_side, 1), "start")

    def finish():
        run(ends_head(), "start")
        run(ends(last, all_last, 0) + ends(side, all_side, 1) + ends_head(), "wait")

    ahead = [(0, start), (1, first)]
    ahead += [(min(2 + k, 5), side_next(s)) for k, s in enumerate(range(stages - 1, 1, -1))]
    ahead += [(3, head_next(0)), (4, last_next), (5, head_next(1))]
    tail = [head_next(s) for s in range(2, stages)] + [turn, side_next(1), last_end]
    tail += [head_back(s) for s in range(stages - 1, 0, -1)] + [side_next(0), side_end, head_back(0), finish]
    return ahead, tail


def per_device(
    images,
    w_first,
    gain_first,
    shift_first,
    w_mid,
    gain_mid,
    shift_mid,
    w_last,
    gain_last,
    shift_last,
    w_side,
    gain_side,
    shift_side,
    cotangent,
):
    n, rows_in, cols_in, cin = images.shape
    mid = w_first.shape[1]
    wide = w_last.shape[1]
    gw = w_mid.shape[2]
    rows_out, cols_out = rows_in // 2, cols_in // 2
    px, q = rows_in * cols_in, rows_out * cols_out
    devices = lax.axis_size("batch") * lax.axis_size("height")
    cells_in = float(n * px * devices)
    cells_out = float(n * q * devices)
    size_h = lax.axis_size("height")
    per = 4
    steps = n // per
    rows = per * q

    anywhere = pl.BlockSpec(memory_space=pl.ANY)
    dma = pltpu.SemaphoreType.DMA
    narrow = jnp.stack([gain_first, shift_first, gain_mid, shift_mid] + [jnp.zeros_like(gain_mid)] * 4)
    wides = jnp.stack([gain_last, shift_last, gain_side, shift_side] + [jnp.zeros_like(gain_last)] * 4)
    flag = (lax.axis_index("height") > 0).astype(F32).reshape(1)
    flag_below = (lax.axis_index("height") < size_h - 1).astype(F32).reshape(1)
    tiled = jnp.tile(w_mid.reshape(9, 1, gw, mid), (1, CHUNK // gw, 1, 1))
    same = (
        lax.broadcasted_iota(jnp.int32, (CHUNK // gw, gw, mid), 0)
        == (lax.broadcasted_iota(jnp.int32, (CHUNK // gw, gw, mid), 2) % CHUNK) // gw
    )
    wbd = jnp.where(same[None], tiled, 0).reshape(9, CHUNK, mid).astype(BF16)

    place = lax.broadcasted_iota(jnp.int32, (px, px), 0)
    plane, i, j = place // q, (place % q) // cols_out, place % cols_out
    source = (2 * i + plane // 2) * cols_in + 2 * j + plane % 2
    perm = (source == lax.broadcasted_iota(jnp.int32, (px, px), 1)).astype(BF16)
    unperm = perm.T
    size_p = per * cols_in
    place = lax.broadcasted_iota(jnp.int32, (size_p, size_p), 0)
    source = (place // cols_in) * cols_in + 2 * (place % cols_out) + (place % cols_in) // cols_out
    perm_rim = (source == lax.broadcasted_iota(jnp.int32, (size_p, size_p), 1)).astype(BF16)

    xp, pre, side_pre, stat, halo_x = call(
        functools.partial(first_body, per, px, q),
        "first_product",
        (steps,),
        [
            pl.BlockSpec((per, rows_in, cols_in, cin), lambda s: (s, 0, 0, 0)),
            whole((px, px)),
            whole((cin, mid)),
            whole((cin, wide)),
            anywhere,
        ],
        [
            rows_spec(per * px, cin),
            rows_spec(per * px, mid),
            rows_spec(rows, wide),
            whole((2 * (mid + wide) // LANES, LANES)),
            anywhere,
        ],
        [
            shape((n * px, cin), BF16),
            shape((n * px, mid)),
            shape((n * q, wide)),
            shape((2 * (mid + wide) // LANES, LANES)),
            shape((n, cols_in, cin), BF16),
        ],
        [pltpu.VMEM((16, mid), F32), pltpu.VMEM((16, wide), F32), dma, dma],
        ident=6,
        flops=2 * n * (px * cin * (mid + px) + q * cin * wide),
        moved=n * px * cin * 8 + n * q * wide * 4 + cin * (mid + wide) * 2,
    )(images, perm, w_first, w_side, images)
    coef1, side_coef = exchange(
        stat,
        [narrow],
        functools.partial(first_totals, cells_in, cells_out, mid, wide),
        [shape((8, mid)), shape((8, wide))],
        0,
    )

    pre_planes = pre.reshape(n, 4, q, mid)
    planes_spec = pl.BlockSpec((per, 4, q, mid), lambda s: (s, 0, 0, 0))
    mid_pre, stat = call(
        functools.partial(conv_body, per, px, q),
        "grouped_conv",
        (steps,),
        [
            planes_spec,
            pl.BlockSpec((per, cols_in, cin), lambda s: (s, 0, 0)),
            pl.BlockSpec(memory_space=pltpu.SMEM),
            whole((cin, mid)),
            whole((size_p, size_p)),
            whole((8, mid)),
            whole((9, CHUNK, mid)),
        ],
        [rows_spec(rows, mid), whole((2 * mid // LANES, LANES))],
        [shape((n * q, mid)), shape((2 * mid // LANES, LANES))],
        [
            pltpu.VMEM((per, q, mid), BF16),
            pltpu.VMEM((per, q, mid), BF16),
            pltpu.VMEM((per, q + 16, mid), BF16),
            pltpu.VMEM((per, q + 16, mid), BF16),
            pltpu.VMEM((16, mid), F32),
        ],
        flops=2 * n * q * mid * CHUNK * 9 + 2 * n * cols_in * cin * mid,
        moved=n * px * mid * 4 + n * q * mid * 4,
    )(pre_planes, halo_x, flag, w_first, perm_rim, coef1, wbd)
    (coef2,) = exchange(
        stat, [narrow], functools.partial(mid_totals, cells_out, mid), [shape((8, mid))], 1
    )

    rims = [pltpu.VMEM((n, cols_out, mid), BF16), dma((steps,)), dma((steps,))]
    mid_act, last_pre, stat, rim_normed = call(
        functools.partial(last_body, per, q),
        "last_product",
        (steps,),
        [rows_spec(rows, mid), whole((8, mid)), whole((mid, wide))],
        [rows_spec(rows, mid), rows_spec(rows, wide), whole((2 * wide // LANES, LANES)), anywhere],
        [
            shape((n * q, mid), BF16),
            shape((n * q, wide)),
            shape((2 * wide // LANES, LANES)),
            shape((n, cols_out, mid), BF16),
        ],
        [pltpu.VMEM((16, wide), F32)] + rims,
        ident=7,
        flops=2 * n * q * mid * wide,
        moved=n * q * (mid * 6 + wide * 4),
    )(mid_pre, coef2, w_last)
    (coef3,) = exchange(
        stat,
        [wides, side_coef],
        functools.partial(last_totals, cells_out, wide),
        [shape((8, wide))],
        2,
    )

    cot = cotangent.reshape(n * q, wide)
    output, stat = call(
        out_body,
        "output",
        (steps,),
        [rows_spec(rows, wide), rows_spec(rows, wide), rows_spec(rows, wide), whole((8, wide))],
        [rows_spec(rows, wide), whole((3 * wide // LANES, LANES))],
        [shape((n * q, wide), BF16), shape((3 * wide // LANES, LANES))],
        [pltpu.VMEM((24, wide), F32)],
        flops=30 * n * q * wide,
        moved=n * q * wide * 12,
    )(last_pre, side_pre, cot, coef3)
    coef4, wide_grads = exchange(
        stat,
        [coef3],
        functools.partial(out_totals, cells_out, wide),
        [shape((8, wide)), shape((8, wide))],
        3,
    )

    xp_planes = xp.reshape(n, 4, q, cin)
    half_l = mid // 2
    stages = stage_count()
    sems = dma((2, 2, stages))
    state = shape((half_l, wide), BF16)
    buf = pltpu.VMEM((half_l, wide), BF16)
    got = pltpu.VMEM((landing(half_l), wide), BF16)
    last_grad, side_grad, g_last = call(
        last_grad_body,
        "last_gradients",
        (steps,),
        [
            rows_spec(rows, wide),
            rows_spec(rows, wide),
            rows_spec(rows, wide),
            whole((8, wide)),
            whole((8, wide)),
            rows_spec(rows, mid),
        ],
        [rows_spec(rows, wide), rows_spec(rows, wide), whole((mid, wide))],
        [
            shape((n * q, wide), BF16),
            shape((n * q, wide), BF16),
            shape((mid, wide), BF16),
        ],
        [pltpu.VMEM((mid, wide), F32)],
        flops=2 * n * q * mid * wide,
        moved=n * q * (wide * 14 + mid * 2) + mid * wide * 2,
    )(last_pre, side_pre, cot, coef3, coef4, mid_act)
    g_side, mate_last = call(
        carrying(functools.partial(side_grad_body, per, q), (2, 1, 1, 1, 1), carry_core),
        "side_gradient",
        (steps,),
        [rows_spec(rows, wide), pl.BlockSpec((per, 1, q, cin), lambda s: (s, 0, 0, 0)), anywhere],
        [whole((cin, wide)), anywhere],
        [shape((cin, wide), BF16), state],
        [pltpu.VMEM((cin, wide), F32), dma, dma],
        flops=2 * n * q * cin * wide,
        moved=n * q * (wide * 2 + cin * 2) + cin * wide * 2,
        ident=8,
    )(side_grad, xp_planes, g_last)

    mid_up, side_back, stat, rim_up, mate_side, state_last = call(
        carrying(functools.partial(mid_back_body, per, q), (6, 3, 4, 2, 4), carry_mid),
        "mid_back",
        (steps,),
        [
            rows_spec(rows, wide),
            rows_spec(rows, wide),
            whole((mid, wide)),
            whole((cin, wide)),
            rows_spec(rows, mid),
            whole((8, mid)),
            anywhere,
            anywhere,
            anywhere,
        ],
        [rows_spec(rows, mid), rows_spec(rows, cin), whole((2 * mid // LANES, LANES))] + [anywhere] * 3,
        [
            shape((n * q, mid)),
            shape((n * q, cin)),
            shape((2 * mid // LANES, LANES)),
            shape((n, cols_out, mid), BF16),
            state,
            state,
        ],
        [pltpu.VMEM((16, mid), F32)] + rims + [buf, got, buf, dma((2,)), dma((2,)), sems, sems],
        flops=4 * n * q * mid * wide,
        moved=n * q * (wide * 4 + mid * 12) + (mid + cin) * wide * 2,
        ident=9,
    )(last_grad, side_grad, w_last, w_side, mid_pre, coef2, g_last, mate_last, g_side)
    coef5, mid_grads = exchange(
        stat,
        [coef2],
        functools.partial(inner_totals, cells_out, mid),
        [shape((8, mid)), shape((8, mid))],
        4,
    )

    rim_spec = pl.BlockSpec((per, cols_out, mid), lambda s: (s, 0, 0))
    smem = pl.BlockSpec(memory_space=pltpu.SMEM)
    first_up, g_mid, stat, shard_last, state_side = call(
        carrying(functools.partial(conv_back_body, per, px, q), (10, 3, 3, 2, 4), carry_conv),
        "grouped_conv_back",
        (steps,),
        [
            rows_spec(rows, mid),
            rows_spec(rows, mid),
            rim_spec,
            rim_spec,
            smem,
            planes_spec,
            whole((8, mid)),
            whole((8, mid)),
            whole((8, mid)),
            whole((9, CHUNK, mid)),
            anywhere,
            anywhere,
            anywhere,
        ],
        [planes_spec, whole((9, gw, mid)), whole((2 * mid // LANES, LANES)), anywhere, anywhere],
        [
            shape((n, 4, q, mid), BF16),
            shape((9, gw, mid), BF16),
            shape((2 * mid // LANES, LANES)),
            state,
            state,
        ],
        [
            pltpu.VMEM((per, q + 16, mid), BF16),
            pltpu.VMEM((per, q + 16, mid), BF16),
            pltpu.VMEM((16, mid), F32),
            pltpu.VMEM((9, CHUNK, mid), F32),
            buf,
            got,
            buf,
            got,
            buf,
            dma((4,)),
            sems,
            sems,
            sems,
            sems,
        ],
        flops=4 * n * q * mid * CHUNK * 9,
        moved=n * q * mid * 8 + n * px * mid * 6,
        vmem=60,
        ident=10,
    )(
        mid_up,
        mid_pre,
        rim_up,
        rim_normed,
        flag_below,
        pre_planes,
        coef2,
        coef5,
        coef1,
        wbd,
        state_last,
        g_side,
        mate_side,
    )
    coef6, first_grads = exchange(
        stat,
        [coef1],
        functools.partial(inner_totals, cells_in, mid),
        [shape((8, mid)), shape((8, mid))],
        5,
    )

    first_grad, g_first, part_last, shard_side = call(
        carrying(first_back_body, (5, 2, 2, 2, 1), carry_first),
        "first_gradient",
        (steps,),
        [
            rows_spec(per * px, mid),
            rows_spec(per * px, mid),
            whole((8, mid)),
            whole((8, mid)),
            rows_spec(per * px, cin),
            anywhere,
            anywhere,
        ],
        [rows_spec(per * px, mid), whole((cin, mid)), anywhere, anywhere],
        [shape((n * px, mid), BF16), shape((cin, mid), BF16), state, state],
        [pltpu.VMEM((cin, mid), F32), buf, buf, got, dma((4,)), sems, sems, sems, sems],
        flops=2 * n * px * mid * cin,
        moved=n * px * (mid * 8 + cin * 2),
        ident=11,
    )(first_up.reshape(n * px, mid), pre, coef1, coef6, xp, shard_last, state_side)

    head_rows = cin + 9 * gw
    unit = 16 * (lax.axis_size("height") * lax.axis_size("batch") // 2)
    full_rows = -(-head_rows // unit) * unit
    half_h = mid // 2
    buf_h = pltpu.VMEM((full_rows, half_h), BF16)
    planes, all_last, all_side, all_head = call(
        carrying(functools.partial(image_back_body, per, px, q), (3, 4, 1, 3, 0), carry_image),
        "image_gradient",
        (steps,),
        [rows_spec(per * px, mid), whole((cin, mid)), rows_spec(rows, cin)] + [anywhere] * 4,
        [rows_spec(per * px, cin)] + [anywhere] * 3,
        [
            shape((n * px, cin), BF16),
            shape((mid, wide), BF16),
            shape((cin, wide), BF16),
            shape((head_rows, mid), BF16),
        ],
        [buf, buf, buf_h, pltpu.VMEM((landing(full_rows), half_h), BF16), buf_h, buf_h]
        + [dma((6,)), dma((10,))]
        + [sems] * 6,
        flops=2 * n * px * cin * mid,
        moved=n * px * (mid * 2 + cin * 2) + n * q * cin * 4,
        ident=12,
    )(first_grad, w_first, side_back, part_last, shard_side, g_first, g_mid.reshape(9 * gw, mid))
    grad_images = call(
        functools.partial(place_body, per, px),
        "image_places",
        (steps,),
        [rows_spec(per * px, cin), whole((px, px))],
        pl.BlockSpec((per, rows_in, cols_in, cin), lambda s: (s, 0, 0, 0)),
        shape((n, rows_in, cols_in, cin), BF16),
        flops=2 * n * px * cin * px,
        moved=n * px * cin * 4,
    )(planes, unperm)

    return (
        output.reshape(n, rows_out, cols_out, wide),
        grad_images,
        all_head[:cin].astype(F32),
        first_grads[1],
        first_grads[0],
        all_head[cin:].reshape(3, 3, gw, mid).astype(F32),
        mid_grads[1],
        mid_grads[0],
        all_last.astype(F32),
        wide_grads[1],
        wide_grads[0],
        all_side.astype(F32),
        wide_grads[2],
        wide_grads[0],
    )


def solution(mesh):
    split = P("batch", "height", None, None)
    in_specs = (split,) + (P(),) * 12 + (split,)
    out_specs = (split, split) + (P(),) * 12
    return jax.shard_map(
        per_device, mesh=mesh, in_specs=in_specs, out_specs=out_specs, check_vma=False
    )
```

```python
import functools

import jax
import jax.numpy as jnp
from jax import lax
from jax.experimental import pallas as pl
from jax.experimental.pallas import tpu as pltpu
from jax.sharding import PartitionSpec as P

EPSILON = 1e-05
LANES = 128
CHUNK = 256
BF16 = jnp.bfloat16
F32 = jnp.float32
MIB = 1 << 20


def dot(a, b):
    return jnp.dot(a, b, preferred_element_type=F32)


def dot_nt(a, b):
    return lax.dot_general(a, b, (((1,), (1,)), ((), ())), preferred_element_type=F32)


def dot_tn(a, b):
    return lax.dot_general(a, b, (((0,), (0,)), ((), ())), preferred_element_type=F32)


def fold(values):
    rows, cols = values.shape
    return jnp.sum(values.reshape(rows // 8, 8, cols), axis=0)


def put_row(ref, first, row):
    for k in range(row.shape[1] // LANES):
        ref[first + k : first + k + 1, :] = row[:, k * LANES : (k + 1) * LANES]


def get_row(values, first, width):
    count = width // LANES
    return jnp.concatenate([values[first + k : first + k + 1, :] for k in range(count)], axis=1)


def sums_out(ref, *partials):
    first = 0
    for part in partials:
        row = jnp.sum(part, axis=0, keepdims=True)
        put_row(ref, first, row)
        first += row.shape[1] // LANES


def whole(shape):
    return pl.BlockSpec(shape, lambda *_: (0,) * len(shape), pipeline_mode=pl.Buffered(1))


def rows_spec(rows, cols):
    return pl.BlockSpec((rows, cols), lambda i: (i, 0))


def call(
    body, name, grid, in_specs, out_specs, out_shape, scratch=(), flops=0, moved=0, vmem=56, ident=None
):
    return pl.pallas_call(
        body,
        name=name,
        grid=grid,
        in_specs=in_specs,
        out_specs=out_specs,
        out_shape=out_shape,
        scratch_shapes=list(scratch),
        compiler_params=pltpu.CompilerParams(
            vmem_limit_bytes=vmem * MIB, collective_id=ident, has_side_effects=ident is not None
        ),
        cost_estimate=pl.CostEstimate(flops=flops, bytes_accessed=moved, transcendentals=0),
    )


def shape(dims, kind=F32):
    return jax.ShapeDtypeStruct(dims, kind)


def everyone():
    batch, height = lax.axis_index("batch"), lax.axis_index("height")
    size_b, size_h = lax.axis_size("batch"), lax.axis_size("height")
    row = [(lax.rem(batch + k, size_b), height) for k in range(1, size_b)]
    return row, [(batch, lax.rem(height + k, size_h)) for k in range(1, size_h)]


def signal(peers):
    barrier = pltpu.get_barrier_semaphore()
    for one in peers:
        pl.semaphore_signal(barrier, inc=1, device_id=one, device_id_type=pl.DeviceIdType.MESH)


def signal_all():
    row, column = everyone()
    signal(row + column)


def wait_all():
    row, column = everyone()
    pl.semaphore_wait(pltpu.get_barrier_semaphore(), len(row + column))


def wait_partners():
    pl.semaphore_wait(pltpu.get_barrier_semaphore(), len(partners()))


def greet(peers):
    signal(peers)
    pl.semaphore_wait(pltpu.get_barrier_semaphore(), len(peers))


def exchange_scratch(rows):
    size_b, size_h = lax.axis_size("batch"), lax.axis_size("height")
    dma = pltpu.SemaphoreType.DMA
    return [
        pltpu.VMEM((rows, LANES), F32),
        pltpu.VMEM((size_b, rows, LANES), F32),
        pltpu.VMEM((size_h, rows, LANES), F32),
        dma((size_b - 1,)),
        dma((size_b,)),
        dma((size_h - 1,)),
        dma((size_h,)),
    ]


def exchange(scratch, epilogue, params, outs):
    stat, got_b, got_h, send_b, recv_b, send_h, recv_h = scratch
    me_b, me_h = lax.axis_index("batch"), lax.axis_index("height")
    row, column = everyone()

    def spread(src, got, me, targets, send, recv):
        size = got.shape[0]
        copies = []
        for k, target in enumerate(targets):
            copies.append(remote(src, got.at[me], send.at[k], recv.at[me], target))
            copies[-1].start()
        for k, target in enumerate(targets):
            other = lax.rem(me + (size - 1 - k), size)
            remote(src, got.at[other], send.at[k], recv.at[other], target).wait_recv()
        total = got[0]
        for k in range(1, size):
            total = total + got[k]
        return total, copies

    got_b[me_b] = stat[...]
    part, copies_b = spread(stat, got_b, me_b, row, send_b, recv_b)
    got_h[me_h] = part
    total, copies_h = spread(got_h.at[me_h], got_h, me_h, column, send_h, recv_h)
    epilogue(total, params, outs)
    run(copies_b + copies_h, "wait_send")


def norm_terms(total, first, width, cells):
    average = get_row(total, first, width) * (1.0 / cells)
    meansq = get_row(total, first + width // LANES, width) * (1.0 / cells)
    inverse = lax.rsqrt(meansq - average * average + EPSILON)
    return inverse, -average * inverse


def fill(ref, rows):
    for k, row in enumerate(rows):
        ref[k : k + 1, :] = row
    ref[len(rows) :, :] = jnp.zeros((8 - len(rows), ref.shape[1]), F32)


def act_rows(inverse, offset, gain, shift):
    return [
        inverse,
        offset,
        0.5 * gain,
        0.5 * shift,
        0.5 * gain * inverse,
        0.5 * (shift + gain * offset),
    ]


def first_totals(cells_in, cells_out, width, wide, total, params, outs):
    gain, shift = as_row(params[0]), as_row(params[1])
    fill(outs[0], act_rows(*norm_terms(total, 0, width, cells_in), gain, shift))
    fill(outs[1], list(norm_terms(total, 2 * width // LANES, wide, cells_out)))


def mid_totals(cells_out, width, total, params, outs):
    gain, shift = as_row(params[0]), as_row(params[1])
    fill(outs[0], act_rows(*norm_terms(total, 0, width, cells_out), gain, shift))


def last_totals(cells_out, wide, total, params, outs):
    gain_last, shift_last, gain_side, shift_side, side = params
    inverse, offset = norm_terms(total, 0, wide, cells_out)
    inverse_s, offset_s = side[0:1, :], side[1:2, :]
    gain_l, gain_s = 0.5 * as_row(gain_last), 0.5 * as_row(gain_side)
    shift = 0.5 * (as_row(shift_last) + as_row(shift_side))
    scales = [gain_l * inverse, gain_s * inverse_s, gain_l * offset + gain_s * offset_s + shift]
    fill(outs[0], [inverse, offset, inverse_s, offset_s] + scales)


def back_rows(scale, total_up, cross, cells):
    return [0.5 * scale, -scale * total_up * (1.0 / cells), -scale * cross * (1.0 / cells)]


def folded(rows, inverse, offset):
    scale, base, cross = rows
    return [scale, cross * inverse, base + cross * offset]


def out_totals(cells_out, wide, total, params, outs):
    coef = params[0]
    step = wide // LANES
    total_up, last_raw, side_raw = [0.5 * get_row(total, k * step, wide) for k in range(3)]
    inverse_l, offset_l, inverse_s, offset_s = [coef[k : k + 1, :] for k in range(4)]
    last_cross = inverse_l * last_raw + offset_l * total_up
    side_cross = inverse_s * side_raw + offset_s * total_up
    rows_l = back_rows(2.0 * coef[4:5, :], total_up, last_cross, cells_out)
    rows_s = back_rows(2.0 * coef[5:6, :], total_up, side_cross, cells_out)
    fill(outs[0], folded(rows_l, inverse_l, offset_l) + folded(rows_s, inverse_s, offset_s))
    fill(outs[1], [total_up, last_cross, side_cross])


def inner_totals(cells, width, total, params, outs):
    coef = params[0]
    total_up = 0.5 * get_row(total, 0, width)
    cross = 0.5 * get_row(total, width // LANES, width)
    fill(outs[0], back_rows(2.0 * coef[4:5, :], total_up, cross, cells))
    fill(outs[1], [total_up, cross])


def half_silu(half):
    return half + half * jnp.tanh(half)


def slope_twice(half, th):
    return (1.0 + th) * (1.0 + half * (1.0 - th))


def to_neighbour(copies, moves_up, what):
    height, size = lax.axis_index("height"), lax.axis_size("height")
    sends = height > 0 if moves_up else height < size - 1
    gets = height < size - 1 if moves_up else height > 0
    if what == "start":
        pl.when(sends)(lambda: run(copies, "start"))
    else:
        pl.when(sends)(lambda: run(copies, "wait_send"))
        pl.when(gets)(lambda: run(copies, "wait_recv"))


def planes_matrix(rows, cols, inverse):
    px, q, half = rows * cols, rows * cols // 4, cols // 2
    place = lax.broadcasted_iota(jnp.int32, (px, px), 1 if inverse else 0)
    pixel = lax.broadcasted_iota(jnp.int32, (px, px), 0 if inverse else 1)
    plane, inner = place // q, place % q
    source = (2 * (inner // half) + plane // 2) * cols + 2 * (inner % half) + plane % 2
    return (source == pixel).astype(F32).astype(BF16)


def row_matrix(count, cols):
    size, half = count * cols, cols // 2
    place = lax.broadcasted_iota(jnp.int32, (size, size), 0)
    pixel = lax.broadcasted_iota(jnp.int32, (size, size), 1)
    source = place // cols * cols + 2 * (place % half) + place % cols // half
    return (source == pixel).astype(F32).astype(BF16)


def spread_weights(w, out):
    gw, width = w.shape[1], w.shape[2]
    group = (lax.broadcasted_iota(jnp.int32, (gw, width), 1) % CHUNK) // gw
    for tap in range(9):
        rows = w[tap].astype(F32)
        for g in range(CHUNK // gw):
            out[tap, g * gw : (g + 1) * gw, :] = jnp.where(group == g, rows, 0.0).astype(BF16)


def as_row(ref):
    return ref[...].reshape(1, ref.shape[0])


def first_body(
    per, px, q, totals, img, w1, ws, gain, shift, xp, pre, side, coef, side_coef, acc, acc_s, perm, *ex
):
    step = pl.program_id(0)
    mid, wide = w1.shape[1], ws.shape[1]

    @pl.when(step == 0)
    def _():
        acc[...] = jnp.zeros_like(acc)
        acc_s[...] = jnp.zeros_like(acc_s)
        perm[...] = planes_matrix(img.shape[1], img.shape[2], False)
        signal_all()

    for k in range(per):
        flat = img[k].reshape(px, img.shape[3])
        moved = dot(perm[...], flat).astype(BF16)
        xp[k * px : (k + 1) * px, :] = moved
        for c in range(0, mid, CHUNK):
            cols = slice(c, c + CHUNK)
            part = dot(moved, w1[:, cols])
            pre[k * px : (k + 1) * px, cols] = part
            acc[0:8, cols] += fold(part)
            acc[8:16, cols] += fold(part * part)
    even = jnp.concatenate([xp[k * px : k * px + q, :] for k in range(per)], axis=0)
    for c in range(0, wide, CHUNK):
        cols = slice(c, c + CHUNK)
        part = dot(even, ws[:, cols])
        side[:, cols] = part
        acc_s[0:8, cols] += fold(part)
        acc_s[8:16, cols] += fold(part * part)

    @pl.when(step == pl.num_programs(0) - 1)
    def _():
        sums_out(ex[0], acc[0:8, :], acc[8:16, :], acc_s[0:8, :], acc_s[8:16, :])
        wait_all()
        exchange(ex, totals, [gain, shift], [coef, side_coef])


def conv_body(per, px, q, totals, pre, halo, w1, coef, w, gain, shift, mid, coef2, *scr):
    a00, a01, a10, a11, wbd, perm, acc, *ex = scr
    step = pl.program_id(0)
    width = w1.shape[1]

    @pl.when(step == 0)
    def _():
        acc[...] = jnp.zeros_like(acc)
        spread_weights(w, wbd)
        perm[...] = row_matrix(per, halo.shape[1])
        signal_all()

    scale, offset = coef[4:5, :], coef[5:6, :]
    flat = halo[...].reshape(per * 32, halo.shape[2])
    rim = half_silu(dot(dot(perm[...], flat).astype(BF16), w1[...]) * scale + offset)
    rim = jnp.where(lax.axis_index("height") > 0, rim, 0.0).astype(BF16)
    rim = rim.reshape(per, 2, 16, width)
    a10[:, 0:16, :] = rim[:, 0]
    a11[:, 0:16, :] = rim[:, 1]
    for plane, ref, top in ((0, a00, 0), (1, a01, 0), (2, a10, 16), (3, a11, 16)):
        half = pre[:, plane] * scale[None] + offset[None]
        ref[:, top : top + q, :] = half_silu(half).astype(BF16)
    rows = per * q
    first_col = lax.broadcasted_iota(jnp.int32, (rows, CHUNK), 0) % 16 == 0
    for c in range(0, width, CHUNK):
        cols = slice(c, c + CHUNK)

        def tap(ref, top, row, col):
            return dot(ref[:, top : top + q, cols].reshape(rows, CHUNK), wbd[row * 3 + col, :, cols])

        straight = (
            tap(a00, 0, 1, 1)
            + tap(a01, 0, 1, 2)
            + tap(a10, 16, 2, 1)
            + tap(a11, 16, 2, 2)
            + tap(a10, 0, 0, 1)
            + tap(a11, 0, 0, 2)
        )
        moved = tap(a01, 0, 1, 0) + tap(a11, 16, 2, 0) + tap(a11, 0, 0, 0)
        part = straight + jnp.where(first_col, 0.0, pltpu.roll(moved, 1, 0))
        mid[:, cols] = part
        acc[0:8, cols] += fold(part)
        acc[8:16, cols] += fold(part * part)

    @pl.when(step == pl.num_programs(0) - 1)
    def _():
        sums_out(ex[0], acc[0:8, :], acc[8:16, :])
        wait_all()
        exchange(ex, totals, [gain, shift], [coef2])


def last_body(per, q, totals, mid, coef, w, gl, sl, gs, ss, side_coef, act, pre, coef3, rim, acc, *ex):
    step = pl.program_id(0)
    width = mid.shape[1]

    @pl.when(step == 0)
    def _():
        acc[...] = jnp.zeros_like(acc)
        signal_all()

    top = mid[...].reshape(per, q, width)[:, 0:16] * coef[0:1, :][None] + coef[1:2, :][None]
    rim[...] = top.astype(BF16)
    half = mid[...] * coef[4:5, :] + coef[5:6, :]
    act[...] = half_silu(half).astype(BF16)
    for c in range(0, w.shape[1], CHUNK):
        cols = slice(c, c + CHUNK)
        part = dot(act[...], w[:, cols])
        pre[:, cols] = part
        acc[0:8, cols] += fold(part)
        acc[8:16, cols] += fold(part * part)

    @pl.when(step == pl.num_programs(0) - 1)
    def _():
        sums_out(ex[0], acc[0:8, :], acc[8:16, :])
        wait_all()
        exchange(ex, totals, [gl, sl, gs, ss, side_coef], [coef3])


def rim_copy(rim, halo, per, step, send, recv):
    images = pl.ds(step * per, per)
    return remote(rim.at[images], halo.at[images], send.at[step], recv.at[step], upper_lower()[1])


def rim_finish(rim, halo, per, send, recv):
    copies = [rim_copy(rim, halo, per, s, send, recv) for s in range(rim.shape[0] // per)]
    to_neighbour(copies, True, "wait")


def out_parts(last, side, cot, coef, cols):
    half = last[:, cols] * coef[4:5, cols] + side[:, cols] * coef[5:6, cols] + coef[6:7, cols]
    th = jnp.tanh(half)
    moved = half * th
    up = cot[:, cols].astype(F32) * ((1.0 + th) * (1.0 + (half - moved)))
    return half + moved, up


def out_body(last, side, cot, coef, out, stat, acc):
    step = pl.program_id(0)

    @pl.when(step == 0)
    def _():
        acc[...] = jnp.zeros_like(acc)

    for c in range(0, last.shape[1], CHUNK):
        cols = slice(c, c + CHUNK)
        value, up = out_parts(last, side, cot, coef, cols)
        out[:, cols] = value.astype(BF16)
        acc[0:8, cols] += fold(up)
        acc[8:16, cols] += fold(up * last[:, cols])
        acc[16:24, cols] += fold(up * side[:, cols])

    @pl.when(step == pl.num_programs(0) - 1)
    def _():
        sums_out(stat, acc[0:8, :], acc[8:16, :], acc[16:24, :])


def last_grad_body(totals, last, side, cot, coef, act, stat, rim, lg, sg, g_last, grads, halo, *scr):
    acc, back, send, recv, *ex = scr
    step = pl.program_id(0)
    row = remote(rim, halo, send, recv, upper_lower()[1])

    @pl.when(step == 0)
    def _():
        signal_all()
        acc[...] = jnp.zeros_like(acc)
        ex[0][...] = stat[...]
        wait_all()
        exchange(ex, totals, [coef], [back, grads])
        to_neighbour([row], True, "start")

    for c in range(0, last.shape[1], CHUNK):
        cols = slice(c, c + CHUNK)
        _, part = out_parts(last, side, cot, coef, cols)
        down = part * back[0:1, cols] + last[:, cols] * back[1:2, cols] + back[2:3, cols]
        down = down.astype(BF16)
        lg[:, cols] = down
        acc[:, cols] += dot_tn(act[...], down)
        down = part * back[3:4, cols] + side[:, cols] * back[4:5, cols] + back[5:6, cols]
        sg[:, cols] = down.astype(BF16)

    @pl.when(step == pl.num_programs(0) - 1)
    def _():
        g_last[...] = acc[...].astype(BF16)
        to_neighbour([row], True, "wait")


def side_grad_body(per, q, hook, sg, even, g_side, acc):
    step = pl.program_id(0)

    @pl.when(step == 0)
    def _():
        acc[...] = jnp.zeros_like(acc)

    hook(0)
    flat = even[...].reshape(per * q, even.shape[3])
    for c in range(0, sg.shape[1], CHUNK):
        cols = slice(c, c + CHUNK)
        acc[:, cols] += dot_tn(flat, sg[:, cols])

    @pl.when(step == pl.num_programs(0) - 1)
    def _():
        g_side[...] = acc[...].astype(BF16)


def mid_back_body(per, q, totals, hook, lg, wl, mid, coef, up, coef5, grads, halo, *scr):
    acc, rim, send, recv, *ex = scr
    hook(-1)
    step = pl.program_id(0)

    @pl.when(step == 0)
    def _():
        acc[...] = jnp.zeros_like(acc)

    hook(0)
    for c in range(0, mid.shape[1], CHUNK):
        cols = slice(c, c + CHUNK)
        if c == 2 * CHUNK:
            hook(1)
        part = dot_nt(lg[...], wl[cols, :])
        normed = mid[:, cols] * coef[0:1, cols] + coef[1:2, cols]
        half = normed * coef[2:3, cols] + coef[3:4, cols]
        part = part * slope_twice(half, jnp.tanh(half))
        up[:, cols] = part
        rim[pl.ds(step * per, per), :, cols] = part.reshape(per, q, CHUNK)[:, 0:16].astype(BF16)
        acc[0:8, cols] += fold(part)
        acc[8:16, cols] += fold(part * normed)
    to_neighbour([rim_copy(rim, halo, per, step, send, recv)], True, "start")

    @pl.when(step == pl.num_programs(0) - 1)
    def _():
        sums_out(ex[0], acc[0:8, :], acc[8:16, :])
        exchange(ex, totals, [coef], [coef5, grads])
        rim_finish(rim, halo, per, send, recv)


def conv_back_body(
    per, px, q, totals, hook, mup, mid, rim_up, rim_normed, pre, coef2, back, coef, w, *refs
):
    up, g_mid, coef6, grads, mg, mgs, acc, acc_g, wbd, *ex = refs
    hook(-1)
    step = pl.program_id(0)
    width = mid.shape[1]
    rows = per * q

    @pl.when(step == 0)
    def _():
        acc[...] = jnp.zeros_like(acc)
        acc_g[...] = jnp.zeros_like(acc_g)
        spread_weights(w, wbd)

    ext = q + 16
    below = lax.axis_index("height") < lax.axis_size("height") - 1
    last_col = lax.broadcasted_iota(jnp.int32, (rows, CHUNK), 0) % 16 == 15
    last_rim = lax.broadcasted_iota(jnp.int32, (per * 16, CHUNK), 0) % 16 == 15
    for c in range(0, width, CHUNK):
        cols = slice(c, c + CHUNK)
        hook(c // CHUNK)
        normed = mid[:, cols] * coef2[0:1, cols] + coef2[1:2, cols]
        grad = (mup[:, cols] * back[0:1, cols] + back[1:2, cols] + normed * back[2:3, cols]).astype(BF16)
        mg[:, 0:q, cols] = grad.reshape(per, q, CHUNK)
        grad = pltpu.roll(grad.astype(F32), rows - 1, 0)
        mgs[:, 0:q, cols] = jnp.where(last_col, 0.0, grad).astype(BF16).reshape(per, q, CHUNK)
        rim = rim_up[:, :, cols].astype(F32).reshape(per * 16, CHUNK) * back[0:1, cols] + back[1:2, cols]
        rim = rim + rim_normed[:, :, cols].astype(F32).reshape(per * 16, CHUNK) * back[2:3, cols]
        rim = jnp.where(below, rim, 0.0).astype(BF16)
        mg[:, q:ext, cols] = rim.reshape(per, 16, CHUNK)
        rim = pltpu.roll(rim.astype(F32), per * 16 - 1, 0)
        mgs[:, q:ext, cols] = jnp.where(last_rim, 0.0, rim).astype(BF16).reshape(per, 16, CHUNK)
        views = [ref[:, top : top + q, cols].reshape(rows, CHUNK) for top in (0, 16) for ref in (mg, mgs)]
        plans = (
            (0, ((1, 1, 0),)),
            (1, ((1, 2, 0), (1, 0, 1))),
            (2, ((2, 1, 0), (0, 1, 2))),
            (3, ((2, 2, 0), (2, 0, 1), (0, 2, 2), (0, 0, 3))),
        )
        for plane, taps in plans:
            total = None
            for row, col, view in taps:
                part = dot_nt(views[view], wbd[row * 3 + col, :, cols])
                total = part if total is None else total + part
            normed = pre[:, plane, :, cols].reshape(rows, CHUNK) * coef[0:1, cols] + coef[1:2, cols]
            half = normed * coef[2:3, cols] + coef[3:4, cols]
            th = jnp.tanh(half)
            act = (half + half * th).astype(BF16)
            total = total * slope_twice(half, th)
            up[:, plane, :, cols] = total.reshape(per, q, CHUNK).astype(BF16)
            acc[0:8, cols] += fold(total)
            acc[8:16, cols] += fold(total * normed)
            for row, col, view in taps:
                acc_g[row * 3 + col, :, cols] += dot_tn(act, views[view])

    @pl.when(step == pl.num_programs(0) - 1)
    def _():
        sums_out(ex[0], acc[0:8, :], acc[8:16, :])
        exchange(ex, totals, [coef], [coef6, grads])
        group = (lax.broadcasted_iota(jnp.int32, (32, width), 1) % CHUNK) // 32
        for tap in range(9):
            total = jnp.zeros((32, width), F32)
            for g in range(CHUNK // 32):
                total = total + jnp.where(group == g, acc_g[tap, g * 32 : (g + 1) * 32, :], 0.0)
            g_mid[tap] = total.astype(BF16)


def first_back_body(hook, up, pre, coef, back, xp, fg, g_first, acc):
    hook(-1)
    step = pl.program_id(0)

    @pl.when(step == 0)
    def _():
        acc[...] = jnp.zeros_like(acc)

    for c in range(0, up.shape[1], CHUNK):
        cols = slice(c, c + CHUNK)
        hook(c // CHUNK)
        normed = pre[:, cols] * coef[0:1, cols] + coef[1:2, cols]
        down = up[:, cols].astype(F32) * back[0:1, cols] + back[1:2, cols]
        down = (down + normed * back[2:3, cols]).astype(BF16)
        fg[:, cols] = down
        acc[:, cols] += dot_tn(xp[...], down)

    @pl.when(step == pl.num_programs(0) - 1)
    def _():
        g_first[...] = acc[...].astype(BF16)


def image_back_body(per, px, q, hook, fg, w1, sg, ws, out):
    hook(-1)
    for c in range(0, w1.shape[0], CHUNK):
        cols = slice(c, c + CHUNK)
        hook(c // CHUNK)
        side_back = dot_nt(sg[...], ws[cols, :])
        for k in range(per):
            part = dot_nt(fg[k * px : (k + 1) * px, :], w1[cols, :])
            even = part[0:q] + side_back[k * q : (k + 1) * q]
            out[k * px : k * px + q, cols] = even.astype(BF16)
            out[k * px + q : (k + 1) * px, cols] = part[q:].astype(BF16)


def place_body(px, planes, last, side, first, taps, wide_g, mid_g, first_g, *refs):
    out, last_out, side_out, first_out, taps_out = refs[:5]
    perm = refs[-1]

    @pl.when(pl.program_id(0) == 0)
    def _():
        perm[...] = planes_matrix(out.shape[1], out.shape[2], True)
        taps_out[...] = taps[...].astype(F32)
        rows = [first_g[1:2], first_g[0:1], mid_g[1:2], mid_g[0:1], wide_g[1:2], wide_g[0:1]]
        for ref, row in zip(refs[5:-1], rows + [wide_g[2:3], wide_g[0:1]]):
            ref[...] = row.reshape(ref.shape)

    for k in range(out.shape[0]):
        part = dot(perm[...], planes[k * px : (k + 1) * px, :]).astype(BF16)
        out[k] = part.reshape(out.shape[1:])
    last_out[...] = last[...].astype(F32)
    side_out[...] = side[...].astype(F32)
    first_out[...] = first[...].astype(F32)


def digit(axis, bit):
    return lax.rem(lax.div(lax.axis_index(axis), 1 << bit), 2)


def peer(axis, bit):
    batch, height = lax.axis_index("batch"), lax.axis_index("height")
    move = (1 - 2 * digit(axis, bit)) * (1 << bit)
    return (batch + move, height) if axis == "batch" else (batch, height + move)


def orders():
    bits_b = lax.axis_size("batch").bit_length() - 1
    bits_h = lax.axis_size("height").bit_length() - 1
    across = [("batch", k) for k in range(1, bits_b)]
    half = len(across) // 2
    x_bits, y_bits = across[:half], across[half:]
    z_bits = [("height", k) for k in range(bits_h)]
    return [x_bits + y_bits + z_bits, y_bits + x_bits + z_bits]


def stage_count():
    return len(orders()[0])


def lengths(rows):
    kept = [rows]
    for _ in range(stage_count()):
        kept.append(kept[-1] // 2 if kept[-1] % 32 == 0 else kept[-1])
    return kept


def landing(rows):
    return sum(lengths(rows)[1:])


def upper_lower():
    batch, height = lax.axis_index("batch"), lax.axis_index("height")
    size = lax.axis_size("height")
    return [(batch, lax.rem(height + 1, size)), (batch, lax.rem(height + size - 1, size))]


def partners():
    return [peer("batch", 0)] + [peer(axis, bit) for axis, bit in orders()[0]]


def remote(src, dst, send, recv, target):
    return pltpu.make_async_remote_copy(
        src_ref=src,
        dst_ref=dst,
        send_sem=send,
        recv_sem=recv,
        device_id=target,
        device_id_type=pl.DeviceIdType.MESH,
    )


class Flow:
    def __init__(self, rows, width, own, got, send, recv):
        self.own, self.got, self.send, self.recv = own, got, send, recv
        self.kept = lengths(rows)
        self.orders = orders()
        self.cols = [slice(0, width // 2), slice(width // 2, width)]
        self.low = []
        for order in self.orders:
            low = [0]
            for s, (axis, bit) in enumerate(order):
                move = digit(axis, bit) * self.kept[s + 1] if self.halved(s) else 0
                low.append(low[-1] + move)
            self.low.append(low)

    def halved(self, s):
        return self.kept[s + 1] < self.kept[s]

    def rows(self, first, count):
        return pl.ds(pl.multiple_of(first, 16), count)

    def keep(self, k, s):
        return self.rows(self.low[k][s], self.kept[s])

    def away(self, k, s):
        if not self.halved(s):
            return self.keep(k, s)
        axis, bit = self.orders[k][s]
        return self.rows(self.low[k][s] + (1 - digit(axis, bit)) * self.kept[s + 1], self.kept[s + 1])

    def place(self, s):
        return pl.ds(sum(self.kept[1 : s + 1]), self.kept[s + 1])

    def scatter(self, k, s):
        return remote(
            self.own.at[self.away(k, s), self.cols[k]],
            self.got.at[self.place(s), self.cols[k]],
            self.send.at[0, k, s],
            self.recv.at[0, k, s],
            peer(*self.orders[k][s]),
        )

    def scatter_start(self, s):
        for k in range(2):
            self.scatter(k, s).start()

    def scatter_finish(self, s):
        for k in range(2):
            self.scatter(k, s).wait()
            rows, cols = self.keep(k, s + 1), self.cols[k]
            total = self.own[rows, cols].astype(F32) + self.got[self.place(s), cols].astype(F32)
            self.own[rows, cols] = total.astype(BF16)

    def gather(self, k, s, rows):
        return remote(
            self.own.at[rows, self.cols[k]],
            self.own.at[rows, self.cols[k]],
            self.send.at[1, k, s],
            self.recv.at[1, k, s],
            peer(*self.orders[k][s]),
        )

    def gather_start(self, s):
        for k in range(2):
            if self.halved(s):
                self.gather(k, s, self.keep(k, s + 1)).start()

    def gather_finish(self, s):
        for k in range(2):
            if self.halved(s):
                self.gather(k, s, self.keep(k, s + 1)).wait_send()
                self.gather(k, s, self.away(k, s)).wait_recv()

    def moves(self, s, hbm, sems, out):
        copies = []
        for k in range(2):
            here = self.own.at[self.keep(k, s), self.cols[k]]
            there = hbm.at[self.keep(k, s), self.cols[k]]
            copies.append(pltpu.make_async_copy(*((here, there) if out else (there, here)), sems.at[k]))
        return copies


def run(copies, what):
    for copy in copies:
        getattr(copy, what)()


def own_half(ref):
    half = ref.shape[0] // 2
    return ref.at[pl.ds(pl.multiple_of(lax.axis_index("batch") % 2 * half, 16), half)]


def other_half(ref):
    half = ref.shape[0] // 2
    return ref.at[pl.ds(pl.multiple_of((1 - lax.axis_index("batch") % 2) * half, 16), half)]


def add_into(ref, other, step=64):
    for first in range(0, other.shape[0], step):
        rows = slice(first, min(first + step, other.shape[0]))
        ref[rows, :] = (ref[rows, :].astype(F32) + other[rows, :].astype(F32)).astype(BF16)


def carrying(body, counts, carry):
    def kernel(*refs):
        groups, first = [], 0
        for count in counts:
            groups.append(refs[first : first + count])
            first += count
        ins, c_ins, outs, c_outs, scr = groups
        c_scr = refs[first:]
        step = pl.program_id(0)
        points, last = carry(c_ins, c_outs, c_scr)

        def hook(point):
            for (when, where), action in points:
                if where == point:
                    pl.when(step == when)(action)

        body(hook, *ins, *outs, *scr)
        for action in last:
            pl.when(step == pl.num_programs(0) - 1)(action)

    return kernel


def carry_core(c_ins, c_outs, c_scr):
    (g_last,), (mate_last,), (send, recv) = c_ins, c_outs, c_scr
    copy = remote(other_half(g_last), mate_last, send, recv, peer("batch", 0))

    def start():
        greet([peer("batch", 0)])
        copy.start()

    return [((0, 0), start)], [copy.wait]


def carry_mid(c_ins, c_outs, c_scr):
    g_last, mate_last, g_side = c_ins
    mate_side, state_last = c_outs
    own, got, tmp, local, core, send, recv = c_scr
    flow = Flow(own.shape[0], own.shape[1], own, got, send, recv)
    copy = remote(other_half(g_side), mate_side, core.at[0], core.at[1], peer("batch", 0))
    loads = [
        pltpu.make_async_copy(own_half(g_last), own, local.at[0]),
        pltpu.make_async_copy(mate_last, tmp, local.at[1]),
    ]

    def start():
        run(loads, "start")
        signal_all()

    def enter():
        wait_all()
        copy.start()

    def first():
        run(loads, "wait")
        add_into(own, tmp)
        flow.scatter_start(0)

    def finish():
        flow.scatter_finish(0)
        dumps = flow.moves(1, state_last, local, True)
        run(dumps, "start")
        copy.wait()
        run(dumps, "wait")

    return [((0, -1), start), ((0, 0), enter), ((0, 1), first)], [finish]


def inner_stages(flow, done, first, until):
    stages = stage_count()

    def down(s):
        def action():
            flow.scatter_finish(s)
            if s + 1 < stages:
                flow.scatter_start(s + 1)
                return
            for k in range(2):
                rows = flow.keep(k, stages)
                done.own[rows, flow.cols[k]] = flow.own[rows, flow.cols[k]]
            done.gather_start(s)

        return action

    def back(s):
        def action():
            done.gather_finish(s)
            if s > until:
                done.gather_start(s - 1)

        return action

    return [down(s) for s in range(first, stages)] + [back(s) for s in range(stages - 1, until - 1, -1)]


def carry_conv(c_ins, c_outs, c_scr):
    state_last, g_side, mate_side = c_ins
    part_last, state_side = c_outs
    own_l, got_l, full_l, own_s, got_s, tmp, local, send_l, recv_l, send_s, recv_s = c_scr
    rows, width = own_l.shape
    last = Flow(rows, width, own_l, got_l, send_l, recv_l)
    done = Flow(rows, width, full_l, None, send_l, recv_l)
    side = Flow(rows, width, own_s, got_s, send_s, recv_s)
    loads_l = last.moves(1, state_last, local, False)
    loads_s = [
        pltpu.make_async_copy(own_half(g_side), own_s, local.at[2]),
        pltpu.make_async_copy(mate_side, tmp, local.at[3]),
    ]
    inner = inner_stages(last, done, 1, 3)

    def start():
        run(loads_l + loads_s, "start")
        signal_all()

    def first():
        run(loads_l, "wait")
        last.scatter_start(1)
        run(loads_s, "wait")
        add_into(own_s, tmp)
        side.scatter_start(0)

    def next_side():
        side.scatter_finish(0)
        side.scatter_start(1)

    def finish():
        side.scatter_finish(1)
        dumps = done.moves(3, part_last, local, True)
        dumps += side.moves(2, state_side, local.at[pl.ds(2, 2)], True)
        run(dumps, "start")
        run(dumps, "wait")

    places = [(2, 0), (3, 2), (5, 0)]
    points = [((0, -1), start), ((0, 0), wait_all), ((0, 2), first), ((4, 0), next_side)]
    points += [(places[min(k, 2)], act) for k, act in enumerate(inner[:-1])]
    return points, [inner[-1], finish]


class Halves:
    def __init__(self, array, own, tmp, sems, core):
        mine, wide = lax.axis_index("batch") % 2, own.shape[1]
        self.own, self.tmp, self.rows = own, tmp, array.shape[0]
        self.cols = pl.ds(pl.multiple_of(mine * wide, LANES), wide)
        away = pl.ds(pl.multiple_of((1 - mine) * wide, LANES), wide)
        rows = slice(0, self.rows)
        self.load = pltpu.make_async_copy(array.at[:, self.cols], own.at[rows], sems.at[0])
        self.mate = remote(
            array.at[:, away], tmp.at[rows], core.at[0], core.at[1], peer("batch", 0)
        )

    def clear(self):
        left = (self.own.shape[0] - self.rows, self.own.shape[1])
        if left[0]:
            self.own[self.rows :, :] = jnp.zeros(left, BF16)
            self.tmp[self.rows :, :] = jnp.zeros(left, BF16)

    def add(self):
        self.load.wait()
        self.mate.wait()
        add_into(self.own, self.tmp)


def ends(src, dst, sem, core):
    return [
        pltpu.make_async_copy(src, dst, sem),
        remote(src, dst, core.at[0], core.at[1], peer("batch", 0)),
    ]


def carry_first(c_ins, c_outs, c_scr):
    part_last, state_side, g_mid = c_ins
    part_half, shard_side, part_mid = c_outs
    own_l, own_s, got_s, local, send_l, recv_l, send_s, recv_s = c_scr[:8]
    own_m, got_m, tmp_m, full_m, core, send_m, recv_m = c_scr[8:]
    taps = Flow(own_m.shape[0], own_m.shape[1], own_m, got_m, send_m, recv_m)
    done = Flow(own_m.shape[0], own_m.shape[1], full_m, None, send_m, recv_m)
    halves = Halves(g_mid, own_m, tmp_m, local.at[pl.ds(4, 1)], core)
    chain = inner_stages(taps, done, 0, 3)
    rows, width = own_l.shape
    last = Flow(rows, width, own_l, None, send_l, recv_l)
    side = Flow(rows, width, own_s, got_s, send_s, recv_s)
    stages = stage_count()
    loads = last.moves(3, part_last, local, False)
    loads += side.moves(2, state_side, local.at[pl.ds(2, 2)], False)

    def start():
        run(loads, "start")
        halves.load.start()
        halves.clear()
        signal(partners())

    def enter():
        wait_partners()
        halves.mate.start()

    def first():
        run(loads, "wait")
        last.gather_start(2)
        side.scatter_start(2)
        halves.add()
        taps.scatter_start(0)

    def next_last(s):
        def action():
            last.gather_finish(s)
            last.gather_start(s - 1)

        return action

    def next_side(s):
        def action():
            side.scatter_finish(s)
            if s + 1 < stages:
                side.scatter_start(s + 1)

        return action

    def finish():
        last.gather_finish(0)
        dumps = last.moves(0, part_half, local, True)
        dumps += side.moves(stages, shard_side, local.at[pl.ds(2, 2)], True)
        dumps += done.moves(3, part_mid, local.at[pl.ds(4, 2)], True)
        run(dumps, "start")
        run(dumps, "wait")

    points = [((0, -1), start), ((0, 0), enter), ((0, 2), first), ((2, 2), next_last(2)), ((3, 2), next_last(1))]
    places = [(3, 2), (5, 1)]
    points += [(places[min(s - 2, 1)], next_side(s)) for s in range(2, stages)]
    places = [(1, 2), (2, 2), (3, 2), (4, 2), (5, 2)]
    points += [(places[min(k, 4)], act) for k, act in enumerate(chain[:-1])]
    return points, [chain[-1], finish]


def carry_image(c_ins, c_outs, c_scr):
    part_last, shard_side, part_mid, g_first = c_ins
    all_last, all_side, all_first, all_mid = c_outs
    own_l, own_s, own_m, own_h, got_h, tmp_h, full_h, local, core = c_scr[:9]
    send_l, recv_l, send_s, recv_s, send_m, recv_m, send_h, recv_h = c_scr[9:]
    last = Flow(own_l.shape[0], own_l.shape[1], own_l, None, send_l, recv_l)
    side = Flow(own_s.shape[0], own_s.shape[1], own_s, None, send_s, recv_s)
    taps = Flow(own_m.shape[0], own_m.shape[1], own_m, None, send_m, recv_m)
    head = Flow(own_h.shape[0], own_h.shape[1], own_h, got_h, send_h, recv_h)
    done = Flow(own_h.shape[0], own_h.shape[1], full_h, None, send_h, recv_h)
    stages = stage_count()
    halves = Halves(g_first, own_h, tmp_h, local.at[pl.ds(0, 1)], core)
    loads = last.moves(0, part_last, local.at[pl.ds(1, 2)], False)
    loads += side.moves(stages, shard_side, local.at[pl.ds(3, 2)], False)
    loads += taps.moves(3, part_mid, local.at[pl.ds(5, 2)], False)
    few = slice(0, all_mid.shape[0])
    ends_last = ends(own_l, own_half(all_last), local.at[1], core.at[pl.ds(2, 2)])
    ends_side = ends(own_s, own_half(all_side), local.at[3], core.at[pl.ds(4, 2)])
    ends_mid = ends(own_m.at[few], all_mid.at[:, halves.cols], local.at[5], core.at[pl.ds(6, 2)])
    ends_head = ends(full_h, all_first.at[:, halves.cols], local.at[0], core.at[pl.ds(8, 2)])

    def start():
        run(loads, "start")
        halves.load.start()
        signal(partners())

    def enter():
        wait_partners()
        halves.mate.start()

    def second():
        run(loads, "wait")
        side.gather_start(stages - 1)
        taps.gather_start(2)
        run(ends_last, "start")

    def third():
        halves.add()
        head.scatter_start(0)

    def back(flow, s, then):
        def action():
            flow.gather_finish(s)
            if s:
                flow.gather_start(s - 1)
            else:
                run(then, "start")

        return action

    def head_next(s):
        def action():
            head.scatter_finish(s)
            if s + 1 < stages:
                head.scatter_start(s + 1)

        return action

    def turn():
        for k in range(2):
            rows_k = head.keep(k, stages)
            full_h[rows_k, head.cols[k]] = own_h[rows_k, head.cols[k]]
        done.gather_start(stages - 1)

    def finish():
        run(ends_last + ends_side + ends_mid + ends_head, "wait")

    points = [((0, -1), start), ((0, 0), enter), ((0, 2), second), ((2, 0), third), ((3, 0), back(taps, 2, None))]
    points += [((5, 0), back(side, stages - 1, None)), ((5, 2), head_next(0))]
    points += [((7, 0), head_next(1)), ((7, 2), back(taps, 1, None))]
    places = [(8, 2), (11, 0)]
    points += [(places[min(k, 1)], back(side, s, None)) for k, s in enumerate(range(stages - 2, 0, -1))]
    places = [(9, 0), (10, 2)]
    points += [(places[min(s - 2, 1)], head_next(s)) for s in range(2, stages)]
    points += [(places[1], turn)]
    tail = [back(taps, 0, ends_mid)]
    tail += [back(done, s, None) for s in range(stages - 1, 1, -1)]
    tail += [back(side, 0, ends_side), back(done, 1, None), back(done, 0, ends_head), finish]
    return points, tail


def per_device(
    images,
    w_first,
    gain_first,
    shift_first,
    w_mid,
    gain_mid,
    shift_mid,
    w_last,
    gain_last,
    shift_last,
    w_side,
    gain_side,
    shift_side,
    cotangent,
):
    n, rows_in, cols_in, cin = images.shape
    mid = w_first.shape[1]
    wide = w_last.shape[1]
    gw = w_mid.shape[2]
    rows_out, cols_out = rows_in // 2, cols_in // 2
    px, q = rows_in * cols_in, rows_out * cols_out
    devices = lax.axis_size("batch") * lax.axis_size("height")
    cells_in = float(n * px * devices)
    cells_out = float(n * q * devices)
    size_h = lax.axis_size("height")
    per = 4
    steps = n // per
    rows = per * q

    anywhere = pl.BlockSpec(memory_space=pl.ANY)
    dma = pltpu.SemaphoreType.DMA
    halo_x = lax.ppermute(images[:, rows_in - 1], "height", [(i, i + 1) for i in range(size_h - 1)])
    taps = w_mid.reshape(9, gw, mid)
    size_p = per * cols_in

    eights, wide_eights = whole((8, mid)), whole((8, wide))
    xp, pre, side_pre, coef1, side_coef = call(
        functools.partial(
            first_body, per, px, q, functools.partial(first_totals, cells_in, cells_out, mid, wide)
        ),
        "first_product",
        (steps,),
        [
            pl.BlockSpec((per, rows_in, cols_in, cin), lambda s: (s, 0, 0, 0)),
            whole((cin, mid)),
            whole((cin, wide)),
            whole((mid,)),
            whole((mid,)),
        ],
        [
            rows_spec(per * px, cin),
            rows_spec(per * px, mid),
            rows_spec(rows, wide),
            eights,
            wide_eights,
        ],
        [
            shape((n * px, cin), BF16),
            shape((n * px, mid)),
            shape((n * q, wide)),
            shape((8, mid)),
            shape((8, wide)),
        ],
        [pltpu.VMEM((16, mid), F32), pltpu.VMEM((16, wide), F32), pltpu.VMEM((px, px), BF16)]
        + exchange_scratch(2 * (mid + wide) // LANES),
        flops=2 * n * (px * cin * (mid + px) + q * cin * wide),
        moved=n * px * cin * 8 + n * q * wide * 4 + cin * (mid + wide) * 2,
        ident=6,
    )(images, w_first, w_side, gain_first, shift_first)

    pre_planes = pre.reshape(n, 4, q, mid)
    planes_spec = pl.BlockSpec((per, 4, q, mid), lambda s: (s, 0, 0, 0))
    mid_pre, coef2 = call(
        functools.partial(conv_body, per, px, q, functools.partial(mid_totals, cells_out, mid)),
        "grouped_conv",
        (steps,),
        [
            planes_spec,
            pl.BlockSpec((per, cols_in, cin), lambda s: (s, 0, 0)),
            whole((cin, mid)),
            eights,
            whole((9, gw, mid)),
            whole((mid,)),
            whole((mid,)),
        ],
        [rows_spec(rows, mid), eights],
        [shape((n * q, mid)), shape((8, mid))],
        [
            pltpu.VMEM((per, q, mid), BF16),
            pltpu.VMEM((per, q, mid), BF16),
            pltpu.VMEM((per, q + 16, mid), BF16),
            pltpu.VMEM((per, q + 16, mid), BF16),
            pltpu.VMEM((9, CHUNK, mid), BF16),
            pltpu.VMEM((size_p, size_p), BF16),
            pltpu.VMEM((16, mid), F32),
        ]
        + exchange_scratch(2 * mid // LANES),
        flops=2 * n * q * mid * CHUNK * 9 + 2 * n * cols_in * cin * mid,
        moved=n * px * mid * 4 + n * q * mid * 4,
        ident=0,
    )(pre_planes, halo_x, w_first, coef1, taps, gain_mid, shift_mid)

    rim_spec = pl.BlockSpec((per, cols_out, mid), lambda s: (s, 0, 0))
    rim_shape = shape((n, cols_out, mid), BF16)
    mid_act, last_pre, coef3, rim_own = call(
        functools.partial(last_body, per, q, functools.partial(last_totals, cells_out, wide)),
        "last_product",
        (steps,),
        [rows_spec(rows, mid), eights, whole((mid, wide))] + [whole((wide,))] * 4 + [wide_eights],
        [rows_spec(rows, mid), rows_spec(rows, wide), wide_eights, rim_spec],
        [shape((n * q, mid), BF16), shape((n * q, wide)), shape((8, wide)), rim_shape],
        [pltpu.VMEM((16, wide), F32)] + exchange_scratch(2 * wide // LANES),
        flops=2 * n * q * mid * wide,
        moved=n * q * (mid * 6 + wide * 4),
        ident=7,
    )(mid_pre, coef2, w_last, gain_last, shift_last, gain_side, shift_side, side_coef)

    cot = cotangent.reshape(n * q, wide)
    stat_rows = 3 * wide // LANES
    output, stat = call(
        out_body,
        "output",
        (steps,),
        [rows_spec(rows, wide), rows_spec(rows, wide), rows_spec(rows, wide), wide_eights],
        [rows_spec(rows, wide), whole((stat_rows, LANES))],
        [shape((n * q, wide), BF16), shape((stat_rows, LANES))],
        [pltpu.VMEM((24, wide), F32)],
        flops=30 * n * q * wide,
        moved=n * q * wide * 12,
    )(last_pre, side_pre, cot, coef3)

    xp_planes = xp.reshape(n, 4, q, cin)
    half_l = mid // 2
    stages = stage_count()
    sems = dma((2, 2, stages))
    state = shape((half_l, wide), BF16)
    buf = pltpu.VMEM((half_l, wide), BF16)
    got = pltpu.VMEM((landing(half_l), wide), BF16)
    last_grad, side_grad, g_last, wide_grads, rim_normed = call(
        functools.partial(last_grad_body, functools.partial(out_totals, cells_out, wide)),
        "last_gradients",
        (steps,),
        [
            rows_spec(rows, wide),
            rows_spec(rows, wide),
            rows_spec(rows, wide),
            wide_eights,
            rows_spec(rows, mid),
            whole((stat_rows, LANES)),
            anywhere,
        ],
        [rows_spec(rows, wide), rows_spec(rows, wide), whole((mid, wide)), wide_eights, anywhere],
        [
            shape((n * q, wide), BF16),
            shape((n * q, wide), BF16),
            shape((mid, wide), BF16),
            shape((8, wide)),
            rim_shape,
        ],
        [pltpu.VMEM((mid, wide), F32), pltpu.VMEM((8, wide), F32), dma, dma]
        + exchange_scratch(stat_rows),
        flops=2 * n * q * mid * wide,
        moved=n * q * (wide * 14 + mid * 2) + mid * wide * 2,
        ident=3,
    )(last_pre, side_pre, cot, coef3, mid_act, stat, rim_own)
    g_side, mate_last = call(
        carrying(functools.partial(side_grad_body, 2 * per, q), (2, 1, 1, 1, 1), carry_core),
        "side_gradient",
        (steps // 2,),
        [
            rows_spec(2 * rows, wide),
            pl.BlockSpec((2 * per, 1, q, cin), lambda s: (s, 0, 0, 0)),
            anywhere,
        ],
        [whole((cin, wide)), anywhere],
        [shape((cin, wide), BF16), state],
        [pltpu.VMEM((cin, wide), F32), dma, dma],
        flops=2 * n * q * cin * wide,
        moved=n * q * (wide * 2 + cin * 2) + cin * wide * 2,
        ident=8,
    )(side_grad, xp_planes, g_last)

    rims = [pltpu.VMEM((n, cols_out, mid), BF16), dma((steps,)), dma((steps,))]
    inner_scratch = exchange_scratch(2 * mid // LANES)
    mid_up, coef5, mid_grads, rim_up, mate_side, state_last = call(
        carrying(
            functools.partial(mid_back_body, per, q, functools.partial(inner_totals, cells_out, mid)),
            (4, 3, 4, 2, 4 + len(inner_scratch)),
            carry_mid,
        ),
        "mid_back",
        (steps,),
        [
            rows_spec(rows, wide),
            whole((mid, wide)),
            rows_spec(rows, mid),
            eights,
            anywhere,
            anywhere,
            anywhere,
        ],
        [rows_spec(rows, mid), eights, eights] + [anywhere] * 3,
        [
            shape((n * q, mid)),
            shape((8, mid)),
            shape((8, mid)),
            rim_shape,
            state,
            state,
        ],
        [pltpu.VMEM((16, mid), F32)]
        + rims
        + inner_scratch
        + [buf, got, buf, dma((2,)), dma((2,)), sems, sems],
        flops=2 * n * q * mid * wide,
        moved=n * q * (wide * 2 + mid * 8) + mid * wide * 2,
        ident=9,
    )(last_grad, w_last, mid_pre, coef2, g_last, mate_last, g_side)

    first_up, g_mid, coef6, first_grads, part_last, state_side = call(
        carrying(
            functools.partial(
                conv_back_body, per, px, q, functools.partial(inner_totals, cells_in, mid)
            ),
            (9, 3, 4, 2, 5 + len(inner_scratch)),
            carry_conv,
        ),
        "grouped_conv_back",
        (steps,),
        [
            rows_spec(rows, mid),
            rows_spec(rows, mid),
            rim_spec,
            rim_spec,
            planes_spec,
            eights,
            eights,
            eights,
            whole((9, gw, mid)),
            anywhere,
            anywhere,
            anywhere,
        ],
        [planes_spec, whole((9, gw, mid)), eights, eights, anywhere, anywhere],
        [
            shape((n, 4, q, mid), BF16),
            shape((9, gw, mid), BF16),
            shape((8, mid)),
            shape((8, mid)),
            state,
            state,
        ],
        [
            pltpu.VMEM((per, q + 16, mid), BF16),
            pltpu.VMEM((per, q + 16, mid), BF16),
            pltpu.VMEM((16, mid), F32),
            pltpu.VMEM((9, CHUNK, mid), F32),
            pltpu.VMEM((9, CHUNK, mid), BF16),
        ]
        + inner_scratch
        + [buf, got, buf, buf, got, buf, dma((4,))]
        + [sems] * 4,
        flops=4 * n * q * mid * CHUNK * 9,
        moved=n * q * mid * 8 + n * px * mid * 6,
        vmem=60,
        ident=10,
    )(
        mid_up,
        mid_pre,
        rim_up,
        rim_normed,
        pre_planes,
        coef2,
        coef5,
        coef1,
        taps,
        state_last,
        g_side,
        mate_side,
    )

    half_m = mid // 2
    unit = 16 * (devices // 2)
    taps_rows = -(-9 * gw // unit) * unit
    buf_m = pltpu.VMEM((taps_rows, half_m), BF16)
    got_m = pltpu.VMEM((landing(taps_rows), half_m), BF16)
    first_grad, g_first, part_half, shard_side, part_mid = call(
        carrying(first_back_body, (5, 3, 2, 3, 1), carry_first),
        "first_gradient",
        (steps,),
        [
            rows_spec(per * px, mid),
            rows_spec(per * px, mid),
            eights,
            eights,
            rows_spec(per * px, cin),
            anywhere,
            anywhere,
            anywhere,
        ],
        [rows_spec(per * px, mid), whole((cin, mid)), anywhere, anywhere, anywhere],
        [
            shape((n * px, mid), BF16),
            shape((cin, mid), BF16),
            state,
            state,
            shape((taps_rows, half_m), BF16),
        ],
        [pltpu.VMEM((cin, mid), F32), buf, buf, got, dma((6,))]
        + [sems] * 4
        + [buf_m, got_m, buf_m, buf_m, dma((2,)), sems, sems],
        flops=2 * n * px * mid * cin,
        moved=n * px * (mid * 8 + cin * 2),
        ident=11,
    )(
        first_up.reshape(n * px, mid),
        pre,
        coef1,
        coef6,
        xp,
        part_last,
        state_side,
        g_mid.reshape(9 * gw, mid),
    )

    buf_h = pltpu.VMEM((cin, half_m), BF16)
    got_h = pltpu.VMEM((landing(cin), half_m), BF16)
    few = per // 2
    planes, all_last, all_side, all_first, all_mid = call(
        carrying(functools.partial(image_back_body, few, px, q), (4, 4, 1, 4, 0), carry_image),
        "image_gradient",
        (n // few,),
        [
            rows_spec(few * px, mid),
            whole((cin, mid)),
            rows_spec(few * q, wide),
            whole((cin, wide)),
        ]
        + [anywhere] * 4,
        [rows_spec(few * px, cin)] + [anywhere] * 4,
        [
            shape((n * px, cin), BF16),
            shape((mid, wide), BF16),
            shape((cin, wide), BF16),
            shape((cin, mid), BF16),
            shape((9 * gw, mid), BF16),
        ],
        [buf, buf, buf_m, buf_h, got_h, buf_h, buf_h, dma((7,)), dma((10,))] + [sems] * 8,
        flops=2 * n * px * cin * mid + 2 * n * q * cin * wide,
        moved=n * px * (mid * 2 + cin * 2) + n * q * wide * 2,
        ident=12,
    )(first_grad, w_first, side_grad, w_side, part_half, shard_side, part_mid, g_first)
    three = 3
    cuts = n // three
    vectors = [mid] * 4 + [wide] * 4
    grad_images, grad_last, grad_side, grad_first, grad_mid, *grad_vectors = call(
        functools.partial(place_body, px),
        "image_places",
        (cuts,),
        [
            rows_spec(three * px, cin),
            rows_spec(mid // cuts, wide),
            rows_spec(cin // cuts, wide),
            rows_spec(cin // cuts, mid),
            whole((9 * gw, mid)),
            wide_eights,
            eights,
            eights,
        ],
        [
            pl.BlockSpec((three, rows_in, cols_in, cin), lambda s: (s, 0, 0, 0)),
            rows_spec(mid // cuts, wide),
            rows_spec(cin // cuts, wide),
            rows_spec(cin // cuts, mid),
            whole((9 * gw, mid)),
        ]
        + [whole((k,)) for k in vectors],
        [
            shape((n, rows_in, cols_in, cin), BF16),
            shape((mid, wide)),
            shape((cin, wide)),
            shape((cin, mid)),
            shape((9 * gw, mid)),
        ]
        + [shape((k,)) for k in vectors],
        [pltpu.VMEM((px, px), BF16)],
        flops=2 * n * px * cin * px,
        moved=n * px * cin * 4 + (mid + cin) * wide * 6 + cin * mid * 6,
    )(planes, all_last, all_side, all_first, all_mid, wide_grads, mid_grads, first_grads)

    return (
        output.reshape(n, rows_out, cols_out, wide),
        grad_images,
        grad_first,
        grad_vectors[0],
        grad_vectors[1],
        grad_mid.reshape(3, 3, gw, mid),
        grad_vectors[2],
        grad_vectors[3],
        grad_last,
        grad_vectors[4],
        grad_vectors[5],
        grad_side,
        grad_vectors[6],
        grad_vectors[7],
    )


def solution(mesh):
    split = P("batch", "height", None, None)
    in_specs = (split,) + (P(),) * 12 + (split,)
    out_specs = (split, split) + (P(),) * 12
    return jax.shard_map(
        per_device, mesh=mesh, in_specs=in_specs, out_specs=out_specs, check_vma=False
    )
```

```python
import functools

import jax
import jax.numpy as jnp
from jax import lax
from jax.experimental import pallas as pl
from jax.experimental.pallas import tpu as pltpu
from jax.sharding import PartitionSpec as P

EPSILON = 1e-05
LANES = 128
CHUNK = 256
BF16 = jnp.bfloat16
F32 = jnp.float32
MIB = 1 << 20


def dot(a, b):
    return jnp.dot(a, b, preferred_element_type=F32)


def dot_nt(a, b):
    return lax.dot_general(a, b, (((1,), (1,)), ((), ())), preferred_element_type=F32)


def dot_tn(a, b):
    return lax.dot_general(a, b, (((0,), (0,)), ((), ())), preferred_element_type=F32)


def fold(values):
    rows, cols = values.shape
    return jnp.sum(values.reshape(rows // 8, 8, cols), axis=0)


def put_row(ref, first, row):
    for k in range(row.shape[1] // LANES):
        ref[first + k : first + k + 1, :] = row[:, k * LANES : (k + 1) * LANES]


def get_row(values, first, width):
    count = width // LANES
    return jnp.concatenate([values[first + k : first + k + 1, :] for k in range(count)], axis=1)


def sums_out(ref, *partials):
    first = 0
    for part in partials:
        row = jnp.sum(part, axis=0, keepdims=True)
        put_row(ref, first, row)
        first += row.shape[1] // LANES


def whole(shape):
    return pl.BlockSpec(shape, lambda *_: (0,) * len(shape), pipeline_mode=pl.Buffered(1))


def rows_spec(rows, cols):
    return pl.BlockSpec((rows, cols), lambda i: (i, 0))


def call(
    body, name, grid, in_specs, out_specs, out_shape, scratch=(), flops=0, moved=0, vmem=56, ident=None
):
    return pl.pallas_call(
        body,
        name=name,
        grid=grid,
        in_specs=in_specs,
        out_specs=out_specs,
        out_shape=out_shape,
        scratch_shapes=list(scratch),
        compiler_params=pltpu.CompilerParams(
            vmem_limit_bytes=vmem * MIB, collective_id=ident, has_side_effects=ident is not None
        ),
        cost_estimate=pl.CostEstimate(flops=flops, bytes_accessed=moved, transcendentals=0),
    )


def shape(dims, kind=F32):
    return jax.ShapeDtypeStruct(dims, kind)


def everyone():
    batch, height = lax.axis_index("batch"), lax.axis_index("height")
    size_b, size_h = lax.axis_size("batch"), lax.axis_size("height")
    row = [(lax.rem(batch + k, size_b), height) for k in range(1, size_b)]
    return row, [(batch, lax.rem(height + k, size_h)) for k in range(1, size_h)]


def signal(peers):
    barrier = pltpu.get_barrier_semaphore()
    for one in peers:
        pl.semaphore_signal(barrier, inc=1, device_id=one, device_id_type=pl.DeviceIdType.MESH)


def signal_all():
    row, column = everyone()
    signal(row + column)


def wait_all():
    row, column = everyone()
    pl.semaphore_wait(pltpu.get_barrier_semaphore(), len(row + column))


def wait_partners():
    pl.semaphore_wait(pltpu.get_barrier_semaphore(), len(partners()))


def greet(peers):
    signal(peers)
    pl.semaphore_wait(pltpu.get_barrier_semaphore(), len(peers))


def exchange_scratch(rows):
    size_b, size_h = lax.axis_size("batch"), lax.axis_size("height")
    dma = pltpu.SemaphoreType.DMA
    return [
        pltpu.VMEM((rows, LANES), F32),
        pltpu.VMEM((size_b, rows, LANES), F32),
        pltpu.VMEM((size_h, rows, LANES), F32),
        dma((size_b - 1,)),
        dma((size_b,)),
        dma((size_h - 1,)),
        dma((size_h,)),
    ]


class Exchange:
    def __init__(self, scratch):
        self.stat, self.got_b, self.got_h, self.send_b, self.recv_b, self.send_h, self.recv_h = scratch
        self.me_b, self.me_h = lax.axis_index("batch"), lax.axis_index("height")
        self.row, self.column = everyone()

    def spread(self, src, got, me, targets, send, recv):
        return [
            remote(src, got.at[me], send.at[k], recv.at[me], target) for k, target in enumerate(targets)
        ]

    def total(self, src, got, me, targets, send, recv):
        size = got.shape[0]
        for k, target in enumerate(targets):
            other = lax.rem(me + (size - 1 - k), size)
            remote(src, got.at[other], send.at[k], recv.at[other], target).wait_recv()
        total = got[0]
        for k in range(1, size):
            total = total + got[k]
        return total

    def over_batch(self):
        return self.stat, self.got_b, self.me_b, self.row, self.send_b, self.recv_b

    def over_height(self):
        return self.got_h.at[self.me_h], self.got_h, self.me_h, self.column, self.send_h, self.recv_h

    def start(self):
        run(self.spread(*self.over_batch()), "start")
        self.got_b[self.me_b] = self.stat[...]

    def turn(self):
        self.got_h[self.me_h] = self.total(*self.over_batch())
        run(self.spread(*self.over_height()), "start")

    def finish(self, epilogue, params, outs):
        epilogue(self.total(*self.over_height()), params, outs)
        run(self.spread(*self.over_batch()) + self.spread(*self.over_height()), "wait_send")


def exchange(scratch, epilogue, params, outs):
    one = Exchange(scratch)
    one.start()
    one.turn()
    one.finish(epilogue, params, outs)


def norm_terms(total, first, width, cells):
    average = get_row(total, first, width) * (1.0 / cells)
    meansq = get_row(total, first + width // LANES, width) * (1.0 / cells)
    inverse = lax.rsqrt(meansq - average * average + EPSILON)
    return inverse, -average * inverse


def fill(ref, rows):
    for k, row in enumerate(rows):
        ref[k : k + 1, :] = row
    ref[len(rows) :, :] = jnp.zeros((8 - len(rows), ref.shape[1]), F32)


def act_rows(inverse, offset, gain, shift):
    return [
        inverse,
        offset,
        0.5 * gain,
        0.5 * shift,
        0.5 * gain * inverse,
        0.5 * (shift + gain * offset),
    ]


def first_totals(cells_in, cells_out, width, wide, total, params, outs):
    gain, shift = as_row(params[0]), as_row(params[1])
    fill(outs[0], act_rows(*norm_terms(total, 0, width, cells_in), gain, shift))
    fill(outs[1], list(norm_terms(total, 2 * width // LANES, wide, cells_out)))


def mid_totals(cells_out, width, total, params, outs):
    gain, shift = as_row(params[0]), as_row(params[1])
    fill(outs[0], act_rows(*norm_terms(total, 0, width, cells_out), gain, shift))


def last_totals(cells_out, wide, total, params, outs):
    gain_last, shift_last, gain_side, shift_side, side = params
    inverse, offset = norm_terms(total, 0, wide, cells_out)
    inverse_s, offset_s = side[0:1, :], side[1:2, :]
    gain_l, gain_s = 0.5 * as_row(gain_last), 0.5 * as_row(gain_side)
    shift = 0.5 * (as_row(shift_last) + as_row(shift_side))
    scales = [gain_l * inverse, gain_s * inverse_s, gain_l * offset + gain_s * offset_s + shift]
    fill(outs[0], [inverse, offset, inverse_s, offset_s] + scales)


def back_rows(scale, total_up, cross, cells):
    return [0.5 * scale, -scale * total_up * (1.0 / cells), -scale * cross * (1.0 / cells)]


def folded(rows, inverse, offset):
    scale, base, cross = rows
    return [scale, cross * inverse, base + cross * offset]


def out_totals(cells_out, wide, total, params, outs):
    coef = params[0]
    step = wide // LANES
    total_up, last_raw, side_raw = [0.5 * get_row(total, k * step, wide) for k in range(3)]
    inverse_l, offset_l, inverse_s, offset_s = [coef[k : k + 1, :] for k in range(4)]
    last_cross = inverse_l * last_raw + offset_l * total_up
    side_cross = inverse_s * side_raw + offset_s * total_up
    rows_l = back_rows(2.0 * coef[4:5, :], total_up, last_cross, cells_out)
    rows_s = back_rows(2.0 * coef[5:6, :], total_up, side_cross, cells_out)
    fill(outs[0], folded(rows_l, inverse_l, offset_l) + folded(rows_s, inverse_s, offset_s))
    fill(outs[1], [total_up, last_cross, side_cross])


def inner_totals(cells, width, total, params, outs):
    coef = params[0]
    total_up = 0.5 * get_row(total, 0, width)
    cross = 0.5 * get_row(total, width // LANES, width)
    fill(outs[0], back_rows(2.0 * coef[4:5, :], total_up, cross, cells))
    fill(outs[1], [total_up, cross])


def half_silu(half):
    return half + half * jnp.tanh(half)


def slope_twice(half, th):
    return (1.0 + th) * (1.0 + half * (1.0 - th))


def to_neighbour(copies, moves_up, what):
    height, size = lax.axis_index("height"), lax.axis_size("height")
    sends = height > 0 if moves_up else height < size - 1
    gets = height < size - 1 if moves_up else height > 0
    if what == "start":
        pl.when(sends)(lambda: run(copies, "start"))
    else:
        pl.when(sends)(lambda: run(copies, "wait_send"))
        pl.when(gets)(lambda: run(copies, "wait_recv"))


def planes_matrix(rows, cols, inverse):
    px, q, half = rows * cols, rows * cols // 4, cols // 2
    place = lax.broadcasted_iota(jnp.int32, (px, px), 1 if inverse else 0)
    pixel = lax.broadcasted_iota(jnp.int32, (px, px), 0 if inverse else 1)
    plane, inner = place // q, place % q
    source = (2 * (inner // half) + plane // 2) * cols + 2 * (inner % half) + plane % 2
    return (source == pixel).astype(F32).astype(BF16)


def row_matrix(count, cols):
    size, half = count * cols, cols // 2
    place = lax.broadcasted_iota(jnp.int32, (size, size), 0)
    pixel = lax.broadcasted_iota(jnp.int32, (size, size), 1)
    source = place // cols * cols + 2 * (place % half) + place % cols // half
    return (source == pixel).astype(F32).astype(BF16)


def spread_weights(w, out):
    gw, width = w.shape[1], w.shape[2]
    group = (lax.broadcasted_iota(jnp.int32, (gw, width), 1) % CHUNK) // gw
    for tap in range(9):
        rows = w[tap].astype(F32)
        for g in range(CHUNK // gw):
            out[tap, g * gw : (g + 1) * gw, :] = jnp.where(group == g, rows, 0.0).astype(BF16)


def as_row(ref):
    return ref[...].reshape(1, ref.shape[0])


def first_body(
    per, px, q, totals, img, w1, ws, gain, shift, xp, pre, side, coef, side_coef, acc, acc_s, perm, *ex
):
    step = pl.program_id(0)
    mid, wide = w1.shape[1], ws.shape[1]

    @pl.when(step == 0)
    def _():
        acc[...] = jnp.zeros_like(acc)
        acc_s[...] = jnp.zeros_like(acc_s)
        perm[...] = planes_matrix(img.shape[1], img.shape[2], False)
        signal_all()

    for k in range(per):
        flat = img[k].reshape(px, img.shape[3])
        moved = dot(perm[...], flat).astype(BF16)
        xp[k * px : (k + 1) * px, :] = moved
        for c in range(0, mid, CHUNK):
            cols = slice(c, c + CHUNK)
            part = dot(moved, w1[:, cols])
            pre[k * px : (k + 1) * px, cols] = part
            acc[0:8, cols] += fold(part)
            acc[8:16, cols] += fold(part * part)
    even = jnp.concatenate([xp[k * px : k * px + q, :] for k in range(per)], axis=0)
    for c in range(0, wide, CHUNK):
        cols = slice(c, c + CHUNK)
        part = dot(even, ws[:, cols])
        side[:, cols] = part
        acc_s[0:8, cols] += fold(part)
        acc_s[8:16, cols] += fold(part * part)

    @pl.when(step == pl.num_programs(0) - 1)
    def _():
        sums_out(ex[0], acc[0:8, :], acc[8:16, :], acc_s[0:8, :], acc_s[8:16, :])
        wait_all()
        exchange(ex, totals, [gain, shift], [coef, side_coef])


def conv_body(per, px, q, totals, pre, halo, w1, coef, w, gain, shift, mid, coef2, *scr):
    a00, a01, a10, a11, wbd, perm, acc, *ex = scr
    step = pl.program_id(0)
    width = w1.shape[1]

    @pl.when(step == 0)
    def _():
        acc[...] = jnp.zeros_like(acc)
        spread_weights(w, wbd)
        perm[...] = row_matrix(per, halo.shape[1])
        signal_all()

    scale, offset = coef[4:5, :], coef[5:6, :]
    flat = halo[...].reshape(per * 32, halo.shape[2])
    rim = half_silu(dot(dot(perm[...], flat).astype(BF16), w1[...]) * scale + offset)
    rim = jnp.where(lax.axis_index("height") > 0, rim, 0.0).astype(BF16)
    rim = rim.reshape(per, 2, 16, width)
    a10[:, 0:16, :] = rim[:, 0]
    a11[:, 0:16, :] = rim[:, 1]
    for plane, ref, top in ((0, a00, 0), (1, a01, 0), (2, a10, 16), (3, a11, 16)):
        half = pre[:, plane] * scale[None] + offset[None]
        ref[:, top : top + q, :] = half_silu(half).astype(BF16)
    rows = per * q
    first_col = lax.broadcasted_iota(jnp.int32, (rows, CHUNK), 0) % 16 == 0
    for c in range(0, width, CHUNK):
        cols = slice(c, c + CHUNK)

        def tap(ref, top, row, col):
            return dot(ref[:, top : top + q, cols].reshape(rows, CHUNK), wbd[row * 3 + col, :, cols])

        straight = (
            tap(a00, 0, 1, 1)
            + tap(a01, 0, 1, 2)
            + tap(a10, 16, 2, 1)
            + tap(a11, 16, 2, 2)
            + tap(a10, 0, 0, 1)
            + tap(a11, 0, 0, 2)
        )
        moved = tap(a01, 0, 1, 0) + tap(a11, 16, 2, 0) + tap(a11, 0, 0, 0)
        part = straight + jnp.where(first_col, 0.0, pltpu.roll(moved, 1, 0))
        mid[:, cols] = part
        acc[0:8, cols] += fold(part)
        acc[8:16, cols] += fold(part * part)

    @pl.when(step == pl.num_programs(0) - 1)
    def _():
        sums_out(ex[0], acc[0:8, :], acc[8:16, :])
        wait_all()
        exchange(ex, totals, [gain, shift], [coef2])


def last_body(per, q, totals, mid, coef, w, gl, sl, gs, ss, side_coef, act, pre, coef3, rim, acc, *ex):
    step = pl.program_id(0)
    width = mid.shape[1]

    @pl.when(step == 0)
    def _():
        acc[...] = jnp.zeros_like(acc)
        signal_all()

    top = mid[...].reshape(per, q, width)[:, 0:16] * coef[0:1, :][None] + coef[1:2, :][None]
    rim[...] = top.astype(BF16)
    half = mid[...] * coef[4:5, :] + coef[5:6, :]
    act[...] = half_silu(half).astype(BF16)
    for c in range(0, w.shape[1], CHUNK):
        cols = slice(c, c + CHUNK)
        part = dot(act[...], w[:, cols])
        pre[:, cols] = part
        acc[0:8, cols] += fold(part)
        acc[8:16, cols] += fold(part * part)

    @pl.when(step == pl.num_programs(0) - 1)
    def _():
        sums_out(ex[0], acc[0:8, :], acc[8:16, :])
        wait_all()
        exchange(ex, totals, [gl, sl, gs, ss, side_coef], [coef3])


def rim_copy(rim, halo, per, step, send, recv):
    images = pl.ds(step * per, per)
    return remote(rim.at[images], halo.at[images], send.at[step], recv.at[step], upper_lower()[1])


def rim_finish(rim, halo, per, send, recv):
    copies = [rim_copy(rim, halo, per, s, send, recv) for s in range(rim.shape[0] // per)]
    to_neighbour(copies, True, "wait")


def out_parts(last, side, cot, coef, cols):
    half = last[:, cols] * coef[4:5, cols] + side[:, cols] * coef[5:6, cols] + coef[6:7, cols]
    th = jnp.tanh(half)
    moved = half * th
    up = cot[:, cols].astype(F32) * ((1.0 + th) * (1.0 + (half - moved)))
    return half + moved, up


def out_body(last, side, cot, coef, out, stat, acc):
    step = pl.program_id(0)

    @pl.when(step == 0)
    def _():
        acc[...] = jnp.zeros_like(acc)

    for c in range(0, last.shape[1], CHUNK):
        cols = slice(c, c + CHUNK)
        value, up = out_parts(last, side, cot, coef, cols)
        out[:, cols] = value.astype(BF16)
        acc[0:8, cols] += fold(up)
        acc[8:16, cols] += fold(up * last[:, cols])
        acc[16:24, cols] += fold(up * side[:, cols])

    @pl.when(step == pl.num_programs(0) - 1)
    def _():
        sums_out(stat, acc[0:8, :], acc[8:16, :], acc[16:24, :])


def last_grad_body(totals, last, side, cot, coef, act, stat, rim, lg, sg, g_last, grads, halo, *scr):
    acc, back, send, recv, *ex = scr
    step = pl.program_id(0)
    row = remote(rim, halo, send, recv, upper_lower()[1])

    @pl.when(step == 0)
    def _():
        signal_all()
        acc[...] = jnp.zeros_like(acc)
        ex[0][...] = stat[...]
        wait_all()
        exchange(ex, totals, [coef], [back, grads])
        to_neighbour([row], True, "start")

    for c in range(0, last.shape[1], CHUNK):
        cols = slice(c, c + CHUNK)
        _, part = out_parts(last, side, cot, coef, cols)
        down = part * back[0:1, cols] + last[:, cols] * back[1:2, cols] + back[2:3, cols]
        down = down.astype(BF16)
        lg[:, cols] = down
        acc[:, cols] += dot_tn(act[...], down)
        down = part * back[3:4, cols] + side[:, cols] * back[4:5, cols] + back[5:6, cols]
        sg[:, cols] = down.astype(BF16)

    @pl.when(step == pl.num_programs(0) - 1)
    def _():
        g_last[...] = acc[...].astype(BF16)
        to_neighbour([row], True, "wait")


def mid_back_body(
    per, q, totals, hook, lg, wl, mid, coef, sg, even, up, coef5, grads, halo, g_side, *scr
):
    acc, acc_s, rim, send, recv, *ex = scr
    step = pl.program_id(0)
    hook(-1)

    @pl.when(step == 0)
    def _():
        acc[...] = jnp.zeros_like(acc)
        acc_s[...] = jnp.zeros_like(acc_s)

    hook(0)
    for c in range(0, mid.shape[1], CHUNK):
        cols = slice(c, c + CHUNK)
        part = dot_nt(lg[...], wl[cols, :])
        normed = mid[:, cols] * coef[0:1, cols] + coef[1:2, cols]
        half = normed * coef[2:3, cols] + coef[3:4, cols]
        part = part * slope_twice(half, jnp.tanh(half))
        up[:, cols] = part
        rim[pl.ds(step * per, per), :, cols] = part.reshape(per, q, CHUNK)[:, 0:16].astype(BF16)
        acc[0:8, cols] += fold(part)
        acc[8:16, cols] += fold(part * normed)
    flat = even[...].reshape(per * q, even.shape[3])
    for c in range(0, sg.shape[1], CHUNK):
        cols = slice(c, c + CHUNK)
        acc_s[:, cols] += dot_tn(flat, sg[:, cols])
    to_neighbour([rim_copy(rim, halo, per, step, send, recv)], True, "start")

    @pl.when(step == pl.num_programs(0) - 1)
    def _():
        sums_out(ex[0], acc[0:8, :], acc[8:16, :])
        one = Exchange(ex)
        one.start()
        g_side[...] = acc_s[...].astype(BF16)
        one.turn()
        one.finish(totals, [coef], [coef5, grads])
        rim_finish(rim, halo, per, send, recv)


def conv_back_body(
    per, px, q, totals, hook, mup, mid, rim_up, rim_normed, pre, coef2, back, coef, w, *refs
):
    up, g_mid, coef6, grads, mg, mgs, acc, acc_g, wbd, *ex = refs
    hook(-1)
    step = pl.program_id(0)
    width = mid.shape[1]
    rows = per * q

    @pl.when(step == 0)
    def _():
        acc[...] = jnp.zeros_like(acc)
        acc_g[...] = jnp.zeros_like(acc_g)
        spread_weights(w, wbd)

    ext = q + 16
    below = lax.axis_index("height") < lax.axis_size("height") - 1
    last_col = lax.broadcasted_iota(jnp.int32, (rows, CHUNK), 0) % 16 == 15
    last_rim = lax.broadcasted_iota(jnp.int32, (per * 16, CHUNK), 0) % 16 == 15
    for c in range(0, width, CHUNK):
        cols = slice(c, c + CHUNK)
        hook(c // CHUNK)
        normed = mid[:, cols] * coef2[0:1, cols] + coef2[1:2, cols]
        grad = (mup[:, cols] * back[0:1, cols] + back[1:2, cols] + normed * back[2:3, cols]).astype(BF16)
        mg[:, 0:q, cols] = grad.reshape(per, q, CHUNK)
        grad = pltpu.roll(grad.astype(F32), rows - 1, 0)
        mgs[:, 0:q, cols] = jnp.where(last_col, 0.0, grad).astype(BF16).reshape(per, q, CHUNK)
        rim = rim_up[:, :, cols].astype(F32).reshape(per * 16, CHUNK) * back[0:1, cols] + back[1:2, cols]
        rim = rim + rim_normed[:, :, cols].astype(F32).reshape(per * 16, CHUNK) * back[2:3, cols]
        rim = jnp.where(below, rim, 0.0).astype(BF16)
        mg[:, q:ext, cols] = rim.reshape(per, 16, CHUNK)
        rim = pltpu.roll(rim.astype(F32), per * 16 - 1, 0)
        mgs[:, q:ext, cols] = jnp.where(last_rim, 0.0, rim).astype(BF16).reshape(per, 16, CHUNK)
        views = [ref[:, top : top + q, cols].reshape(rows, CHUNK) for top in (0, 16) for ref in (mg, mgs)]
        plans = (
            (0, ((1, 1, 0),)),
            (1, ((1, 2, 0), (1, 0, 1))),
            (2, ((2, 1, 0), (0, 1, 2))),
            (3, ((2, 2, 0), (2, 0, 1), (0, 2, 2), (0, 0, 3))),
        )
        for plane, taps in plans:
            total = None
            for row, col, view in taps:
                part = dot_nt(views[view], wbd[row * 3 + col, :, cols])
                total = part if total is None else total + part
            normed = pre[:, plane, :, cols].reshape(rows, CHUNK) * coef[0:1, cols] + coef[1:2, cols]
            half = normed * coef[2:3, cols] + coef[3:4, cols]
            th = jnp.tanh(half)
            act = (half + half * th).astype(BF16)
            total = total * slope_twice(half, th)
            up[:, plane, :, cols] = total.reshape(per, q, CHUNK).astype(BF16)
            acc[0:8, cols] += fold(total)
            acc[8:16, cols] += fold(total * normed)
            for row, col, view in taps:
                acc_g[row * 3 + col, :, cols] += dot_tn(act, views[view])

    @pl.when(step == pl.num_programs(0) - 1)
    def _():
        sums_out(ex[0], acc[0:8, :], acc[8:16, :])
        one = Exchange(ex)
        one.start()
        group = (lax.broadcasted_iota(jnp.int32, (32, width), 1) % CHUNK) // 32
        for tap in range(9):
            total = jnp.zeros((32, width), F32)
            for g in range(CHUNK // 32):
                total = total + jnp.where(group == g, acc_g[tap, g * 32 : (g + 1) * 32, :], 0.0)
            g_mid[tap] = total.astype(BF16)
        one.turn()
        one.finish(totals, [coef], [coef6, grads])


def first_grad(up, pre, coef, back, cols):
    normed = pre[:, cols] * coef[0:1, cols] + coef[1:2, cols]
    down = up[:, cols].astype(F32) * back[0:1, cols] + back[1:2, cols]
    return (down + normed * back[2:3, cols]).astype(BF16)


def first_back_body(hook, up, pre, coef, back, xp, g_first, acc):
    hook(-1)
    step = pl.program_id(0)

    @pl.when(step == 0)
    def _():
        acc[...] = jnp.zeros_like(acc)

    hook(0)
    for c in range(0, up.shape[1], CHUNK):
        cols = slice(c, c + CHUNK)
        acc[:, cols] += dot_tn(xp[...], first_grad(up, pre, coef, back, cols))

    @pl.when(step == pl.num_programs(0) - 1)
    def _():
        g_first[...] = acc[...].astype(BF16)


def image_back_body(per, px, q, hook, up, pre, coef, back, w1, sg, ws, out, fg, w1t, wst):
    hook(-1)
    step = pl.program_id(0)

    @pl.when(step == 0)
    def _():
        for c in range(0, w1.shape[0], CHUNK):
            cols = slice(c, c + CHUNK)
            w1t[:, cols] = w1[cols, :].T
            wst[:, cols] = ws[cols, :].T

    hook(0)
    for c in range(0, up.shape[1], CHUNK):
        cols = slice(c, c + CHUNK)
        fg[:, cols] = first_grad(up, pre, coef, back, cols)
    for c in range(0, w1.shape[0], CHUNK):
        cols = slice(c, c + CHUNK)
        side_back = dot(sg[...], wst[:, cols])
        part = dot(fg[...], w1t[:, cols])
        for k in range(per):
            even = part[k * px : k * px + q] + side_back[k * q : (k + 1) * q]
            out[k * px : k * px + q, cols] = even.astype(BF16)
            out[k * px + q : (k + 1) * px, cols] = part[k * px + q : (k + 1) * px].astype(BF16)


def place_body(px, planes, last, side, first, taps, wide_g, mid_g, first_g, *refs):
    out, last_out, side_out, first_out, taps_out = refs[:5]
    perm = refs[-1]

    @pl.when(pl.program_id(0) == 0)
    def _():
        perm[...] = planes_matrix(out.shape[1], out.shape[2], True)
        taps_out[...] = taps[...].astype(F32)
        rows = [first_g[1:2], first_g[0:1], mid_g[1:2], mid_g[0:1], wide_g[1:2], wide_g[0:1]]
        for ref, row in zip(refs[5:-1], rows + [wide_g[2:3], wide_g[0:1]]):
            ref[...] = row.reshape(ref.shape)

    for k in range(out.shape[0]):
        part = dot(perm[...], planes[k * px : (k + 1) * px, :]).astype(BF16)
        out[k] = part.reshape(out.shape[1:])
    last_out[...] = last[...].astype(F32)
    side_out[...] = side[...].astype(F32)
    first_out[...] = first[...].astype(F32)


def digit(axis, bit):
    return lax.rem(lax.div(lax.axis_index(axis), 1 << bit), 2)


def peer(axis, bit):
    batch, height = lax.axis_index("batch"), lax.axis_index("height")
    move = (1 - 2 * digit(axis, bit)) * (1 << bit)
    return (batch + move, height) if axis == "batch" else (batch, height + move)


def orders():
    bits_b = lax.axis_size("batch").bit_length() - 1
    bits_h = lax.axis_size("height").bit_length() - 1
    across = [("batch", k) for k in range(1, bits_b)]
    half = len(across) // 2
    x_bits, y_bits = across[:half], across[half:]
    z_bits = [("height", k) for k in range(bits_h)]
    return [x_bits + y_bits + z_bits, y_bits + x_bits + z_bits]


def stage_count():
    return len(orders()[0])


def lengths(rows):
    kept = [rows]
    for _ in range(stage_count()):
        kept.append(kept[-1] // 2 if kept[-1] % 32 == 0 else kept[-1])
    return kept


def landing(rows):
    return sum(lengths(rows)[1:])


def upper_lower():
    batch, height = lax.axis_index("batch"), lax.axis_index("height")
    size = lax.axis_size("height")
    return [(batch, lax.rem(height + 1, size)), (batch, lax.rem(height + size - 1, size))]


def partners():
    return [peer("batch", 0)] + [peer(axis, bit) for axis, bit in orders()[0]]


def remote(src, dst, send, recv, target):
    return pltpu.make_async_remote_copy(
        src_ref=src,
        dst_ref=dst,
        send_sem=send,
        recv_sem=recv,
        device_id=target,
        device_id_type=pl.DeviceIdType.MESH,
    )


class Flow:
    def __init__(self, rows, width, own, got, send, recv):
        self.own, self.got, self.send, self.recv = own, got, send, recv
        self.kept = lengths(rows)
        self.orders = orders()
        self.cols = [slice(0, width // 2), slice(width // 2, width)]
        self.low = []
        for order in self.orders:
            low = [0]
            for s, (axis, bit) in enumerate(order):
                move = digit(axis, bit) * self.kept[s + 1] if self.halved(s) else 0
                low.append(low[-1] + move)
            self.low.append(low)

    def halved(self, s):
        return self.kept[s + 1] < self.kept[s]

    def rows(self, first, count):
        return pl.ds(pl.multiple_of(first, 16), count)

    def keep(self, k, s):
        return self.rows(self.low[k][s], self.kept[s])

    def away(self, k, s):
        if not self.halved(s):
            return self.keep(k, s)
        axis, bit = self.orders[k][s]
        return self.rows(self.low[k][s] + (1 - digit(axis, bit)) * self.kept[s + 1], self.kept[s + 1])

    def place(self, s):
        return pl.ds(sum(self.kept[1 : s + 1]), self.kept[s + 1])

    def scatter(self, k, s):
        return remote(
            self.own.at[self.away(k, s), self.cols[k]],
            self.got.at[self.place(s), self.cols[k]],
            self.send.at[0, k, s],
            self.recv.at[0, k, s],
            peer(*self.orders[k][s]),
        )

    def scatter_start(self, s):
        for k in range(2):
            self.scatter(k, s).start()

    def scatter_finish(self, s):
        for k in range(2):
            self.scatter(k, s).wait()
            rows, cols = self.keep(k, s + 1), self.cols[k]
            total = self.own[rows, cols].astype(F32) + self.got[self.place(s), cols].astype(F32)
            self.own[rows, cols] = total.astype(BF16)

    def gather(self, k, s, rows):
        return remote(
            self.own.at[rows, self.cols[k]],
            self.own.at[rows, self.cols[k]],
            self.send.at[1, k, s],
            self.recv.at[1, k, s],
            peer(*self.orders[k][s]),
        )

    def gather_start(self, s):
        for k in range(2):
            if self.halved(s):
                self.gather(k, s, self.keep(k, s + 1)).start()

    def gather_finish(self, s):
        for k in range(2):
            if self.halved(s):
                self.gather(k, s, self.keep(k, s + 1)).wait_send()
                self.gather(k, s, self.away(k, s)).wait_recv()

    def moves(self, s, hbm, sems, out):
        copies = []
        for k in range(2):
            here = self.own.at[self.keep(k, s), self.cols[k]]
            there = hbm.at[self.keep(k, s), self.cols[k]]
            copies.append(pltpu.make_async_copy(*((here, there) if out else (there, here)), sems.at[k]))
        return copies


def run(copies, what):
    for copy in copies:
        getattr(copy, what)()


def own_half(ref):
    half = ref.shape[0] // 2
    return ref.at[pl.ds(pl.multiple_of(lax.axis_index("batch") % 2 * half, 16), half)]


def other_half(ref):
    half = ref.shape[0] // 2
    return ref.at[pl.ds(pl.multiple_of((1 - lax.axis_index("batch") % 2) * half, 16), half)]


def add_into(ref, other, step=64):
    for first in range(0, ref.shape[0], step):
        rows = slice(first, min(first + step, ref.shape[0]))
        ref[rows, :] = (ref[rows, :].astype(F32) + other[rows, :].astype(F32)).astype(BF16)


def carrying(body, counts, carry):
    def kernel(*refs):
        groups, first = [], 0
        for count in counts:
            groups.append(refs[first : first + count])
            first += count
        ins, c_ins, outs, c_outs, scr = groups
        c_scr = refs[first:]
        step = pl.program_id(0)
        points, last = carry(c_ins, c_outs, c_scr)

        def hook(point):
            for (when, where), action in points:
                if where == point:
                    pl.when(step == when)(action)

        body(hook, *ins, *outs, *scr)
        for action in last:
            pl.when(step == pl.num_programs(0) - 1)(action)

    return kernel


def carry_mid(c_ins, c_outs, c_scr):
    (g_last,) = c_ins
    (state_last,) = c_outs
    own, got, tmp, local, core, send, recv = c_scr
    flow = Flow(own.shape[0], own.shape[1], own, got, send, recv)
    load = pltpu.make_async_copy(own_half(g_last), own, local.at[0])
    copy = remote(other_half(g_last), tmp, core.at[0], core.at[1], peer("batch", 0))

    def start():
        load.start()
        signal_all()

    def enter():
        wait_all()
        copy.start()

    def first():
        load.wait()
        copy.wait()
        add_into(own, tmp)
        flow.scatter_start(0)

    def finish():
        flow.scatter_finish(0)
        dumps = flow.moves(1, state_last, local, True)
        run(dumps, "start")
        run(dumps, "wait")

    return [((0, -1), start), ((0, 0), enter), ((2, 0), first)], [finish]


def inner_stages(flow, done, first, until):
    stages = stage_count()

    def down(s):
        def action():
            flow.scatter_finish(s)
            if s + 1 < stages:
                flow.scatter_start(s + 1)
                return
            for k in range(2):
                rows = flow.keep(k, stages)
                done.own[rows, flow.cols[k]] = flow.own[rows, flow.cols[k]]
            done.gather_start(s)

        return action

    def back(s):
        def action():
            done.gather_finish(s)
            if s > until:
                done.gather_start(s - 1)

        return action

    return [down(s) for s in range(first, stages)] + [back(s) for s in range(stages - 1, until - 1, -1)]


def carry_conv(c_ins, c_outs, c_scr):
    state_last, g_side = c_ins
    part_last, state_side = c_outs
    own_l, got_l, full_l, own_s, got_s, tmp, local, core, send_l, recv_l, send_s, recv_s = c_scr
    rows, width = own_l.shape
    last = Flow(rows, width, own_l, got_l, send_l, recv_l)
    done = Flow(rows, width, full_l, None, send_l, recv_l)
    side = Flow(rows, width, own_s, got_s, send_s, recv_s)
    loads = last.moves(1, state_last, local, False)
    load = pltpu.make_async_copy(own_half(g_side), own_s, local.at[2])
    copy = remote(other_half(g_side), tmp, core.at[0], core.at[1], peer("batch", 0))
    inner = inner_stages(last, done, 1, 2)

    def start():
        run(loads, "start")
        load.start()
        signal_all()

    def enter():
        wait_all()
        run(loads, "wait")
        last.scatter_start(1)
        copy.start()

    def first_side():
        load.wait()
        copy.wait()
        add_into(own_s, tmp)
        side.scatter_start(0)

    def next_side(s):
        def action():
            side.scatter_finish(s)
            side.scatter_start(s + 1)

        return action

    def finish():
        side.scatter_finish(1)
        dumps = done.moves(2, part_last, local, True)
        dumps += side.moves(2, state_side, local.at[pl.ds(2, 2)], True)
        run(dumps, "start")
        run(dumps, "wait")

    points = [((0, -1), start), ((0, 0), enter), ((1, 0), first_side)]
    places = [(1, 2), (3, 0), (4, 1), (5, 2)]
    points += [(places[min(k, 3)], act) for k, act in enumerate(inner[:-1])]
    points += [((4, 0), next_side(0))]
    return points, [inner[-1], finish]


class Halves:
    def __init__(self, array, own, tmp, sems, core):
        mine, wide = lax.axis_index("batch") % 2, own.shape[1]
        self.own, self.tmp, self.rows = own, tmp, array.shape[0]
        self.cols = pl.ds(pl.multiple_of(mine * wide, LANES), wide)
        away = pl.ds(pl.multiple_of((1 - mine) * wide, LANES), wide)
        rows = slice(0, self.rows)
        self.load = pltpu.make_async_copy(array.at[:, self.cols], own.at[rows], sems.at[0])
        self.mate = remote(
            array.at[:, away], tmp.at[rows], core.at[0], core.at[1], peer("batch", 0)
        )

    def clear(self):
        left = (self.own.shape[0] - self.rows, self.own.shape[1])
        if left[0]:
            self.own[self.rows :, :] = jnp.zeros(left, BF16)
            self.tmp[self.rows :, :] = jnp.zeros(left, BF16)

    def add(self):
        self.load.wait()
        self.mate.wait()
        add_into(self.own, self.tmp)


def ends(src, dst, sem, core):
    return [
        pltpu.make_async_copy(src, dst, sem),
        remote(src, dst, core.at[0], core.at[1], peer("batch", 0)),
    ]


def carry_first(c_ins, c_outs, c_scr):
    part_last, state_side = c_ins
    half_last, part_side = c_outs
    own_l, own_s, got_s, full_s, local, send_l, recv_l, send_s, recv_s = c_scr
    rows, width = own_l.shape
    last = Flow(rows, width, own_l, None, send_l, recv_l)
    side = Flow(rows, width, own_s, got_s, send_s, recv_s)
    done_s = Flow(rows, width, full_s, None, send_s, recv_s)
    inner = inner_stages(side, done_s, 2, 3)
    loads = last.moves(2, part_last, local, False)
    loads += side.moves(2, state_side, local.at[pl.ds(2, 2)], False)

    def start():
        run(loads, "start")
        signal(partners())

    def enter():
        wait_partners()
        run(loads, "wait")
        last.gather_start(1)
        side.scatter_start(2)

    def next_last():
        last.gather_finish(1)
        last.gather_start(0)

    def finish():
        last.gather_finish(0)
        dumps = last.moves(0, half_last, local, True)
        dumps += done_s.moves(3, part_side, local.at[pl.ds(2, 2)], True)
        run(dumps, "start")
        run(dumps, "wait")

    points = [((0, -1), start), ((0, 0), enter), ((3, 0), next_last)]
    points += [((min(4 + 4 * k, 8), 0), act) for k, act in enumerate(inner[:-1])]
    return points, [inner[-1], finish]


def carry_image(c_ins, c_outs, c_scr):
    half_last, part_side, g_mid, g_first = c_ins
    all_last, all_side, all_first, all_mid = c_outs
    own_l, own_s, own_m, got_m, tmp_m, full_m, tmp_h, local, core = c_scr[:9]
    send_s, recv_s, send_m, recv_m = c_scr[9:13]
    side = Flow(own_s.shape[0], own_s.shape[1], own_s, None, send_s, recv_s)
    heads, dones = [], []
    for k in (13, 18):
        own_h, got_h, full_h, send_h, recv_h = c_scr[k : k + 5]
        heads.append(Flow(own_h.shape[0], own_h.shape[1], own_h, got_h, send_h, recv_h))
        dones.append(Flow(own_h.shape[0], own_h.shape[1], full_h, None, send_h, recv_h))
    heads.append(Flow(own_m.shape[0], own_m.shape[1], own_m, got_m, send_m, recv_m))
    dones.append(Flow(own_m.shape[0], own_m.shape[1], full_m, None, send_m, recv_m))
    halves = Halves(g_mid, own_m, tmp_m, local.at[pl.ds(5, 1)], core.at[pl.ds(6, 2)])
    few_h = c_scr[13].shape[0]
    parts_h = [slice(0, few_h), slice(few_h, 2 * few_h)]
    stages = stage_count()
    loads_h = [
        pltpu.make_async_copy(own_half(g_first).at[part], flow.own, local.at[7 + k])
        for k, (part, flow) in enumerate(zip(parts_h, heads))
    ]
    copy = remote(other_half(g_first), tmp_h, core.at[0], core.at[1], peer("batch", 0))
    loads = side.moves(3, part_side, local.at[pl.ds(3, 2)], False)
    few = slice(0, all_mid.shape[0])
    load_l = pltpu.make_async_copy(half_last, own_l, local.at[0])
    ends_last = ends(own_l, own_half(all_last), local.at[1], core.at[pl.ds(2, 2)])
    ends_side = ends(own_s, own_half(all_side), local.at[3], core.at[pl.ds(4, 2)])
    ends_head = []
    for k, (part, flow) in enumerate(zip(parts_h, dones)):
        pair = core.at[pl.ds(8 + 2 * k, 2)]
        ends_head.append(ends(flow.own, own_half(all_first).at[part], local.at[7 + k], pair))
    pair = core.at[pl.ds(12, 2)]
    ends_head.append(ends(full_m.at[few], all_mid.at[:, halves.cols], local.at[5], pair))

    def start():
        run(loads_h + loads + [load_l, halves.load], "start")
        halves.clear()
        signal(partners())

    def enter():
        wait_partners()
        copy.start()
        halves.mate.start()
        run(loads, "wait")
        side.gather_start(2)

    def first():
        run(loads_h, "wait")
        copy.wait()
        for part, flow in zip(parts_h, heads):
            add_into(flow.own, tmp_h.at[part])
            flow.scatter_start(0)
        halves.add()
        heads[2].scatter_start(0)
        load_l.wait()
        run(ends_last, "start")

    def back(flow, s, then):
        def action():
            flow.gather_finish(s)
            if s:
                flow.gather_start(s - 1)
            else:
                run(then, "start")

        return action

    def head_next(s):
        def action():
            for flow, done in zip(heads, dones):
                flow.scatter_finish(s)
                if s + 1 < stages:
                    flow.scatter_start(s + 1)
                    continue
                for k in range(2):
                    rows_k = flow.keep(k, stages)
                    done.own[rows_k, flow.cols[k]] = flow.own[rows_k, flow.cols[k]]
                done.gather_start(s)

        return action

    def head_back(s):
        def action():
            for done, end in zip(dones, ends_head):
                back(done, s, end)()

        return action

    def finish():
        for end in [ends_last, ends_side] + ends_head:
            run(end, "wait")

    points = [((0, -1), start), ((0, 0), enter), ((2, 0), first), ((4, 0), back(side, 2, None))]
    points += [((4, 0), head_next(0)), ((6, 0), head_next(1))]
    points += [((7, 0), back(side, 1, None))]
    places = [8, 10]
    points += [((places[min(s - 2, 1)], 0), head_next(s)) for s in range(2, stages)]
    tail = [head_back(s) for s in range(stages - 1, 1, -1)]
    tail += [back(side, 0, ends_side), head_back(1), head_back(0), finish]
    return points, tail


def per_device(
    images,
    w_first,
    gain_first,
    shift_first,
    w_mid,
    gain_mid,
    shift_mid,
    w_last,
    gain_last,
    shift_last,
    w_side,
    gain_side,
    shift_side,
    cotangent,
):
    n, rows_in, cols_in, cin = images.shape
    mid = w_first.shape[1]
    wide = w_last.shape[1]
    gw = w_mid.shape[2]
    rows_out, cols_out = rows_in // 2, cols_in // 2
    px, q = rows_in * cols_in, rows_out * cols_out
    devices = lax.axis_size("batch") * lax.axis_size("height")
    cells_in = float(n * px * devices)
    cells_out = float(n * q * devices)
    size_h = lax.axis_size("height")
    per = 4
    steps = n // per
    rows = per * q

    anywhere = pl.BlockSpec(memory_space=pl.ANY)
    dma = pltpu.SemaphoreType.DMA
    halo_x = lax.ppermute(images[:, rows_in - 1], "height", [(i, i + 1) for i in range(size_h - 1)])
    taps = w_mid.reshape(9, gw, mid)
    size_p = per * cols_in

    eights, wide_eights = whole((8, mid)), whole((8, wide))
    xp, pre, side_pre, coef1, side_coef = call(
        functools.partial(
            first_body, per, px, q, functools.partial(first_totals, cells_in, cells_out, mid, wide)
        ),
        "first_product",
        (steps,),
        [
            pl.BlockSpec((per, rows_in, cols_in, cin), lambda s: (s, 0, 0, 0)),
            whole((cin, mid)),
            whole((cin, wide)),
            whole((mid,)),
            whole((mid,)),
        ],
        [
            rows_spec(per * px, cin),
            rows_spec(per * px, mid),
            rows_spec(rows, wide),
            eights,
            wide_eights,
        ],
        [
            shape((n * px, cin), BF16),
            shape((n * px, mid)),
            shape((n * q, wide)),
            shape((8, mid)),
            shape((8, wide)),
        ],
        [pltpu.VMEM((16, mid), F32), pltpu.VMEM((16, wide), F32), pltpu.VMEM((px, px), BF16)]
        + exchange_scratch(2 * (mid + wide) // LANES),
        flops=2 * n * (px * cin * (mid + px) + q * cin * wide),
        moved=n * px * cin * 8 + n * q * wide * 4 + cin * (mid + wide) * 2,
        ident=6,
    )(images, w_first, w_side, gain_first, shift_first)

    pre_planes = pre.reshape(n, 4, q, mid)
    planes_spec = pl.BlockSpec((per, 4, q, mid), lambda s: (s, 0, 0, 0))
    mid_pre, coef2 = call(
        functools.partial(conv_body, per, px, q, functools.partial(mid_totals, cells_out, mid)),
        "grouped_conv",
        (steps,),
        [
            planes_spec,
            pl.BlockSpec((per, cols_in, cin), lambda s: (s, 0, 0)),
            whole((cin, mid)),
            eights,
            whole((9, gw, mid)),
            whole((mid,)),
            whole((mid,)),
        ],
        [rows_spec(rows, mid), eights],
        [shape((n * q, mid)), shape((8, mid))],
        [
            pltpu.VMEM((per, q, mid), BF16),
            pltpu.VMEM((per, q, mid), BF16),
            pltpu.VMEM((per, q + 16, mid), BF16),
            pltpu.VMEM((per, q + 16, mid), BF16),
            pltpu.VMEM((9, CHUNK, mid), BF16),
            pltpu.VMEM((size_p, size_p), BF16),
            pltpu.VMEM((16, mid), F32),
        ]
        + exchange_scratch(2 * mid // LANES),
        flops=2 * n * q * mid * CHUNK * 9 + 2 * n * cols_in * cin * mid,
        moved=n * px * mid * 4 + n * q * mid * 4,
        ident=0,
    )(pre_planes, halo_x, w_first, coef1, taps, gain_mid, shift_mid)

    rim_spec = pl.BlockSpec((per, cols_out, mid), lambda s: (s, 0, 0))
    rim_shape = shape((n, cols_out, mid), BF16)
    mid_act, last_pre, coef3, rim_own = call(
        functools.partial(last_body, per, q, functools.partial(last_totals, cells_out, wide)),
        "last_product",
        (steps,),
        [rows_spec(rows, mid), eights, whole((mid, wide))] + [whole((wide,))] * 4 + [wide_eights],
        [rows_spec(rows, mid), rows_spec(rows, wide), wide_eights, rim_spec],
        [shape((n * q, mid), BF16), shape((n * q, wide)), shape((8, wide)), rim_shape],
        [pltpu.VMEM((16, wide), F32)] + exchange_scratch(2 * wide // LANES),
        flops=2 * n * q * mid * wide,
        moved=n * q * (mid * 6 + wide * 4),
        ident=7,
    )(mid_pre, coef2, w_last, gain_last, shift_last, gain_side, shift_side, side_coef)

    cot = cotangent.reshape(n * q, wide)
    stat_rows = 3 * wide // LANES
    output, stat = call(
        out_body,
        "output",
        (steps,),
        [rows_spec(rows, wide), rows_spec(rows, wide), rows_spec(rows, wide), wide_eights],
        [rows_spec(rows, wide), whole((stat_rows, LANES))],
        [shape((n * q, wide), BF16), shape((stat_rows, LANES))],
        [pltpu.VMEM((24, wide), F32)],
        flops=30 * n * q * wide,
        moved=n * q * wide * 12,
    )(last_pre, side_pre, cot, coef3)

    xp_planes = xp.reshape(n, 4, q, cin)
    half_l = mid // 2
    stages = stage_count()
    sems = dma((2, 2, stages))
    state = shape((half_l, wide), BF16)
    buf = pltpu.VMEM((half_l, wide), BF16)
    got = pltpu.VMEM((landing(half_l), wide), BF16)
    last_grad, side_grad, g_last, wide_grads, rim_normed = call(
        functools.partial(last_grad_body, functools.partial(out_totals, cells_out, wide)),
        "last_gradients",
        (steps,),
        [
            rows_spec(rows, wide),
            rows_spec(rows, wide),
            rows_spec(rows, wide),
            wide_eights,
            rows_spec(rows, mid),
            whole((stat_rows, LANES)),
            anywhere,
        ],
        [rows_spec(rows, wide), rows_spec(rows, wide), whole((mid, wide)), wide_eights, anywhere],
        [
            shape((n * q, wide), BF16),
            shape((n * q, wide), BF16),
            shape((mid, wide), BF16),
            shape((8, wide)),
            rim_shape,
        ],
        [pltpu.VMEM((mid, wide), F32), pltpu.VMEM((8, wide), F32), dma, dma]
        + exchange_scratch(stat_rows),
        flops=2 * n * q * mid * wide,
        moved=n * q * (wide * 14 + mid * 2) + mid * wide * 2,
        ident=3,
    )(last_pre, side_pre, cot, coef3, mid_act, stat, rim_own)
    rims = [pltpu.VMEM((n, cols_out, mid), BF16), dma((steps,)), dma((steps,))]
    inner_scratch = exchange_scratch(2 * mid // LANES)
    mid_up, coef5, mid_grads, rim_up, g_side, state_last = call(
        carrying(
            functools.partial(mid_back_body, per, q, functools.partial(inner_totals, cells_out, mid)),
            (6, 1, 5, 1, 5 + len(inner_scratch)),
            carry_mid,
        ),
        "mid_back",
        (steps,),
        [
            rows_spec(rows, wide),
            whole((mid, wide)),
            rows_spec(rows, mid),
            eights,
            rows_spec(rows, wide),
            pl.BlockSpec((per, 1, q, cin), lambda s: (s, 0, 0, 0)),
            anywhere,
        ],
        [rows_spec(rows, mid), eights, eights, anywhere, whole((cin, wide)), anywhere],
        [
            shape((n * q, mid)),
            shape((8, mid)),
            shape((8, mid)),
            rim_shape,
            shape((cin, wide), BF16),
            state,
        ],
        [pltpu.VMEM((16, mid), F32), pltpu.VMEM((cin, wide), F32)]
        + rims
        + inner_scratch
        + [buf, got, buf, dma((2,)), dma((2,)), sems, sems],
        flops=2 * n * q * (mid + cin) * wide,
        moved=n * q * (wide * 4 + mid * 10) + mid * wide * 4,
        ident=9,
    )(last_grad, w_last, mid_pre, coef2, side_grad, xp_planes, g_last)

    first_up, g_mid, coef6, first_grads, part_last, state_side = call(
        carrying(
            functools.partial(
                conv_back_body, per, px, q, functools.partial(inner_totals, cells_in, mid)
            ),
            (9, 2, 4, 2, 5 + len(inner_scratch)),
            carry_conv,
        ),
        "grouped_conv_back",
        (steps,),
        [
            rows_spec(rows, mid),
            rows_spec(rows, mid),
            rim_spec,
            rim_spec,
            planes_spec,
            eights,
            eights,
            eights,
            whole((9, gw, mid)),
            anywhere,
            anywhere,
        ],
        [planes_spec, whole((9, gw, mid)), eights, eights, anywhere, anywhere],
        [
            shape((n, 4, q, mid), BF16),
            shape((9, gw, mid), BF16),
            shape((8, mid)),
            shape((8, mid)),
            state,
            state,
        ],
        [
            pltpu.VMEM((per, q + 16, mid), BF16),
            pltpu.VMEM((per, q + 16, mid), BF16),
            pltpu.VMEM((16, mid), F32),
            pltpu.VMEM((9, CHUNK, mid), F32),
            pltpu.VMEM((9, CHUNK, mid), BF16),
        ]
        + inner_scratch
        + [buf, got, buf, buf, got, buf, dma((4,)), dma((2,))]
        + [sems] * 4,
        flops=4 * n * q * mid * CHUNK * 9,
        moved=n * q * mid * 8 + n * px * mid * 6,
        vmem=60,
        ident=10,
    )(
        mid_up,
        mid_pre,
        rim_up,
        rim_normed,
        pre_planes,
        coef2,
        coef5,
        coef1,
        taps,
        state_last,
        g_side,
    )

    flat_up = first_up.reshape(n * px, mid)
    few = per // 2
    g_first, half_last, part_side = call(
        carrying(first_back_body, (5, 2, 1, 2, 1), carry_first),
        "first_gradient",
        (n // few,),
        [
            rows_spec(few * px, mid),
            rows_spec(few * px, mid),
            eights,
            eights,
            rows_spec(few * px, cin),
            anywhere,
            anywhere,
        ],
        [whole((cin, mid)), anywhere, anywhere],
        [shape((cin, mid), BF16), state, state],
        [pltpu.VMEM((cin, mid), F32), buf, buf, got, buf, dma((4,))] + [sems] * 4,
        flops=2 * n * px * mid * cin,
        moved=n * px * (mid * 6 + cin * 2),
        ident=11,
    )(flat_up, pre, coef1, coef6, xp, part_last, state_side)

    half_m = mid // 2
    unit = 16 * (devices // 2)
    taps_rows = -(-9 * gw // unit) * unit
    buf_m = pltpu.VMEM((taps_rows, half_m), BF16)
    got_m = pltpu.VMEM((landing(taps_rows), half_m), BF16)
    quarter = cin // 4
    buf_h = pltpu.VMEM((quarter, mid), BF16)
    got_h = pltpu.VMEM((landing(quarter), mid), BF16)
    planes, all_last, all_side, all_first, all_mid = call(
        carrying(functools.partial(image_back_body, few, px, q), (7, 4, 1, 4, 3), carry_image),
        "image_gradient",
        (n // few,),
        [
            rows_spec(few * px, mid),
            rows_spec(few * px, mid),
            eights,
            eights,
            whole((cin, mid)),
            rows_spec(few * q, wide),
            whole((cin, wide)),
        ]
        + [anywhere] * 4,
        [rows_spec(few * px, cin)] + [anywhere] * 4,
        [
            shape((n * px, cin), BF16),
            shape((mid, wide), BF16),
            shape((cin, wide), BF16),
            shape((cin, mid), BF16),
            shape((9 * gw, mid), BF16),
        ],
        [
            pltpu.VMEM((few * px, mid), BF16),
            pltpu.VMEM((mid, cin), BF16),
            pltpu.VMEM((wide, cin), BF16),
        ]
        + [buf, buf, buf_m, got_m, buf_m, buf_m, pltpu.VMEM((2 * quarter, mid), BF16)]
        + [dma((9,)), dma((14,))]
        + [sems] * 4
        + [buf_h, got_h, buf_h, sems, sems] * 2,
        flops=2 * n * px * cin * mid + 2 * n * q * cin * wide,
        moved=n * px * (mid * 6 + cin * 2) + n * q * wide * 2,
        ident=12,
    )(
        flat_up,
        pre,
        coef1,
        coef6,
        w_first,
        side_grad,
        w_side,
        half_last,
        part_side,
        g_mid.reshape(9 * gw, mid),
        g_first,
    )
    three = 3
    cuts = n // three
    vectors = [mid] * 4 + [wide] * 4
    grad_images, grad_last, grad_side, grad_first, grad_mid, *grad_vectors = call(
        functools.partial(place_body, px),
        "image_places",
        (cuts,),
        [
            rows_spec(three * px, cin),
            rows_spec(mid // cuts, wide),
            rows_spec(cin // cuts, wide),
            rows_spec(cin // cuts, mid),
            whole((9 * gw, mid)),
            wide_eights,
            eights,
            eights,
        ],
        [
            pl.BlockSpec((three, rows_in, cols_in, cin), lambda s: (s, 0, 0, 0)),
            rows_spec(mid // cuts, wide),
            rows_spec(cin // cuts, wide),
            rows_spec(cin // cuts, mid),
            whole((9 * gw, mid)),
        ]
        + [whole((k,)) for k in vectors],
        [
            shape((n, rows_in, cols_in, cin), BF16),
            shape((mid, wide)),
            shape((cin, wide)),
            shape((cin, mid)),
            shape((9 * gw, mid)),
        ]
        + [shape((k,)) for k in vectors],
        [pltpu.VMEM((px, px), BF16)],
        flops=2 * n * px * cin * px,
        moved=n * px * cin * 4 + (mid + cin) * wide * 6 + cin * mid * 6,
    )(planes, all_last, all_side, all_first, all_mid, wide_grads, mid_grads, first_grads)

    return (
        output.reshape(n, rows_out, cols_out, wide),
        grad_images,
        grad_first,
        grad_vectors[0],
        grad_vectors[1],
        grad_mid.reshape(3, 3, gw, mid),
        grad_vectors[2],
        grad_vectors[3],
        grad_last,
        grad_vectors[4],
        grad_vectors[5],
        grad_side,
        grad_vectors[6],
        grad_vectors[7],
    )


def solution(mesh):
    split = P("batch", "height", None, None)
    in_specs = (split,) + (P(),) * 12 + (split,)
    out_specs = (split, split) + (P(),) * 12
    return jax.shard_map(
        per_device, mesh=mesh, in_specs=in_specs, out_specs=out_specs, check_vma=False
    )
```

```python
import functools

import jax
import jax.numpy as jnp
from jax import lax
from jax.experimental import pallas as pl
from jax.experimental.pallas import tpu as pltpu
from jax.sharding import PartitionSpec as P

EPSILON = 1e-05
LANES = 128
CHUNK = 256
BF16 = jnp.bfloat16
F32 = jnp.float32
MIB = 1 << 20


def dot(a, b):
    return jnp.dot(a, b, preferred_element_type=F32)


def dot_nt(a, b):
    return lax.dot_general(a, b, (((1,), (1,)), ((), ())), preferred_element_type=F32)


def dot_tn(a, b):
    return lax.dot_general(a, b, (((0,), (0,)), ((), ())), preferred_element_type=F32)


def fold(values):
    rows, cols = values.shape
    return jnp.sum(values.reshape(rows // 8, 8, cols), axis=0)


def put_row(ref, first, row):
    for k in range(row.shape[1] // LANES):
        ref[first + k : first + k + 1, :] = row[:, k * LANES : (k + 1) * LANES]


def get_row(values, first, width):
    count = width // LANES
    return jnp.concatenate([values[first + k : first + k + 1, :] for k in range(count)], axis=1)


def sums_out(ref, *partials):
    first = 0
    for part in partials:
        row = jnp.sum(part, axis=0, keepdims=True)
        put_row(ref, first, row)
        first += row.shape[1] // LANES


def whole(shape):
    return pl.BlockSpec(shape, lambda *_: (0,) * len(shape), pipeline_mode=pl.Buffered(1))


def rows_spec(rows, cols):
    return pl.BlockSpec((rows, cols), lambda i: (i, 0))


def call(
    body, name, grid, in_specs, out_specs, out_shape, scratch=(), flops=0, moved=0, vmem=56, ident=None
):
    return pl.pallas_call(
        body,
        name=name,
        grid=grid,
        in_specs=in_specs,
        out_specs=out_specs,
        out_shape=out_shape,
        scratch_shapes=list(scratch),
        compiler_params=pltpu.CompilerParams(
            vmem_limit_bytes=vmem * MIB, collective_id=ident, has_side_effects=ident is not None
        ),
        cost_estimate=pl.CostEstimate(flops=flops, bytes_accessed=moved, transcendentals=0),
    )


def shape(dims, kind=F32):
    return jax.ShapeDtypeStruct(dims, kind)


def everyone():
    batch, height = lax.axis_index("batch"), lax.axis_index("height")
    size_b, size_h = lax.axis_size("batch"), lax.axis_size("height")
    row = [(lax.rem(batch + k, size_b), height) for k in range(1, size_b)]
    return row, [(batch, lax.rem(height + k, size_h)) for k in range(1, size_h)]


def signal(peers):
    barrier = pltpu.get_barrier_semaphore()
    for one in peers:
        pl.semaphore_signal(barrier, inc=1, device_id=one, device_id_type=pl.DeviceIdType.MESH)


def signal_all():
    row, column = everyone()
    signal(row + column)


def wait_all():
    row, column = everyone()
    pl.semaphore_wait(pltpu.get_barrier_semaphore(), len(row + column))


def wait_partners():
    pl.semaphore_wait(pltpu.get_barrier_semaphore(), len(partners()))


def greet(peers):
    signal(peers)
    pl.semaphore_wait(pltpu.get_barrier_semaphore(), len(peers))


def exchange_scratch(rows):
    size_b, size_h = lax.axis_size("batch"), lax.axis_size("height")
    dma = pltpu.SemaphoreType.DMA
    return [
        pltpu.VMEM((rows, LANES), F32),
        pltpu.VMEM((size_b, rows, LANES), F32),
        pltpu.VMEM((size_h, rows, LANES), F32),
        dma((size_b - 1,)),
        dma((size_b,)),
        dma((size_h - 1,)),
        dma((size_h,)),
    ]


class Exchange:
    def __init__(self, scratch):
        self.stat, self.got_b, self.got_h, self.send_b, self.recv_b, self.send_h, self.recv_h = scratch
        self.me_b, self.me_h = lax.axis_index("batch"), lax.axis_index("height")
        self.row, self.column = everyone()

    def spread(self, src, got, me, targets, send, recv):
        return [
            remote(src, got.at[me], send.at[k], recv.at[me], target) for k, target in enumerate(targets)
        ]

    def total(self, src, got, me, targets, send, recv):
        size = got.shape[0]
        for k, target in enumerate(targets):
            other = lax.rem(me + (size - 1 - k), size)
            remote(src, got.at[other], send.at[k], recv.at[other], target).wait_recv()
        total = got[0]
        for k in range(1, size):
            total = total + got[k]
        return total

    def over_batch(self):
        return self.stat, self.got_b, self.me_b, self.row, self.send_b, self.recv_b

    def over_height(self):
        return self.got_h.at[self.me_h], self.got_h, self.me_h, self.column, self.send_h, self.recv_h

    def start(self):
        run(self.spread(*self.over_batch()), "start")
        self.got_b[self.me_b] = self.stat[...]

    def turn(self):
        self.got_h[self.me_h] = self.total(*self.over_batch())
        run(self.spread(*self.over_height()), "start")

    def finish(self, epilogue, params, outs):
        epilogue(self.total(*self.over_height()), params, outs)
        run(self.spread(*self.over_batch()) + self.spread(*self.over_height()), "wait_send")


def exchange(scratch, epilogue, params, outs):
    one = Exchange(scratch)
    one.start()
    one.turn()
    one.finish(epilogue, params, outs)


def norm_terms(total, first, width, cells):
    average = get_row(total, first, width) * (1.0 / cells)
    meansq = get_row(total, first + width // LANES, width) * (1.0 / cells)
    inverse = lax.rsqrt(meansq - average * average + EPSILON)
    return inverse, -average * inverse


def fill(ref, rows):
    for k, row in enumerate(rows):
        ref[k : k + 1, :] = row
    ref[len(rows) :, :] = jnp.zeros((8 - len(rows), ref.shape[1]), F32)


def act_rows(inverse, offset, gain, shift):
    return [
        inverse,
        offset,
        0.5 * gain,
        0.5 * shift,
        0.5 * gain * inverse,
        0.5 * (shift + gain * offset),
    ]


def first_totals(cells_in, width, total, params, outs):
    gain, shift = as_row(params[0]), as_row(params[1])
    fill(outs[0], act_rows(*norm_terms(total, 0, width, cells_in), gain, shift))


def mid_totals(cells_out, width, wide, total, params, outs):
    gain, shift = as_row(params[0]), as_row(params[1])
    fill(outs[0], act_rows(*norm_terms(total, 0, width, cells_out), gain, shift))
    fill(outs[1], list(norm_terms(total, 2 * width // LANES, wide, cells_out)))


def last_totals(cells_out, wide, total, params, outs):
    gain_last, shift_last, gain_side, shift_side, side = params
    inverse, offset = norm_terms(total, 0, wide, cells_out)
    inverse_s, offset_s = side[0:1, :], side[1:2, :]
    gain_l, gain_s = 0.5 * as_row(gain_last), 0.5 * as_row(gain_side)
    shift = 0.5 * (as_row(shift_last) + as_row(shift_side))
    scales = [gain_l * inverse, gain_s * inverse_s, gain_l * offset + gain_s * offset_s + shift]
    fill(outs[0], [inverse, offset, inverse_s, offset_s] + scales)


def back_rows(scale, total_up, cross, cells):
    return [0.5 * scale, -scale * total_up * (1.0 / cells), -scale * cross * (1.0 / cells)]


def folded(rows, inverse, offset):
    scale, base, cross = rows
    return [scale, cross * inverse, base + cross * offset]


def out_totals(cells_out, wide, total, params, outs):
    coef = params[0]
    step = wide // LANES
    total_up, last_raw, side_raw = [0.5 * get_row(total, k * step, wide) for k in range(3)]
    inverse_l, offset_l, inverse_s, offset_s = [coef[k : k + 1, :] for k in range(4)]
    last_cross = inverse_l * last_raw + offset_l * total_up
    side_cross = inverse_s * side_raw + offset_s * total_up
    rows_l = back_rows(2.0 * coef[4:5, :], total_up, last_cross, cells_out)
    rows_s = back_rows(2.0 * coef[5:6, :], total_up, side_cross, cells_out)
    fill(outs[0], folded(rows_l, inverse_l, offset_l) + folded(rows_s, inverse_s, offset_s))
    fill(outs[1], [total_up, last_cross, side_cross])


def inner_totals(cells, width, total, params, outs):
    coef = params[0]
    total_up = 0.5 * get_row(total, 0, width)
    cross = 0.5 * get_row(total, width // LANES, width)
    fill(outs[0], back_rows(2.0 * coef[4:5, :], total_up, cross, cells))
    fill(outs[1], [total_up, cross])


def half_silu(half):
    return half + half * jnp.tanh(half)


def slope_twice(half, th):
    return (1.0 + th) * (1.0 + half * (1.0 - th))


def to_neighbour(copies, moves_up, what):
    height, size = lax.axis_index("height"), lax.axis_size("height")
    sends = height > 0 if moves_up else height < size - 1
    gets = height < size - 1 if moves_up else height > 0
    if what == "start":
        pl.when(sends)(lambda: run(copies, "start"))
    else:
        pl.when(sends)(lambda: run(copies, "wait_send"))
        pl.when(gets)(lambda: run(copies, "wait_recv"))


def planes_matrix(rows, cols, inverse):
    px, q, half = rows * cols, rows * cols // 4, cols // 2
    place = lax.broadcasted_iota(jnp.int32, (px, px), 1 if inverse else 0)
    pixel = lax.broadcasted_iota(jnp.int32, (px, px), 0 if inverse else 1)
    plane, inner = place // q, place % q
    source = (2 * (inner // half) + plane // 2) * cols + 2 * (inner % half) + plane % 2
    return (source == pixel).astype(F32).astype(BF16)


def row_matrix(count, cols):
    size, half = count * cols, cols // 2
    place = lax.broadcasted_iota(jnp.int32, (size, size), 0)
    pixel = lax.broadcasted_iota(jnp.int32, (size, size), 1)
    source = place // cols * cols + 2 * (place % half) + place % cols // half
    return (source == pixel).astype(F32).astype(BF16)


def spread_weights(w, out):
    gw, width = w.shape[1], w.shape[2]
    group = (lax.broadcasted_iota(jnp.int32, (gw, width), 1) % CHUNK) // gw
    for tap in range(9):
        rows = w[tap].astype(F32)
        for g in range(CHUNK // gw):
            out[tap, g * gw : (g + 1) * gw, :] = jnp.where(group == g, rows, 0.0).astype(BF16)


def as_row(ref):
    return ref[...].reshape(1, ref.shape[0])


def first_body(
    per, px, q, totals, img, w1, ws, gain, shift, xp, pre, side, coef, side_stat, acc, acc_s, perm, evens, *ex
):
    step, steps = pl.program_id(0), pl.num_programs(0) // 2
    mid, wide = w1.shape[1], ws.shape[1]
    rows = per * q

    @pl.when(step == 0)
    def _():
        acc[...] = jnp.zeros_like(acc)
        acc_s[...] = jnp.zeros_like(acc_s)
        perm[...] = planes_matrix(img.shape[1], img.shape[2], False)
        signal_all()

    @pl.when(step < steps)
    def _():
        for k in range(per):
            flat = img[k].reshape(px, img.shape[3])
            xp[k * px : (k + 1) * px, :] = dot(perm[...], flat).astype(BF16)
        even = jnp.concatenate([xp[k * px : k * px + q, :] for k in range(per)], axis=0)
        evens[pl.ds(pl.multiple_of(step * rows, 16), rows), :] = even
        for c in range(0, mid, CHUNK):
            cols = slice(c, c + CHUNK)
            part = dot(xp[...], w1[:, cols])
            pre[:, cols] = part
            acc[0:8, cols] += fold(part)
            acc[8:16, cols] += fold(part * part)

    @pl.when(step == steps)
    def _():
        sums_out(ex[0], acc[0:8, :], acc[8:16, :])
        wait_all()
        Exchange(ex).start()

    @pl.when(step == steps + 2)
    def _():
        Exchange(ex).turn()

    @pl.when(step >= steps)
    def _():
        even = evens[pl.ds(pl.multiple_of((step - steps) * rows, 16), rows), :]
        for c in range(0, wide, CHUNK):
            cols = slice(c, c + CHUNK)
            part = dot(even, ws[:, cols])
            side[:, cols] = part
            acc_s[0:8, cols] += fold(part)
            acc_s[8:16, cols] += fold(part * part)

    @pl.when(step == pl.num_programs(0) - 1)
    def _():
        sums_out(side_stat, acc_s[0:8, :], acc_s[8:16, :])
        Exchange(ex).finish(totals, [gain, shift], [coef])


def conv_body(
    per, px, q, totals, pre, halo, w1, coef, w, gain, shift, side_stat, mid, coef2, side_coef, *scr
):
    a00, a01, a10, a11, wbd, perm, acc, *ex = scr
    step = pl.program_id(0)
    width = w1.shape[1]

    @pl.when(step == 0)
    def _():
        acc[...] = jnp.zeros_like(acc)
        spread_weights(w, wbd)
        perm[...] = row_matrix(per, halo.shape[1])
        signal_all()

    scale, offset = coef[4:5, :], coef[5:6, :]
    flat = halo[...].reshape(per * 32, halo.shape[2])
    rim = half_silu(dot(dot(perm[...], flat).astype(BF16), w1[...]) * scale + offset)
    rim = jnp.where(lax.axis_index("height") > 0, rim, 0.0).astype(BF16)
    rim = rim.reshape(per, 2, 16, width)
    a10[:, 0:16, :] = rim[:, 0]
    a11[:, 0:16, :] = rim[:, 1]
    for plane, ref, top in ((0, a00, 0), (1, a01, 0), (2, a10, 16), (3, a11, 16)):
        half = pre[:, plane] * scale[None] + offset[None]
        ref[:, top : top + q, :] = half_silu(half).astype(BF16)
    rows = per * q
    first_col = lax.broadcasted_iota(jnp.int32, (rows, CHUNK), 0) % 16 == 0
    for c in range(0, width, CHUNK):
        cols = slice(c, c + CHUNK)

        def tap(ref, top, row, col):
            return dot(ref[:, top : top + q, cols].reshape(rows, CHUNK), wbd[row * 3 + col, :, cols])

        straight = (
            tap(a00, 0, 1, 1)
            + tap(a01, 0, 1, 2)
            + tap(a10, 16, 2, 1)
            + tap(a11, 16, 2, 2)
            + tap(a10, 0, 0, 1)
            + tap(a11, 0, 0, 2)
        )
        moved = tap(a01, 0, 1, 0) + tap(a11, 16, 2, 0) + tap(a11, 0, 0, 0)
        part = straight + jnp.where(first_col, 0.0, pltpu.roll(moved, 1, 0))
        mid[:, cols] = part
        acc[0:8, cols] += fold(part)
        acc[8:16, cols] += fold(part * part)

    @pl.when(step == pl.num_programs(0) - 1)
    def _():
        sums_out(ex[0], acc[0:8, :], acc[8:16, :])
        ex[0][2 * width // LANES :, :] = side_stat[...]
        wait_all()
        exchange(ex, totals, [gain, shift], [coef2, side_coef])


def last_body(per, q, totals, mid, coef, w, gl, sl, gs, ss, side_coef, act, pre, coef3, rim, acc, *ex):
    step = pl.program_id(0)
    width = mid.shape[1]

    @pl.when(step == 0)
    def _():
        acc[...] = jnp.zeros_like(acc)
        signal_all()

    top = mid[...].reshape(per, q, width)[:, 0:16] * coef[0:1, :][None] + coef[1:2, :][None]
    rim[...] = top.astype(BF16)
    half = mid[...] * coef[4:5, :] + coef[5:6, :]
    act[...] = half_silu(half).astype(BF16)
    for c in range(0, w.shape[1], CHUNK):
        cols = slice(c, c + CHUNK)
        part = dot(act[...], w[:, cols])
        pre[:, cols] = part
        acc[0:8, cols] += fold(part)
        acc[8:16, cols] += fold(part * part)

    @pl.when(step == pl.num_programs(0) - 1)
    def _():
        sums_out(ex[0], acc[0:8, :], acc[8:16, :])
        wait_all()
        exchange(ex, totals, [gl, sl, gs, ss, side_coef], [coef3])


def rim_copy(rim, halo, per, step, send, recv):
    images = pl.ds(step * per, per)
    return remote(rim.at[images], halo.at[images], send.at[step], recv.at[step], upper_lower()[1])


def rim_finish(rim, halo, per, send, recv):
    copies = [rim_copy(rim, halo, per, s, send, recv) for s in range(rim.shape[0] // per)]
    to_neighbour(copies, True, "wait")


def out_parts(last, side, cot, coef, cols):
    half = last[:, cols] * coef[4:5, cols] + side[:, cols] * coef[5:6, cols] + coef[6:7, cols]
    th = jnp.tanh(half)
    moved = half * th
    up = cot[:, cols].astype(F32) * ((1.0 + th) * (1.0 + (half - moved)))
    return half + moved, up


def out_body(last, side, cot, coef, out, stat, acc):
    step = pl.program_id(0)

    @pl.when(step == 0)
    def _():
        acc[...] = jnp.zeros_like(acc)

    for c in range(0, last.shape[1], CHUNK):
        cols = slice(c, c + CHUNK)
        value, up = out_parts(last, side, cot, coef, cols)
        out[:, cols] = value.astype(BF16)
        acc[0:8, cols] += fold(up)
        acc[8:16, cols] += fold(up * last[:, cols])
        acc[16:24, cols] += fold(up * side[:, cols])

    @pl.when(step == pl.num_programs(0) - 1)
    def _():
        sums_out(stat, acc[0:8, :], acc[8:16, :], acc[16:24, :])


def last_grad_body(totals, last, side, cot, coef, act, stat, rim, lg, sg, g_last, grads, halo, *scr):
    acc, back, send, recv, *ex = scr
    step = pl.program_id(0)
    row = remote(rim, halo, send, recv, upper_lower()[1])

    @pl.when(step == 0)
    def _():
        signal_all()
        acc[...] = jnp.zeros_like(acc)
        ex[0][...] = stat[...]
        wait_all()
        exchange(ex, totals, [coef], [back, grads])
        to_neighbour([row], True, "start")

    for c in range(0, last.shape[1], CHUNK):
        cols = slice(c, c + CHUNK)
        _, part = out_parts(last, side, cot, coef, cols)
        down = part * back[0:1, cols] + last[:, cols] * back[1:2, cols] + back[2:3, cols]
        down = down.astype(BF16)
        lg[:, cols] = down
        acc[:, cols] += dot_tn(act[...], down)
        down = part * back[3:4, cols] + side[:, cols] * back[4:5, cols] + back[5:6, cols]
        sg[:, cols] = down.astype(BF16)

    @pl.when(step == pl.num_programs(0) - 1)
    def _():
        g_last[...] = acc[...].astype(BF16)
        to_neighbour([row], True, "wait")


def mid_back_body(
    per, q, totals, hook, lg, wl, mid, coef, sg, even, up, coef5, grads, halo, g_side, *scr
):
    acc, acc_s, rim, send, recv, *ex = scr
    step, steps = pl.program_id(0), pl.num_programs(0) // 2
    hook(-1)

    @pl.when(step == 0)
    def _():
        acc[...] = jnp.zeros_like(acc)
        acc_s[...] = jnp.zeros_like(acc_s)

    hook(0)

    @pl.when(step < steps)
    def _():
        for c in range(0, mid.shape[1], CHUNK):
            cols = slice(c, c + CHUNK)
            part = dot_nt(lg[...], wl[cols, :])
            normed = mid[:, cols] * coef[0:1, cols] + coef[1:2, cols]
            half = normed * coef[2:3, cols] + coef[3:4, cols]
            part = part * slope_twice(half, jnp.tanh(half))
            up[:, cols] = part
            rim[pl.ds(step * per, per), :, cols] = part.reshape(per, q, CHUNK)[:, 0:16].astype(BF16)
            acc[0:8, cols] += fold(part)
            acc[8:16, cols] += fold(part * normed)
        to_neighbour([rim_copy(rim, halo, per, step, send, recv)], True, "start")

    @pl.when(step == steps)
    def _():
        sums_out(ex[0], acc[0:8, :], acc[8:16, :])
        Exchange(ex).start()

    @pl.when(step >= steps)
    def _():
        flat = even[...].reshape(per * q, even.shape[3])
        for c in range(0, sg.shape[1], CHUNK):
            cols = slice(c, c + CHUNK)
            acc_s[:, cols] += dot_tn(flat, sg[:, cols])

    @pl.when(step == pl.num_programs(0) - 1)
    def _():
        one = Exchange(ex)
        one.turn()
        g_side[...] = acc_s[...].astype(BF16)
        one.finish(totals, [coef], [coef5, grads])
        rim_finish(rim, halo, per, send, recv)


def conv_back_body(
    per, px, q, totals, hook, mup, mid, rim_up, rim_normed, pre, coef2, back, coef, w, *refs
):
    up, g_mid, coef6, grads, mg, mgs, acc, acc_g, wbd, *ex = refs
    hook(-1)
    step = pl.program_id(0)
    width = mid.shape[1]
    rows = per * q

    @pl.when(step == 0)
    def _():
        acc[...] = jnp.zeros_like(acc)
        acc_g[...] = jnp.zeros_like(acc_g)
        spread_weights(w, wbd)

    ext = q + 16
    below = lax.axis_index("height") < lax.axis_size("height") - 1
    last_col = lax.broadcasted_iota(jnp.int32, (rows, CHUNK), 0) % 16 == 15
    last_rim = lax.broadcasted_iota(jnp.int32, (per * 16, CHUNK), 0) % 16 == 15
    for c in range(0, width, CHUNK):
        cols = slice(c, c + CHUNK)
        hook(c // CHUNK)
        normed = mid[:, cols] * coef2[0:1, cols] + coef2[1:2, cols]
        grad = (mup[:, cols] * back[0:1, cols] + back[1:2, cols] + normed * back[2:3, cols]).astype(BF16)
        mg[:, 0:q, cols] = grad.reshape(per, q, CHUNK)
        grad = pltpu.roll(grad.astype(F32), rows - 1, 0)
        mgs[:, 0:q, cols] = jnp.where(last_col, 0.0, grad).astype(BF16).reshape(per, q, CHUNK)
        rim = rim_up[:, :, cols].astype(F32).reshape(per * 16, CHUNK) * back[0:1, cols] + back[1:2, cols]
        rim = rim + rim_normed[:, :, cols].astype(F32).reshape(per * 16, CHUNK) * back[2:3, cols]
        rim = jnp.where(below, rim, 0.0).astype(BF16)
        mg[:, q:ext, cols] = rim.reshape(per, 16, CHUNK)
        rim = pltpu.roll(rim.astype(F32), per * 16 - 1, 0)
        mgs[:, q:ext, cols] = jnp.where(last_rim, 0.0, rim).astype(BF16).reshape(per, 16, CHUNK)
        views = [ref[:, top : top + q, cols].reshape(rows, CHUNK) for top in (0, 16) for ref in (mg, mgs)]
        plans = (
            (0, ((1, 1, 0),)),
            (1, ((1, 2, 0), (1, 0, 1))),
            (2, ((2, 1, 0), (0, 1, 2))),
            (3, ((2, 2, 0), (2, 0, 1), (0, 2, 2), (0, 0, 3))),
        )
        for plane, taps in plans:
            total = None
            for row, col, view in taps:
                part = dot_nt(views[view], wbd[row * 3 + col, :, cols])
                total = part if total is None else total + part
            normed = pre[:, plane, :, cols].reshape(rows, CHUNK) * coef[0:1, cols] + coef[1:2, cols]
            half = normed * coef[2:3, cols] + coef[3:4, cols]
            th = jnp.tanh(half)
            act = (half + half * th).astype(BF16)
            total = total * slope_twice(half, th)
            up[:, plane, :, cols] = total.reshape(per, q, CHUNK).astype(BF16)
            acc[0:8, cols] += fold(total)
            acc[8:16, cols] += fold(total * normed)
            for row, col, view in taps:
                acc_g[row * 3 + col, :, cols] += dot_tn(act, views[view])

    @pl.when(step == pl.num_programs(0) - 1)
    def _():
        sums_out(ex[0], acc[0:8, :], acc[8:16, :])
        one = Exchange(ex)
        one.start()
        group = (lax.broadcasted_iota(jnp.int32, (32, width), 1) % CHUNK) // 32
        for tap in range(9):
            total = jnp.zeros((32, width), F32)
            for g in range(CHUNK // 32):
                total = total + jnp.where(group == g, acc_g[tap, g * 32 : (g + 1) * 32, :], 0.0)
            g_mid[tap] = total.astype(BF16)
        one.turn()
        one.finish(totals, [coef], [coef6, grads])


def first_grad(up, pre, coef, back, cols):
    normed = pre[:, cols] * coef[0:1, cols] + coef[1:2, cols]
    down = up[:, cols].astype(F32) * back[0:1, cols] + back[1:2, cols]
    return (down + normed * back[2:3, cols]).astype(BF16)


def first_back_body(hook, up, pre, coef, back, xp, g_near, g_far, acc):
    hook(-1)
    step, steps = pl.program_id(0), pl.num_programs(0) // 2

    @pl.when(lax.rem(step, steps) == 0)
    def _():
        acc[...] = jnp.zeros_like(acc)

    hook(0)
    for c in range(0, up.shape[1], CHUNK):
        cols = slice(c, c + CHUNK)
        acc[:, cols] += dot_tn(xp[...], first_grad(up, pre, coef, back, cols))

    @pl.when(step == steps - 1)
    def _():
        g_near[...] = acc[...].astype(BF16)

    @pl.when(step == 2 * steps - 1)
    def _():
        g_far[...] = acc[...].astype(BF16)


def image_back_body(per, px, q, hook, up, pre, coef, back, w1, sg, ws, out, fg, w1t, wst):
    hook(-1)
    step = pl.program_id(0)

    @pl.when(step == 0)
    def _():
        for c in range(0, w1.shape[0], CHUNK):
            cols = slice(c, c + CHUNK)
            w1t[:, cols] = w1[cols, :].T
            wst[:, cols] = ws[cols, :].T

    hook(0)
    for c in range(0, up.shape[1], CHUNK):
        cols = slice(c, c + CHUNK)
        fg[:, cols] = first_grad(up, pre, coef, back, cols)
    for c in range(0, w1.shape[0], CHUNK):
        cols = slice(c, c + CHUNK)
        side_back = dot(sg[...], wst[:, cols])
        part = dot(fg[...], w1t[:, cols])
        for k in range(per):
            even = part[k * px : k * px + q] + side_back[k * q : (k + 1) * q]
            out[k * px : k * px + q, cols] = even.astype(BF16)
            out[k * px + q : (k + 1) * px, cols] = part[k * px + q : (k + 1) * px].astype(BF16)


def place_body(px, planes, last, side, near, far, taps, wide_g, mid_g, first_g, *refs):
    out, last_out, side_out, first_out, taps_out = refs[:5]
    perm = refs[-1]

    @pl.when(pl.program_id(0) == 0)
    def _():
        perm[...] = planes_matrix(out.shape[1], out.shape[2], True)
        taps_out[...] = taps[...].astype(F32)
        rows = [first_g[1:2], first_g[0:1], mid_g[1:2], mid_g[0:1], wide_g[1:2], wide_g[0:1]]
        for ref, row in zip(refs[5:-1], rows + [wide_g[2:3], wide_g[0:1]]):
            ref[...] = row.reshape(ref.shape)

    for k in range(out.shape[0]):
        part = dot(perm[...], planes[k * px : (k + 1) * px, :]).astype(BF16)
        out[k] = part.reshape(out.shape[1:])
    last_out[...] = last[...].astype(F32)
    side_out[...] = side[...].astype(F32)
    half = near.shape[1]
    first_out[:, :half] = near[...].astype(F32)
    first_out[:, half:] = far[...].astype(F32)


def digit(axis, bit):
    return lax.rem(lax.div(lax.axis_index(axis), 1 << bit), 2)


def peer(axis, bit):
    batch, height = lax.axis_index("batch"), lax.axis_index("height")
    move = (1 - 2 * digit(axis, bit)) * (1 << bit)
    return (batch + move, height) if axis == "batch" else (batch, height + move)


def orders():
    bits_b = lax.axis_size("batch").bit_length() - 1
    bits_h = lax.axis_size("height").bit_length() - 1
    across = [("batch", k) for k in range(1, bits_b)]
    half = len(across) // 2
    x_bits, y_bits = across[:half], across[half:]
    z_bits = [("height", k) for k in range(bits_h)]
    return [x_bits + y_bits + z_bits, y_bits + x_bits + z_bits]


def stage_count():
    return len(orders()[0])


def lengths(rows):
    kept = [rows]
    for _ in range(stage_count()):
        kept.append(kept[-1] // 2 if kept[-1] % 32 == 0 else kept[-1])
    return kept


def landing(rows):
    return sum(lengths(rows)[1:])


def upper_lower():
    batch, height = lax.axis_index("batch"), lax.axis_index("height")
    size = lax.axis_size("height")
    return [(batch, lax.rem(height + 1, size)), (batch, lax.rem(height + size - 1, size))]


def partners():
    return [peer("batch", 0)] + [peer(axis, bit) for axis, bit in orders()[0]]


def remote(src, dst, send, recv, target):
    return pltpu.make_async_remote_copy(
        src_ref=src,
        dst_ref=dst,
        send_sem=send,
        recv_sem=recv,
        device_id=target,
        device_id_type=pl.DeviceIdType.MESH,
    )


class Flow:
    def __init__(self, rows, width, own, got, send, recv):
        self.own, self.got, self.send, self.recv = own, got, send, recv
        self.kept = lengths(rows)
        self.orders = orders()
        self.cols = [slice(0, width // 2), slice(width // 2, width)]
        self.low = []
        for order in self.orders:
            low = [0]
            for s, (axis, bit) in enumerate(order):
                move = digit(axis, bit) * self.kept[s + 1] if self.halved(s) else 0
                low.append(low[-1] + move)
            self.low.append(low)

    def halved(self, s):
        return self.kept[s + 1] < self.kept[s]

    def rows(self, first, count):
        return pl.ds(pl.multiple_of(first, 16), count)

    def keep(self, k, s):
        return self.rows(self.low[k][s], self.kept[s])

    def away(self, k, s):
        if not self.halved(s):
            return self.keep(k, s)
        axis, bit = self.orders[k][s]
        return self.rows(self.low[k][s] + (1 - digit(axis, bit)) * self.kept[s + 1], self.kept[s + 1])

    def place(self, s):
        return pl.ds(sum(self.kept[1 : s + 1]), self.kept[s + 1])

    def scatter(self, k, s):
        return remote(
            self.own.at[self.away(k, s), self.cols[k]],
            self.got.at[self.place(s), self.cols[k]],
            self.send.at[0, k, s],
            self.recv.at[0, k, s],
            peer(*self.orders[k][s]),
        )

    def scatter_start(self, s):
        for k in range(2):
            self.scatter(k, s).start()

    def scatter_finish(self, s):
        for k in range(2):
            self.scatter(k, s).wait()
            rows, cols = self.keep(k, s + 1), self.cols[k]
            total = self.own[rows, cols].astype(F32) + self.got[self.place(s), cols].astype(F32)
            self.own[rows, cols] = total.astype(BF16)

    def gather(self, k, s, rows):
        return remote(
            self.own.at[rows, self.cols[k]],
            self.own.at[rows, self.cols[k]],
            self.send.at[1, k, s],
            self.recv.at[1, k, s],
            peer(*self.orders[k][s]),
        )

    def gather_start(self, s):
        for k in range(2):
            if self.halved(s):
                self.gather(k, s, self.keep(k, s + 1)).start()

    def gather_finish(self, s):
        for k in range(2):
            if self.halved(s):
                self.gather(k, s, self.keep(k, s + 1)).wait_send()
                self.gather(k, s, self.away(k, s)).wait_recv()

    def moves(self, s, hbm, sems, out):
        copies = []
        for k in range(2):
            here = self.own.at[self.keep(k, s), self.cols[k]]
            there = hbm.at[self.keep(k, s), self.cols[k]]
            copies.append(pltpu.make_async_copy(*((here, there) if out else (there, here)), sems.at[k]))
        return copies


def run(copies, what):
    for copy in copies:
        getattr(copy, what)()


def own_half(ref):
    half = ref.shape[0] // 2
    return ref.at[pl.ds(pl.multiple_of(lax.axis_index("batch") % 2 * half, 16), half)]


def other_half(ref):
    half = ref.shape[0] // 2
    return ref.at[pl.ds(pl.multiple_of((1 - lax.axis_index("batch") % 2) * half, 16), half)]


def add_into(ref, other, step=64):
    for first in range(0, ref.shape[0], step):
        rows = slice(first, min(first + step, ref.shape[0]))
        ref[rows, :] = (ref[rows, :].astype(F32) + other[rows, :].astype(F32)).astype(BF16)


def carrying(body, counts, carry):
    def kernel(*refs):
        groups, first = [], 0
        for count in counts:
            groups.append(refs[first : first + count])
            first += count
        ins, c_ins, outs, c_outs, scr = groups
        c_scr = refs[first:]
        step = pl.program_id(0)
        points, last = carry(c_ins, c_outs, c_scr, outs)

        def hook(point):
            for (when, where), action in points:
                if where == point:
                    pl.when(step == when)(action)

        body(hook, *ins, *outs, *scr)
        for action in last:
            pl.when(step == pl.num_programs(0) - 1)(action)

    return kernel


def carry_mid(c_ins, c_outs, c_scr, outs):
    (g_last,) = c_ins
    (state_last,) = c_outs
    own, got, tmp, local, core, send, recv = c_scr
    flow = Flow(own.shape[0], own.shape[1], own, got, send, recv)
    load = pltpu.make_async_copy(own_half(g_last), own, local.at[0])
    copy = remote(other_half(g_last), tmp, core.at[0], core.at[1], peer("batch", 0))

    def start():
        load.start()
        signal_all()

    def enter():
        wait_all()
        copy.start()

    def first():
        load.wait()
        copy.wait()
        add_into(own, tmp)
        flow.scatter_start(0)

    def finish():
        flow.scatter_finish(0)
        dumps = flow.moves(1, state_last, local, True)
        run(dumps, "start")
        run(dumps, "wait")

    return [((0, -1), start), ((0, 0), enter), ((3, 0), first)], [finish]


def inner_stages(flow, done, first, until):
    stages = stage_count()

    def down(s):
        def action():
            flow.scatter_finish(s)
            if s + 1 < stages:
                flow.scatter_start(s + 1)
                return
            for k in range(2):
                rows = flow.keep(k, stages)
                done.own[rows, flow.cols[k]] = flow.own[rows, flow.cols[k]]
            done.gather_start(s)

        return action

    def back(s):
        def action():
            done.gather_finish(s)
            if s > until:
                done.gather_start(s - 1)

        return action

    return [down(s) for s in range(first, stages)] + [back(s) for s in range(stages - 1, until - 1, -1)]


def carry_conv(c_ins, c_outs, c_scr, outs):
    state_last, g_side = c_ins
    part_last, state_side = c_outs
    own_l, got_l, full_l, own_s, got_s, tmp, local, core, send_l, recv_l, send_s, recv_s = c_scr
    rows, width = own_l.shape
    last = Flow(rows, width, own_l, got_l, send_l, recv_l)
    done = Flow(rows, width, full_l, None, send_l, recv_l)
    side = Flow(rows, width, own_s, got_s, send_s, recv_s)
    loads = last.moves(1, state_last, local, False)
    load = pltpu.make_async_copy(own_half(g_side), own_s, local.at[2])
    copy = remote(other_half(g_side), tmp, core.at[0], core.at[1], peer("batch", 0))
    inner = inner_stages(last, done, 1, 2)

    def start():
        run(loads, "start")
        load.start()
        signal_all()

    def enter():
        wait_all()
        run(loads, "wait")
        last.scatter_start(1)
        copy.start()

    def first_side():
        load.wait()
        copy.wait()
        add_into(own_s, tmp)
        side.scatter_start(0)

    def next_side(s):
        def action():
            side.scatter_finish(s)
            side.scatter_start(s + 1)

        return action

    def finish():
        side.scatter_finish(1)
        dumps = done.moves(2, part_last, local, True)
        dumps += side.moves(2, state_side, local.at[pl.ds(2, 2)], True)
        run(dumps, "start")
        run(dumps, "wait")

    points = [((0, -1), start), ((0, 0), enter), ((1, 0), first_side)]
    places = [(1, 2), (3, 0), (4, 1), (5, 2)]
    points += [(places[min(k, 3)], act) for k, act in enumerate(inner[:-1])]
    points += [((4, 0), next_side(0))]
    return points, [inner[-1], finish]


class Halves:
    def __init__(self, array, own, tmp, sems, core):
        mine, wide = lax.axis_index("batch") % 2, own.shape[1]
        self.own, self.tmp, self.rows = own, tmp, array.shape[0]
        self.cols = pl.ds(pl.multiple_of(mine * wide, LANES), wide)
        away = pl.ds(pl.multiple_of((1 - mine) * wide, LANES), wide)
        rows = slice(0, self.rows)
        self.load = pltpu.make_async_copy(array.at[:, self.cols], own.at[rows], sems.at[0])
        self.mate = remote(
            array.at[:, away], tmp.at[rows], core.at[0], core.at[1], peer("batch", 0)
        )

    def clear(self):
        left = (self.own.shape[0] - self.rows, self.own.shape[1])
        if left[0]:
            self.own[self.rows :, :] = jnp.zeros(left, BF16)
            self.tmp[self.rows :, :] = jnp.zeros(left, BF16)

    def add(self):
        self.load.wait()
        self.mate.wait()
        add_into(self.own, self.tmp)


def ends(src, dst, sem, core):
    return [
        pltpu.make_async_copy(src, dst, sem),
        remote(src, dst, core.at[0], core.at[1], peer("batch", 0)),
    ]


def carry_first(c_ins, c_outs, c_scr, outs):
    part_last, state_side = c_ins
    half_last, part_side, state_near = c_outs
    own_l, own_s, got_s, full_s, local, send_l, recv_l, send_s, recv_s = c_scr[:9]
    own_h, got_h, tmp_h, core, send_h, recv_h = c_scr[9:]
    rows, width = own_l.shape
    last = Flow(rows, width, own_l, None, send_l, recv_l)
    side = Flow(rows, width, own_s, got_s, send_s, recv_s)
    done_s = Flow(rows, width, full_s, None, send_s, recv_s)
    head = Flow(own_h.shape[0], own_h.shape[1], own_h, got_h, send_h, recv_h)
    inner = inner_stages(side, done_s, 2, 3)
    loads = last.moves(2, part_last, local, False)
    loads += side.moves(2, state_side, local.at[pl.ds(2, 2)], False)
    load = pltpu.make_async_copy(own_half(outs[0]), own_h, local.at[4])
    copy = remote(other_half(outs[0]), tmp_h, core.at[0], core.at[1], peer("batch", 0))

    def start():
        run(loads, "start")
        signal(partners())

    def enter():
        wait_partners()
        run(loads, "wait")
        last.gather_start(1)
        side.scatter_start(2)

    def next_last():
        last.gather_finish(1)
        last.gather_start(0)

    def head_core():
        load.start()
        copy.start()

    def head_first():
        load.wait()
        copy.wait()
        add_into(own_h, tmp_h)
        head.scatter_start(0)

    def finish():
        last.gather_finish(0)
        head.scatter_finish(0)
        dumps = last.moves(0, half_last, local, True)
        dumps += done_s.moves(3, part_side, local.at[pl.ds(2, 2)], True)
        dumps += head.moves(1, state_near, local.at[pl.ds(4, 2)], True)
        run(dumps, "start")
        run(dumps, "wait")

    points = [((0, -1), start), ((0, 0), enter), ((3, 0), next_last)]
    points += [((min(4 + 4 * k, 8), 0), act) for k, act in enumerate(inner[:-1])]
    points += [((6, 0), head_core), ((8, 0), head_first)]
    return points, [inner[-1], finish]


def carry_image(c_ins, c_outs, c_scr, outs):
    half_last, part_side, g_mid, state_near, g_far = c_ins
    all_last, all_side, all_near, all_far, all_mid = c_outs
    own_l, own_s, own_m, got_m, tmp_m, full_m, tmp_h, local, core = c_scr[:9]
    send_s, recv_s, send_m, recv_m = c_scr[9:13]
    near, got_n, full_n, send_n, recv_n = c_scr[13:18]
    far, got_f, full_f, send_f, recv_f = c_scr[18:]

    def pair(own, got, full, send, recv):
        first = Flow(own.shape[0], own.shape[1], own, got, send, recv)
        return first, Flow(own.shape[0], own.shape[1], full, None, send, recv)

    side = Flow(own_s.shape[0], own_s.shape[1], own_s, None, send_s, recv_s)
    flow_n, done_n = pair(near, got_n, full_n, send_n, recv_n)
    flow_f, done_f = pair(far, got_f, full_f, send_f, recv_f)
    flow_m, done_m = pair(own_m, got_m, full_m, send_m, recv_m)
    halves = Halves(g_mid, own_m, tmp_m, local.at[pl.ds(5, 1)], core.at[pl.ds(6, 2)])
    load_l = pltpu.make_async_copy(half_last, own_l, local.at[0])
    load_f = pltpu.make_async_copy(own_half(g_far), far, local.at[9])
    copy = remote(other_half(g_far), tmp_h, core.at[0], core.at[1], peer("batch", 0))
    loads = side.moves(3, part_side, local.at[pl.ds(3, 2)], False)
    loads += flow_n.moves(1, state_near, local.at[pl.ds(7, 2)], False)
    few = slice(0, all_mid.shape[0])
    ends_last = ends(own_l, own_half(all_last), local.at[1], core.at[pl.ds(2, 2)])
    ends_side = ends(own_s, own_half(all_side), local.at[3], core.at[pl.ds(4, 2)])
    ends_n = ends(full_n, own_half(all_near), local.at[7], core.at[pl.ds(8, 2)])
    ends_f = ends(full_f, own_half(all_far), local.at[9], core.at[pl.ds(10, 2)])
    ends_m = ends(full_m.at[few], all_mid.at[:, halves.cols], local.at[5], core.at[pl.ds(12, 2)])

    def start():
        run(loads + [load_l, load_f, halves.load], "start")
        halves.clear()
        signal(partners())

    def enter():
        wait_partners()
        copy.start()
        halves.mate.start()
        run(loads, "wait")
        flow_n.scatter_start(1)
        side.gather_start(2)

    def first():
        load_f.wait()
        copy.wait()
        add_into(far, tmp_h)
        flow_f.scatter_start(0)
        halves.add()
        flow_m.scatter_start(0)
        load_l.wait()
        run(ends_last, "start")

    def side_next(s):
        def action():
            side.gather_finish(s)
            if s:
                side.gather_start(s - 1)
            else:
                run(ends_side, "start")

        return action

    def chain(flow, done, stage, end):
        actions = inner_stages(flow, done, stage, 0)
        return actions + [lambda: run(end, "start")]

    def both(one, two):
        def action():
            one()
            two()

        return action

    def finish():
        for end in (ends_last, ends_side, ends_n, ends_f, ends_m):
            run(end, "wait")

    chain_n = chain(flow_n, done_n, 1, ends_n)
    chain_f = chain(flow_f, done_f, 0, ends_f)
    chain_m = chain(flow_m, done_m, 0, ends_m)
    chain_f = [both(one, two) for one, two in zip(chain_f, chain_m)]
    points = [((0, -1), start), ((0, 0), enter), ((1, 0), first)]
    points += [((2 + 2 * k, 0), act) for k, act in enumerate(chain_n[:5])]
    points += [((3 + 2 * k, 0), act) for k, act in enumerate(chain_f[:5])]
    points += [((3, 0), side_next(2)), ((6, 0), side_next(1))]
    tail, rest_n, rest_f = [], chain_n[5:], chain_f[5:]
    for k in range(max(len(rest_n), len(rest_f))):
        tail += rest_n[k : k + 1] + rest_f[k : k + 1]
        if k == 1:
            tail.append(side_next(0))
    return points, tail + [finish]


def per_device(
    images,
    w_first,
    gain_first,
    shift_first,
    w_mid,
    gain_mid,
    shift_mid,
    w_last,
    gain_last,
    shift_last,
    w_side,
    gain_side,
    shift_side,
    cotangent,
):
    n, rows_in, cols_in, cin = images.shape
    mid = w_first.shape[1]
    wide = w_last.shape[1]
    gw = w_mid.shape[2]
    rows_out, cols_out = rows_in // 2, cols_in // 2
    px, q = rows_in * cols_in, rows_out * cols_out
    devices = lax.axis_size("batch") * lax.axis_size("height")
    cells_in = float(n * px * devices)
    cells_out = float(n * q * devices)
    size_h = lax.axis_size("height")
    per = 4
    steps = n // per
    rows = per * q

    anywhere = pl.BlockSpec(memory_space=pl.ANY)
    dma = pltpu.SemaphoreType.DMA
    halo_x = lax.ppermute(images[:, rows_in - 1], "height", [(i, i + 1) for i in range(size_h - 1)])
    taps = w_mid.reshape(9, gw, mid)
    size_p = per * cols_in

    eights, wide_eights = whole((8, mid)), whole((8, wide))
    def early(s):
        return jnp.minimum(s, steps - 1)

    def late(s):
        return jnp.maximum(s - steps, 0)

    def early_rows(count, cols):
        return pl.BlockSpec((count, cols), lambda s: (early(s), 0))

    def late_rows(count, cols):
        return pl.BlockSpec((count, cols), lambda s: (late(s), 0))

    xp, pre, side_pre, coef1, side_stat = call(
        functools.partial(
            first_body, per, px, q, functools.partial(first_totals, cells_in, mid)
        ),
        "first_product",
        (2 * steps,),
        [
            pl.BlockSpec((per, rows_in, cols_in, cin), lambda s: (early(s), 0, 0, 0)),
            whole((cin, mid)),
            whole((cin, wide)),
            whole((mid,)),
            whole((mid,)),
        ],
        [
            early_rows(per * px, cin),
            early_rows(per * px, mid),
            late_rows(rows, wide),
            eights,
            whole((2 * wide // LANES, LANES)),
        ],
        [
            shape((n * px, cin), BF16),
            shape((n * px, mid)),
            shape((n * q, wide)),
            shape((8, mid)),
            shape((2 * wide // LANES, LANES)),
        ],
        [pltpu.VMEM((16, mid), F32), pltpu.VMEM((16, wide), F32), pltpu.VMEM((px, px), BF16)]
        + [pltpu.VMEM((n * q, cin), BF16)]
        + exchange_scratch(2 * mid // LANES),
        flops=2 * n * (px * cin * (mid + px) + q * cin * wide),
        moved=n * px * cin * 8 + n * q * wide * 4 + cin * (mid + wide) * 2,
        ident=6,
    )(images, w_first, w_side, gain_first, shift_first)

    pre_planes = pre.reshape(n, 4, q, mid)
    planes_spec = pl.BlockSpec((per, 4, q, mid), lambda s: (s, 0, 0, 0))
    mid_pre, coef2, side_coef = call(
        functools.partial(conv_body, per, px, q, functools.partial(mid_totals, cells_out, mid, wide)),
        "grouped_conv",
        (steps,),
        [
            planes_spec,
            pl.BlockSpec((per, cols_in, cin), lambda s: (s, 0, 0)),
            whole((cin, mid)),
            eights,
            whole((9, gw, mid)),
            whole((mid,)),
            whole((mid,)),
            whole((2 * wide // LANES, LANES)),
        ],
        [rows_spec(rows, mid), eights, wide_eights],
        [shape((n * q, mid)), shape((8, mid)), shape((8, wide))],
        [
            pltpu.VMEM((per, q, mid), BF16),
            pltpu.VMEM((per, q, mid), BF16),
            pltpu.VMEM((per, q + 16, mid), BF16),
            pltpu.VMEM((per, q + 16, mid), BF16),
            pltpu.VMEM((9, CHUNK, mid), BF16),
            pltpu.VMEM((size_p, size_p), BF16),
            pltpu.VMEM((16, mid), F32),
        ]
        + exchange_scratch(2 * (mid + wide) // LANES),
        flops=2 * n * q * mid * CHUNK * 9 + 2 * n * cols_in * cin * mid,
        moved=n * px * mid * 4 + n * q * mid * 4,
        ident=0,
    )(pre_planes, halo_x, w_first, coef1, taps, gain_mid, shift_mid, side_stat)

    rim_spec = pl.BlockSpec((per, cols_out, mid), lambda s: (s, 0, 0))
    rim_shape = shape((n, cols_out, mid), BF16)
    mid_act, last_pre, coef3, rim_own = call(
        functools.partial(last_body, per, q, functools.partial(last_totals, cells_out, wide)),
        "last_product",
        (steps,),
        [rows_spec(rows, mid), eights, whole((mid, wide))] + [whole((wide,))] * 4 + [wide_eights],
        [rows_spec(rows, mid), rows_spec(rows, wide), wide_eights, rim_spec],
        [shape((n * q, mid), BF16), shape((n * q, wide)), shape((8, wide)), rim_shape],
        [pltpu.VMEM((16, wide), F32)] + exchange_scratch(2 * wide // LANES),
        flops=2 * n * q * mid * wide,
        moved=n * q * (mid * 6 + wide * 4),
        ident=7,
    )(mid_pre, coef2, w_last, gain_last, shift_last, gain_side, shift_side, side_coef)

    cot = cotangent.reshape(n * q, wide)
    stat_rows = 3 * wide // LANES
    output, stat = call(
        out_body,
        "output",
        (steps,),
        [rows_spec(rows, wide), rows_spec(rows, wide), rows_spec(rows, wide), wide_eights],
        [rows_spec(rows, wide), whole((stat_rows, LANES))],
        [shape((n * q, wide), BF16), shape((stat_rows, LANES))],
        [pltpu.VMEM((24, wide), F32)],
        flops=30 * n * q * wide,
        moved=n * q * wide * 12,
    )(last_pre, side_pre, cot, coef3)

    xp_planes = xp.reshape(n, 4, q, cin)
    half_l = mid // 2
    stages = stage_count()
    sems = dma((2, 2, stages))
    state = shape((half_l, wide), BF16)
    buf = pltpu.VMEM((half_l, wide), BF16)
    got = pltpu.VMEM((landing(half_l), wide), BF16)
    last_grad, side_grad, g_last, wide_grads, rim_normed = call(
        functools.partial(last_grad_body, functools.partial(out_totals, cells_out, wide)),
        "last_gradients",
        (steps,),
        [
            rows_spec(rows, wide),
            rows_spec(rows, wide),
            rows_spec(rows, wide),
            wide_eights,
            rows_spec(rows, mid),
            whole((stat_rows, LANES)),
            anywhere,
        ],
        [rows_spec(rows, wide), rows_spec(rows, wide), whole((mid, wide)), wide_eights, anywhere],
        [
            shape((n * q, wide), BF16),
            shape((n * q, wide), BF16),
            shape((mid, wide), BF16),
            shape((8, wide)),
            rim_shape,
        ],
        [pltpu.VMEM((mid, wide), F32), pltpu.VMEM((8, wide), F32), dma, dma]
        + exchange_scratch(stat_rows),
        flops=2 * n * q * mid * wide,
        moved=n * q * (wide * 14 + mid * 2) + mid * wide * 2,
        ident=3,
    )(last_pre, side_pre, cot, coef3, mid_act, stat, rim_own)
    rims = [pltpu.VMEM((n, cols_out, mid), BF16), dma((steps,)), dma((steps,))]
    inner_scratch = exchange_scratch(2 * mid // LANES)
    mid_up, coef5, mid_grads, rim_up, g_side, state_last = call(
        carrying(
            functools.partial(mid_back_body, per, q, functools.partial(inner_totals, cells_out, mid)),
            (6, 1, 5, 1, 5 + len(inner_scratch)),
            carry_mid,
        ),
        "mid_back",
        (2 * steps,),
        [
            early_rows(rows, wide),
            whole((mid, wide)),
            early_rows(rows, mid),
            eights,
            late_rows(rows, wide),
            pl.BlockSpec((per, 1, q, cin), lambda s: (late(s), 0, 0, 0)),
            anywhere,
        ],
        [early_rows(rows, mid), eights, eights, anywhere, whole((cin, wide)), anywhere],
        [
            shape((n * q, mid)),
            shape((8, mid)),
            shape((8, mid)),
            rim_shape,
            shape((cin, wide), BF16),
            state,
        ],
        [pltpu.VMEM((16, mid), F32), pltpu.VMEM((cin, wide), F32)]
        + rims
        + inner_scratch
        + [buf, got, buf, dma((2,)), dma((2,)), sems, sems],
        flops=2 * n * q * (mid + cin) * wide,
        moved=n * q * (wide * 4 + mid * 10) + mid * wide * 4,
        ident=9,
    )(last_grad, w_last, mid_pre, coef2, side_grad, xp_planes, g_last)

    first_up, g_mid, coef6, first_grads, part_last, state_side = call(
        carrying(
            functools.partial(
                conv_back_body, per, px, q, functools.partial(inner_totals, cells_in, mid)
            ),
            (9, 2, 4, 2, 5 + len(inner_scratch)),
            carry_conv,
        ),
        "grouped_conv_back",
        (steps,),
        [
            rows_spec(rows, mid),
            rows_spec(rows, mid),
            rim_spec,
            rim_spec,
            planes_spec,
            eights,
            eights,
            eights,
            whole((9, gw, mid)),
            anywhere,
            anywhere,
        ],
        [planes_spec, whole((9, gw, mid)), eights, eights, anywhere, anywhere],
        [
            shape((n, 4, q, mid), BF16),
            shape((9, gw, mid), BF16),
            shape((8, mid)),
            shape((8, mid)),
            state,
            state,
        ],
        [
            pltpu.VMEM((per, q + 16, mid), BF16),
            pltpu.VMEM((per, q + 16, mid), BF16),
            pltpu.VMEM((16, mid), F32),
            pltpu.VMEM((9, CHUNK, mid), F32),
            pltpu.VMEM((9, CHUNK, mid), BF16),
        ]
        + inner_scratch
        + [buf, got, buf, buf, got, buf, dma((4,)), dma((2,))]
        + [sems] * 4,
        flops=4 * n * q * mid * CHUNK * 9,
        moved=n * q * mid * 8 + n * px * mid * 6,
        vmem=60,
        ident=10,
    )(
        mid_up,
        mid_pre,
        rim_up,
        rim_normed,
        pre_planes,
        coef2,
        coef5,
        coef1,
        taps,
        state_last,
        g_side,
    )

    flat_up = first_up.reshape(n * px, mid)
    few = per // 2
    half_m = mid // 2
    half_h = cin // 2
    kept_h = shape((half_h, half_m), BF16)
    buf_h = pltpu.VMEM((half_h, half_m), BF16)
    got_h = pltpu.VMEM((landing(half_h), half_m), BF16)
    part_spec = pl.BlockSpec((per * px, half_m), lambda s: (lax.rem(s, steps), lax.div(s, steps)))
    rows_part = pl.BlockSpec((8, half_m), lambda s: (0, lax.div(s, steps)))
    g_near, g_far, half_last, part_side, state_near = call(
        carrying(first_back_body, (5, 2, 2, 3, 1), carry_first),
        "first_gradient",
        (2 * steps,),
        [
            part_spec,
            part_spec,
            rows_part,
            rows_part,
            pl.BlockSpec((per * px, cin), lambda s: (lax.rem(s, steps), 0)),
            anywhere,
            anywhere,
        ],
        [whole((cin, half_m)), whole((cin, half_m))] + [anywhere] * 3,
        [shape((cin, half_m), BF16), shape((cin, half_m), BF16), state, state, kept_h],
        [pltpu.VMEM((cin, half_m), F32), buf, buf, got, buf, dma((6,))]
        + [sems] * 4
        + [buf_h, got_h, buf_h, dma((2,)), sems, sems],
        flops=2 * n * px * mid * cin,
        moved=n * px * (mid * 6 + cin * 4),
        ident=11,
    )(flat_up, pre, coef1, coef6, xp, part_last, state_side)

    unit = 16 * (devices // 2)
    taps_rows = -(-9 * gw // unit) * unit
    buf_m = pltpu.VMEM((taps_rows, half_m), BF16)
    got_m = pltpu.VMEM((landing(taps_rows), half_m), BF16)
    planes, all_last, all_side, all_near, all_far, all_mid = call(
        carrying(functools.partial(image_back_body, few, px, q), (7, 5, 1, 5, 3), carry_image),
        "image_gradient",
        (n // few,),
        [
            rows_spec(few * px, mid),
            rows_spec(few * px, mid),
            eights,
            eights,
            whole((cin, mid)),
            rows_spec(few * q, wide),
            whole((cin, wide)),
        ]
        + [anywhere] * 5,
        [rows_spec(few * px, cin)] + [anywhere] * 5,
        [
            shape((n * px, cin), BF16),
            shape((mid, wide), BF16),
            shape((cin, wide), BF16),
            shape((cin, half_m), BF16),
            shape((cin, half_m), BF16),
            shape((9 * gw, mid), BF16),
        ],
        [
            pltpu.VMEM((few * px, mid), BF16),
            pltpu.VMEM((mid, cin), BF16),
            pltpu.VMEM((wide, cin), BF16),
        ]
        + [buf, buf, buf_m, got_m, buf_m, buf_m, buf_h]
        + [dma((10,)), dma((14,))]
        + [sems] * 4
        + [buf_h, got_h, buf_h, sems, sems] * 2,
        flops=2 * n * px * cin * mid + 2 * n * q * cin * wide,
        moved=n * px * (mid * 6 + cin * 2) + n * q * wide * 2,
        ident=12,
    )(
        flat_up,
        pre,
        coef1,
        coef6,
        w_first,
        side_grad,
        w_side,
        half_last,
        part_side,
        g_mid.reshape(9 * gw, mid),
        state_near,
        g_far,
    )
    three = 3
    cuts = n // three
    vectors = [mid] * 4 + [wide] * 4
    grad_images, grad_last, grad_side, grad_first, grad_mid, *grad_vectors = call(
        functools.partial(place_body, px),
        "image_places",
        (cuts,),
        [
            rows_spec(three * px, cin),
            rows_spec(mid // cuts, wide),
            rows_spec(cin // cuts, wide),
            rows_spec(cin // cuts, half_m),
            rows_spec(cin // cuts, half_m),
            whole((9 * gw, mid)),
            wide_eights,
            eights,
            eights,
        ],
        [
            pl.BlockSpec((three, rows_in, cols_in, cin), lambda s: (s, 0, 0, 0)),
            rows_spec(mid // cuts, wide),
            rows_spec(cin // cuts, wide),
            rows_spec(cin // cuts, mid),
            whole((9 * gw, mid)),
        ]
        + [whole((k,)) for k in vectors],
        [
            shape((n, rows_in, cols_in, cin), BF16),
            shape((mid, wide)),
            shape((cin, wide)),
            shape((cin, mid)),
            shape((9 * gw, mid)),
        ]
        + [shape((k,)) for k in vectors],
        [pltpu.VMEM((px, px), BF16)],
        flops=2 * n * px * cin * px,
        moved=n * px * cin * 4 + (mid + cin) * wide * 6 + cin * mid * 6,
    )(planes, all_last, all_side, all_near, all_far, all_mid, wide_grads, mid_grads, first_grads)

    return (
        output.reshape(n, rows_out, cols_out, wide),
        grad_images,
        grad_first,
        grad_vectors[0],
        grad_vectors[1],
        grad_mid.reshape(3, 3, gw, mid),
        grad_vectors[2],
        grad_vectors[3],
        grad_last,
        grad_vectors[4],
        grad_vectors[5],
        grad_side,
        grad_vectors[6],
        grad_vectors[7],
    )


def solution(mesh):
    split = P("batch", "height", None, None)
    in_specs = (split,) + (P(),) * 12 + (split,)
    out_specs = (split, split) + (P(),) * 12
    return jax.shard_map(
        per_device, mesh=mesh, in_specs=in_specs, out_specs=out_specs, check_vma=False
    )
```

```python
import functools

import jax
import jax.numpy as jnp
from jax import lax
from jax.experimental import pallas as pl
from jax.experimental.pallas import tpu as pltpu
from jax.sharding import PartitionSpec as P

EPSILON = 1e-05
LANES = 128
CHUNK = 256
BF16 = jnp.bfloat16
F32 = jnp.float32
MIB = 1 << 20


def dot(a, b):
    return jnp.dot(a, b, preferred_element_type=F32)


def dot_nt(a, b):
    return lax.dot_general(a, b, (((1,), (1,)), ((), ())), preferred_element_type=F32)


def dot_tn(a, b):
    return lax.dot_general(a, b, (((0,), (0,)), ((), ())), preferred_element_type=F32)


def fold(values):
    rows, cols = values.shape
    return jnp.sum(values.reshape(rows // 8, 8, cols), axis=0)


def put_row(ref, first, row):
    for k in range(row.shape[1] // LANES):
        ref[first + k : first + k + 1, :] = row[:, k * LANES : (k + 1) * LANES]


def get_row(values, first, width):
    count = width // LANES
    return jnp.concatenate([values[first + k : first + k + 1, :] for k in range(count)], axis=1)


def sums_out(ref, *partials):
    first = 0
    for part in partials:
        row = jnp.sum(part, axis=0, keepdims=True)
        put_row(ref, first, row)
        first += row.shape[1] // LANES


def whole(shape):
    return pl.BlockSpec(shape, lambda *_: (0,) * len(shape), pipeline_mode=pl.Buffered(1))


def rows_spec(rows, cols):
    return pl.BlockSpec((rows, cols), lambda i: (i, 0))


def call(
    body, name, grid, in_specs, out_specs, out_shape, scratch=(), flops=0, moved=0, vmem=56, ident=None
):
    return pl.pallas_call(
        body,
        name=name,
        grid=grid,
        in_specs=in_specs,
        out_specs=out_specs,
        out_shape=out_shape,
        scratch_shapes=list(scratch),
        compiler_params=pltpu.CompilerParams(
            vmem_limit_bytes=vmem * MIB, collective_id=ident, has_side_effects=ident is not None
        ),
        cost_estimate=pl.CostEstimate(flops=flops, bytes_accessed=moved, transcendentals=0),
    )


def shape(dims, kind=F32):
    return jax.ShapeDtypeStruct(dims, kind)


def everyone():
    batch, height = lax.axis_index("batch"), lax.axis_index("height")
    size_b, size_h = lax.axis_size("batch"), lax.axis_size("height")
    row = [(lax.rem(batch + k, size_b), height) for k in range(1, size_b)]
    return row, [(batch, lax.rem(height + k, size_h)) for k in range(1, size_h)]


def signal(peers):
    barrier = pltpu.get_barrier_semaphore()
    for one in peers:
        pl.semaphore_signal(barrier, inc=1, device_id=one, device_id_type=pl.DeviceIdType.MESH)


def signal_all():
    row, column = everyone()
    signal(row + column)


def wait_all():
    row, column = everyone()
    pl.semaphore_wait(pltpu.get_barrier_semaphore(), len(row + column))


def wait_partners():
    pl.semaphore_wait(pltpu.get_barrier_semaphore(), len(partners()))


def greet(peers):
    signal(peers)
    pl.semaphore_wait(pltpu.get_barrier_semaphore(), len(peers))


def exchange_scratch(rows):
    size_b, size_h = lax.axis_size("batch"), lax.axis_size("height")
    dma = pltpu.SemaphoreType.DMA
    return [
        pltpu.VMEM((rows, LANES), F32),
        pltpu.VMEM((size_b, rows, LANES), F32),
        pltpu.VMEM((size_h, rows, LANES), F32),
        dma((size_b - 1,)),
        dma((size_b,)),
        dma((size_h - 1,)),
        dma((size_h,)),
    ]


class Exchange:
    def __init__(self, scratch):
        self.stat, self.got_b, self.got_h, self.send_b, self.recv_b, self.send_h, self.recv_h = scratch
        self.me_b, self.me_h = lax.axis_index("batch"), lax.axis_index("height")
        self.row, self.column = everyone()

    def spread(self, src, got, me, targets, send, recv):
        return [
            remote(src, got.at[me], send.at[k], recv.at[me], target) for k, target in enumerate(targets)
        ]

    def total(self, src, got, me, targets, send, recv):
        size = got.shape[0]
        for k, target in enumerate(targets):
            other = lax.rem(me + (size - 1 - k), size)
            remote(src, got.at[other], send.at[k], recv.at[other], target).wait_recv()
        total = got[0]
        for k in range(1, size):
            total = total + got[k]
        return total

    def over_batch(self):
        return self.stat, self.got_b, self.me_b, self.row, self.send_b, self.recv_b

    def over_height(self):
        return self.got_h.at[self.me_h], self.got_h, self.me_h, self.column, self.send_h, self.recv_h

    def start(self):
        run(self.spread(*self.over_batch()), "start")
        self.got_b[self.me_b] = self.stat[...]

    def turn(self):
        self.got_h[self.me_h] = self.total(*self.over_batch())
        run(self.spread(*self.over_height()), "start")

    def finish(self, epilogue, params, outs):
        epilogue(self.total(*self.over_height()), params, outs)
        run(self.spread(*self.over_batch()) + self.spread(*self.over_height()), "wait_send")


def exchange(scratch, epilogue, params, outs):
    one = Exchange(scratch)
    one.start()
    one.turn()
    one.finish(epilogue, params, outs)


def norm_terms(total, first, width, cells):
    average = get_row(total, first, width) * (1.0 / cells)
    meansq = get_row(total, first + width // LANES, width) * (1.0 / cells)
    inverse = lax.rsqrt(meansq - average * average + EPSILON)
    return inverse, -average * inverse


def fill(ref, rows):
    for k, row in enumerate(rows):
        ref[k : k + 1, :] = row
    ref[len(rows) :, :] = jnp.zeros((8 - len(rows), ref.shape[1]), F32)


def act_rows(inverse, offset, gain, shift):
    return [
        inverse,
        offset,
        0.5 * gain,
        0.5 * shift,
        0.5 * gain * inverse,
        0.5 * (shift + gain * offset),
    ]


def first_totals(cells_in, width, total, params, outs):
    gain, shift = as_row(params[0]), as_row(params[1])
    fill(outs[0], act_rows(*norm_terms(total, 0, width, cells_in), gain, shift))


def mid_totals(cells_out, width, wide, total, params, outs):
    gain, shift = as_row(params[0]), as_row(params[1])
    fill(outs[0], act_rows(*norm_terms(total, 0, width, cells_out), gain, shift))
    fill(outs[1], list(norm_terms(total, 2 * width // LANES, wide, cells_out)))


def last_totals(cells_out, wide, total, params, outs):
    gain_last, shift_last, gain_side, shift_side, side = params
    inverse, offset = norm_terms(total, 0, wide, cells_out)
    inverse_s, offset_s = side[0:1, :], side[1:2, :]
    gain_l, gain_s = 0.5 * as_row(gain_last), 0.5 * as_row(gain_side)
    shift = 0.5 * (as_row(shift_last) + as_row(shift_side))
    scales = [gain_l * inverse, gain_s * inverse_s, gain_l * offset + gain_s * offset_s + shift]
    fill(outs[0], [inverse, offset, inverse_s, offset_s] + scales)


def back_rows(scale, total_up, cross, cells):
    return [0.5 * scale, -scale * total_up * (1.0 / cells), -scale * cross * (1.0 / cells)]


def folded(rows, inverse, offset):
    scale, base, cross = rows
    return [scale, cross * inverse, base + cross * offset]


def out_totals(cells_out, wide, total, params, outs):
    coef = params[0]
    step = wide // LANES
    total_up, last_raw, side_raw = [0.5 * get_row(total, k * step, wide) for k in range(3)]
    inverse_l, offset_l, inverse_s, offset_s = [coef[k : k + 1, :] for k in range(4)]
    last_cross = inverse_l * last_raw + offset_l * total_up
    side_cross = inverse_s * side_raw + offset_s * total_up
    rows_l = back_rows(2.0 * coef[4:5, :], total_up, last_cross, cells_out)
    rows_s = back_rows(2.0 * coef[5:6, :], total_up, side_cross, cells_out)
    fill(outs[0], folded(rows_l, inverse_l, offset_l) + folded(rows_s, inverse_s, offset_s))
    fill(outs[1], [total_up, last_cross, side_cross])


def inner_totals(cells, width, total, params, outs):
    coef = params[0]
    total_up = 0.5 * get_row(total, 0, width)
    cross = 0.5 * get_row(total, width // LANES, width)
    fill(outs[0], back_rows(2.0 * coef[4:5, :], total_up, cross, cells))
    fill(outs[1], [total_up, cross])


def half_silu(half):
    return half + half * jnp.tanh(half)


def slope_twice(half, th):
    return (1.0 + th) * (1.0 + half * (1.0 - th))


def to_neighbour(copies, moves_up, what):
    height, size = lax.axis_index("height"), lax.axis_size("height")
    sends = height > 0 if moves_up else height < size - 1
    gets = height < size - 1 if moves_up else height > 0
    if what == "start":
        pl.when(sends)(lambda: run(copies, "start"))
    else:
        pl.when(sends)(lambda: run(copies, "wait_send"))
        pl.when(gets)(lambda: run(copies, "wait_recv"))


def planes_matrix(rows, cols, inverse):
    px, q, half = rows * cols, rows * cols // 4, cols // 2
    place = lax.broadcasted_iota(jnp.int32, (px, px), 1 if inverse else 0)
    pixel = lax.broadcasted_iota(jnp.int32, (px, px), 0 if inverse else 1)
    plane, inner = place // q, place % q
    source = (2 * (inner // half) + plane // 2) * cols + 2 * (inner % half) + plane % 2
    return (source == pixel).astype(F32).astype(BF16)


def row_matrix(count, cols):
    size, half = count * cols, cols // 2
    place = lax.broadcasted_iota(jnp.int32, (size, size), 0)
    pixel = lax.broadcasted_iota(jnp.int32, (size, size), 1)
    source = place // cols * cols + 2 * (place % half) + place % cols // half
    return (source == pixel).astype(F32).astype(BF16)


def spread_weights(w, out):
    gw, width = w.shape[1], w.shape[2]
    group = (lax.broadcasted_iota(jnp.int32, (gw, width), 1) % CHUNK) // gw
    for tap in range(9):
        rows = w[tap].astype(F32)
        for g in range(CHUNK // gw):
            out[tap, g * gw : (g + 1) * gw, :] = jnp.where(group == g, rows, 0.0).astype(BF16)


def as_row(ref):
    return ref[...].reshape(1, ref.shape[0])


def first_body(
    per, px, q, totals, img, w1, ws, gain, shift, xp, pre, side, coef, side_stat, acc, acc_s, perm, evens, *ex
):
    step, steps = pl.program_id(0), pl.num_programs(0) // 2
    mid, wide = w1.shape[1], ws.shape[1]
    rows = per * q

    @pl.when(step == 0)
    def _():
        acc[...] = jnp.zeros_like(acc)
        acc_s[...] = jnp.zeros_like(acc_s)
        perm[...] = planes_matrix(img.shape[1], img.shape[2], False)
        signal_all()

    @pl.when(step < steps)
    def _():
        for k in range(per):
            flat = img[k].reshape(px, img.shape[3])
            xp[k * px : (k + 1) * px, :] = dot(perm[...], flat).astype(BF16)
        even = jnp.concatenate([xp[k * px : k * px + q, :] for k in range(per)], axis=0)
        evens[pl.ds(pl.multiple_of(step * rows, 16), rows), :] = even
        for c in range(0, mid, CHUNK):
            cols = slice(c, c + CHUNK)
            part = dot(xp[...], w1[:, cols])
            pre[:, cols] = part
            acc[0:8, cols] += fold(part)
            acc[8:16, cols] += fold(part * part)

    @pl.when(step == steps)
    def _():
        sums_out(ex[0], acc[0:8, :], acc[8:16, :])
        wait_all()
        Exchange(ex).start()

    @pl.when(step == steps + 2)
    def _():
        Exchange(ex).turn()

    @pl.when(step >= steps)
    def _():
        even = evens[pl.ds(pl.multiple_of((step - steps) * rows, 16), rows), :]
        for c in range(0, wide, CHUNK):
            cols = slice(c, c + CHUNK)
            part = dot(even, ws[:, cols])
            side[:, cols] = part
            acc_s[0:8, cols] += fold(part)
            acc_s[8:16, cols] += fold(part * part)

    @pl.when(step == pl.num_programs(0) - 1)
    def _():
        sums_out(side_stat, acc_s[0:8, :], acc_s[8:16, :])
        Exchange(ex).finish(totals, [gain, shift], [coef])


def conv_body(
    per, px, q, totals, pre, halo, w1, coef, w, gain, shift, side_stat, mid, coef2, side_coef, *scr
):
    a00, a01, a10, a11, wbd, perm, acc, *ex = scr
    step = pl.program_id(0)
    width = w1.shape[1]

    @pl.when(step == 0)
    def _():
        acc[...] = jnp.zeros_like(acc)
        spread_weights(w, wbd)
        perm[...] = row_matrix(per, halo.shape[1])
        signal_all()

    scale, offset = coef[4:5, :], coef[5:6, :]
    flat = halo[...].reshape(per * 32, halo.shape[2])
    rim = half_silu(dot(dot(perm[...], flat).astype(BF16), w1[...]) * scale + offset)
    rim = jnp.where(lax.axis_index("height") > 0, rim, 0.0).astype(BF16)
    rim = rim.reshape(per, 2, 16, width)
    a10[:, 0:16, :] = rim[:, 0]
    a11[:, 0:16, :] = rim[:, 1]
    for plane, ref, top in ((0, a00, 0), (1, a01, 0), (2, a10, 16), (3, a11, 16)):
        half = pre[:, plane] * scale[None] + offset[None]
        ref[:, top : top + q, :] = half_silu(half).astype(BF16)
    rows = per * q
    first_col = lax.broadcasted_iota(jnp.int32, (rows, CHUNK), 0) % 16 == 0
    for c in range(0, width, CHUNK):
        cols = slice(c, c + CHUNK)

        def tap(ref, top, row, col):
            return dot(ref[:, top : top + q, cols].reshape(rows, CHUNK), wbd[row * 3 + col, :, cols])

        straight = (
            tap(a00, 0, 1, 1)
            + tap(a01, 0, 1, 2)
            + tap(a10, 16, 2, 1)
            + tap(a11, 16, 2, 2)
            + tap(a10, 0, 0, 1)
            + tap(a11, 0, 0, 2)
        )
        moved = tap(a01, 0, 1, 0) + tap(a11, 16, 2, 0) + tap(a11, 0, 0, 0)
        part = straight + jnp.where(first_col, 0.0, pltpu.roll(moved, 1, 0))
        mid[:, cols] = part
        acc[0:8, cols] += fold(part)
        acc[8:16, cols] += fold(part * part)

    @pl.when(step == pl.num_programs(0) - 1)
    def _():
        sums_out(ex[0], acc[0:8, :], acc[8:16, :])
        ex[0][2 * width // LANES :, :] = side_stat[...]
        wait_all()
        exchange(ex, totals, [gain, shift], [coef2, side_coef])


def last_body(per, q, totals, mid, coef, w, gl, sl, gs, ss, side_coef, act, pre, coef3, rim, acc, *ex):
    step = pl.program_id(0)
    width = mid.shape[1]

    @pl.when(step == 0)
    def _():
        acc[...] = jnp.zeros_like(acc)
        signal_all()

    top = mid[...].reshape(per, q, width)[:, 0:16] * coef[0:1, :][None] + coef[1:2, :][None]
    rim[...] = top.astype(BF16)
    half = mid[...] * coef[4:5, :] + coef[5:6, :]
    act[...] = half_silu(half).astype(BF16)
    for c in range(0, w.shape[1], CHUNK):
        cols = slice(c, c + CHUNK)
        part = dot(act[...], w[:, cols])
        pre[:, cols] = part
        acc[0:8, cols] += fold(part)
        acc[8:16, cols] += fold(part * part)

    @pl.when(step == pl.num_programs(0) - 1)
    def _():
        sums_out(ex[0], acc[0:8, :], acc[8:16, :])
        wait_all()
        exchange(ex, totals, [gl, sl, gs, ss, side_coef], [coef3])


def rim_copy(rim, halo, per, step, send, recv):
    images = pl.ds(step * per, per)
    return remote(rim.at[images], halo.at[images], send.at[step], recv.at[step], upper_lower()[1])


def rim_finish(rim, halo, per, send, recv):
    copies = [rim_copy(rim, halo, per, s, send, recv) for s in range(rim.shape[0] // per)]
    to_neighbour(copies, True, "wait")


def out_parts(last, side, cot, coef, cols):
    half = last[:, cols] * coef[4:5, cols] + side[:, cols] * coef[5:6, cols] + coef[6:7, cols]
    th = jnp.tanh(half)
    moved = half * th
    up = cot[:, cols].astype(F32) * ((1.0 + th) * (1.0 + (half - moved)))
    return half + moved, up


def out_body(last, side, cot, coef, out, stat, acc):
    step = pl.program_id(0)

    @pl.when(step == 0)
    def _():
        acc[...] = jnp.zeros_like(acc)

    for c in range(0, last.shape[1], CHUNK):
        cols = slice(c, c + CHUNK)
        value, up = out_parts(last, side, cot, coef, cols)
        out[:, cols] = value.astype(BF16)
        acc[0:8, cols] += fold(up)
        acc[8:16, cols] += fold(up * last[:, cols])
        acc[16:24, cols] += fold(up * side[:, cols])

    @pl.when(step == pl.num_programs(0) - 1)
    def _():
        sums_out(stat, acc[0:8, :], acc[8:16, :], acc[16:24, :])


def last_grad_body(totals, last, side, cot, coef, act, stat, rim, lg, sg, g_last, grads, halo, *scr):
    acc, back, send, recv, *ex = scr
    step = pl.program_id(0)
    row = remote(rim, halo, send, recv, upper_lower()[1])

    @pl.when(step == 0)
    def _():
        signal_all()
        acc[...] = jnp.zeros_like(acc)
        ex[0][...] = stat[...]
        wait_all()
        exchange(ex, totals, [coef], [back, grads])
        to_neighbour([row], True, "start")

    for c in range(0, last.shape[1], CHUNK):
        cols = slice(c, c + CHUNK)
        _, part = out_parts(last, side, cot, coef, cols)
        down = part * back[0:1, cols] + last[:, cols] * back[1:2, cols] + back[2:3, cols]
        down = down.astype(BF16)
        lg[:, cols] = down
        acc[:, cols] += dot_tn(act[...], down)
        down = part * back[3:4, cols] + side[:, cols] * back[4:5, cols] + back[5:6, cols]
        sg[:, cols] = down.astype(BF16)

    @pl.when(step == pl.num_programs(0) - 1)
    def _():
        g_last[...] = acc[...].astype(BF16)
        to_neighbour([row], True, "wait")


def mid_back_body(
    per, q, totals, hook, lg, wl, mid, coef, sg, even, up, coef5, grads, halo, g_side, *scr
):
    acc, acc_s, rim, send, recv, *ex = scr
    step, steps = pl.program_id(0), pl.num_programs(0) // 2
    hook(-1)

    @pl.when(step == 0)
    def _():
        acc[...] = jnp.zeros_like(acc)
        acc_s[...] = jnp.zeros_like(acc_s)

    hook(0)

    @pl.when(step < steps)
    def _():
        for c in range(0, mid.shape[1], CHUNK):
            cols = slice(c, c + CHUNK)
            part = dot_nt(lg[...], wl[cols, :])
            normed = mid[:, cols] * coef[0:1, cols] + coef[1:2, cols]
            half = normed * coef[2:3, cols] + coef[3:4, cols]
            part = part * slope_twice(half, jnp.tanh(half))
            up[:, cols] = part
            rim[pl.ds(step * per, per), :, cols] = part.reshape(per, q, CHUNK)[:, 0:16].astype(BF16)
            acc[0:8, cols] += fold(part)
            acc[8:16, cols] += fold(part * normed)
        to_neighbour([rim_copy(rim, halo, per, step, send, recv)], True, "start")

    @pl.when(step == steps)
    def _():
        sums_out(ex[0], acc[0:8, :], acc[8:16, :])
        Exchange(ex).start()

    @pl.when(step >= steps)
    def _():
        flat = even[...].reshape(per * q, even.shape[3])
        for c in range(0, sg.shape[1], CHUNK):
            cols = slice(c, c + CHUNK)
            acc_s[:, cols] += dot_tn(flat, sg[:, cols])

    @pl.when(step == pl.num_programs(0) - 1)
    def _():
        one = Exchange(ex)
        one.turn()
        g_side[...] = acc_s[...].astype(BF16)
        one.finish(totals, [coef], [coef5, grads])
        rim_finish(rim, halo, per, send, recv)


def conv_back_body(
    per, px, q, totals, hook, mup, mid, rim_up, rim_normed, pre, coef2, back, coef, w, *refs
):
    up, g_mid, coef6, grads, mg, mgs, acc, acc_g, wbd, *ex = refs
    hook(-1)
    step = pl.program_id(0)
    width = mid.shape[1]
    rows = per * q

    @pl.when(step == 0)
    def _():
        acc[...] = jnp.zeros_like(acc)
        acc_g[...] = jnp.zeros_like(acc_g)
        spread_weights(w, wbd)

    ext = q + 16
    below = lax.axis_index("height") < lax.axis_size("height") - 1
    last_col = lax.broadcasted_iota(jnp.int32, (rows, CHUNK), 0) % 16 == 15
    last_rim = lax.broadcasted_iota(jnp.int32, (per * 16, CHUNK), 0) % 16 == 15
    for c in range(0, width, CHUNK):
        cols = slice(c, c + CHUNK)
        hook(c // CHUNK)
        normed = mid[:, cols] * coef2[0:1, cols] + coef2[1:2, cols]
        grad = (mup[:, cols] * back[0:1, cols] + back[1:2, cols] + normed * back[2:3, cols]).astype(BF16)
        mg[:, 0:q, cols] = grad.reshape(per, q, CHUNK)
        grad = pltpu.roll(grad.astype(F32), rows - 1, 0)
        mgs[:, 0:q, cols] = jnp.where(last_col, 0.0, grad).astype(BF16).reshape(per, q, CHUNK)
        rim = rim_up[:, :, cols].astype(F32).reshape(per * 16, CHUNK) * back[0:1, cols] + back[1:2, cols]
        rim = rim + rim_normed[:, :, cols].astype(F32).reshape(per * 16, CHUNK) * back[2:3, cols]
        rim = jnp.where(below, rim, 0.0).astype(BF16)
        mg[:, q:ext, cols] = rim.reshape(per, 16, CHUNK)
        rim = pltpu.roll(rim.astype(F32), per * 16 - 1, 0)
        mgs[:, q:ext, cols] = jnp.where(last_rim, 0.0, rim).astype(BF16).reshape(per, 16, CHUNK)
        views = [ref[:, top : top + q, cols].reshape(rows, CHUNK) for top in (0, 16) for ref in (mg, mgs)]
        plans = (
            (0, ((1, 1, 0),)),
            (1, ((1, 2, 0), (1, 0, 1))),
            (2, ((2, 1, 0), (0, 1, 2))),
            (3, ((2, 2, 0), (2, 0, 1), (0, 2, 2), (0, 0, 3))),
        )
        for plane, taps in plans:
            total = None
            for row, col, view in taps:
                part = dot_nt(views[view], wbd[row * 3 + col, :, cols])
                total = part if total is None else total + part
            normed = pre[:, plane, :, cols].reshape(rows, CHUNK) * coef[0:1, cols] + coef[1:2, cols]
            half = normed * coef[2:3, cols] + coef[3:4, cols]
            th = jnp.tanh(half)
            act = (half + half * th).astype(BF16)
            total = total * slope_twice(half, th)
            up[:, plane, :, cols] = total.reshape(per, q, CHUNK).astype(BF16)
            acc[0:8, cols] += fold(total)
            acc[8:16, cols] += fold(total * normed)
            for row, col, view in taps:
                acc_g[row * 3 + col, :, cols] += dot_tn(act, views[view])

    @pl.when(step == pl.num_programs(0) - 1)
    def _():
        sums_out(ex[0], acc[0:8, :], acc[8:16, :])
        one = Exchange(ex)
        one.start()
        group = (lax.broadcasted_iota(jnp.int32, (32, width), 1) % CHUNK) // 32
        for tap in range(9):
            total = jnp.zeros((32, width), F32)
            for g in range(CHUNK // 32):
                total = total + jnp.where(group == g, acc_g[tap, g * 32 : (g + 1) * 32, :], 0.0)
            g_mid[tap] = total.astype(BF16)
        one.turn()
        one.finish(totals, [coef], [coef6, grads])


def first_grad(up, pre, coef, back, cols):
    normed = pre[:, cols] * coef[0:1, cols] + coef[1:2, cols]
    down = up[:, cols].astype(F32) * back[0:1, cols] + back[1:2, cols]
    return (down + normed * back[2:3, cols]).astype(BF16)


def first_back_body(hook, up, pre, coef, back, xp, g_near, g_far, acc):
    hook(-1)
    step, steps = pl.program_id(0), pl.num_programs(0) // 2

    @pl.when(lax.rem(step, steps) == 0)
    def _():
        acc[...] = jnp.zeros_like(acc)

    hook(0)
    for c in range(0, up.shape[1], CHUNK):
        cols = slice(c, c + CHUNK)
        acc[:, cols] += dot_tn(xp[...], first_grad(up, pre, coef, back, cols))

    @pl.when(step == steps - 1)
    def _():
        g_near[...] = acc[...].astype(BF16)

    @pl.when(step == 2 * steps - 1)
    def _():
        g_far[...] = acc[...].astype(BF16)


def image_back_body(per, px, q, hook, up, pre, coef, back, w1, sg, ws, out, fg, w1t, wst):
    hook(-1)
    step = pl.program_id(0)

    @pl.when(step == 0)
    def _():
        for c in range(0, w1.shape[0], CHUNK):
            cols = slice(c, c + CHUNK)
            w1t[:, cols] = w1[cols, :].T
            wst[:, cols] = ws[cols, :].T

    hook(0)
    for c in range(0, up.shape[1], CHUNK):
        cols = slice(c, c + CHUNK)
        fg[:, cols] = first_grad(up, pre, coef, back, cols)
    for c in range(0, w1.shape[0], CHUNK):
        cols = slice(c, c + CHUNK)
        side_back = dot(sg[...], wst[:, cols])
        part = dot(fg[...], w1t[:, cols])
        for k in range(per):
            even = part[k * px : k * px + q] + side_back[k * q : (k + 1) * q]
            out[k * px : k * px + q, cols] = even.astype(BF16)
            out[k * px + q : (k + 1) * px, cols] = part[k * px + q : (k + 1) * px].astype(BF16)


def place_body(px, planes, last, side, near, far, taps, wide_g, mid_g, first_g, *refs):
    out, last_out, side_out, first_out, taps_out = refs[:5]
    perm = refs[-1]

    @pl.when(pl.program_id(0) == 0)
    def _():
        perm[...] = planes_matrix(out.shape[1], out.shape[2], True)
        taps_out[...] = taps[...].astype(F32)
        rows = [first_g[1:2], first_g[0:1], mid_g[1:2], mid_g[0:1], wide_g[1:2], wide_g[0:1]]
        for ref, row in zip(refs[5:-1], rows + [wide_g[2:3], wide_g[0:1]]):
            ref[...] = row.reshape(ref.shape)

    for k in range(out.shape[0]):
        part = dot(perm[...], planes[k * px : (k + 1) * px, :]).astype(BF16)
        out[k] = part.reshape(out.shape[1:])
    last_out[...] = last[...].astype(F32)
    side_out[...] = side[...].astype(F32)
    half = near.shape[1]
    first_out[:, :half] = near[...].astype(F32)
    first_out[:, half:] = far[...].astype(F32)


def digit(axis, bit):
    return lax.rem(lax.div(lax.axis_index(axis), 1 << bit), 2)


def peer(axis, bit):
    batch, height = lax.axis_index("batch"), lax.axis_index("height")
    move = (1 - 2 * digit(axis, bit)) * (1 << bit)
    return (batch + move, height) if axis == "batch" else (batch, height + move)


def orders():
    bits_b = lax.axis_size("batch").bit_length() - 1
    bits_h = lax.axis_size("height").bit_length() - 1
    across = [("batch", k) for k in range(1, bits_b)]
    half = len(across) // 2
    x_bits, y_bits = across[:half], across[half:]
    z_bits = [("height", k) for k in range(bits_h)]
    return [x_bits + y_bits + z_bits, y_bits + x_bits + z_bits]


def stage_count():
    return len(orders()[0])


def lengths(rows):
    kept = [rows]
    for _ in range(stage_count()):
        kept.append(kept[-1] // 2 if kept[-1] % 32 == 0 else kept[-1])
    return kept


def landing(rows):
    return sum(lengths(rows)[1:])


def upper_lower():
    batch, height = lax.axis_index("batch"), lax.axis_index("height")
    size = lax.axis_size("height")
    return [(batch, lax.rem(height + 1, size)), (batch, lax.rem(height + size - 1, size))]


def partners():
    return [peer("batch", 0)] + [peer(axis, bit) for axis, bit in orders()[0]]


def remote(src, dst, send, recv, target):
    return pltpu.make_async_remote_copy(
        src_ref=src,
        dst_ref=dst,
        send_sem=send,
        recv_sem=recv,
        device_id=target,
        device_id_type=pl.DeviceIdType.MESH,
    )


class Flow:
    def __init__(self, rows, width, own, got, send, recv):
        self.own, self.got, self.send, self.recv = own, got, send, recv
        self.kept = lengths(rows)
        self.orders = orders()
        self.cols = [slice(0, width // 2), slice(width // 2, width)]
        self.low = []
        for order in self.orders:
            low = [0]
            for s, (axis, bit) in enumerate(order):
                move = digit(axis, bit) * self.kept[s + 1] if self.halved(s) else 0
                low.append(low[-1] + move)
            self.low.append(low)

    def halved(self, s):
        return self.kept[s + 1] < self.kept[s]

    def rows(self, first, count):
        return pl.ds(pl.multiple_of(first, 16), count)

    def keep(self, k, s):
        return self.rows(self.low[k][s], self.kept[s])

    def away(self, k, s):
        if not self.halved(s):
            return self.keep(k, s)
        axis, bit = self.orders[k][s]
        return self.rows(self.low[k][s] + (1 - digit(axis, bit)) * self.kept[s + 1], self.kept[s + 1])

    def place(self, s):
        return pl.ds(sum(self.kept[1 : s + 1]), self.kept[s + 1])

    def scatter(self, k, s):
        return remote(
            self.own.at[self.away(k, s), self.cols[k]],
            self.got.at[self.place(s), self.cols[k]],
            self.send.at[0, k, s],
            self.recv.at[0, k, s],
            peer(*self.orders[k][s]),
        )

    def scatter_start(self, s):
        for k in range(2):
            self.scatter(k, s).start()

    def scatter_finish(self, s):
        for k in range(2):
            self.scatter(k, s).wait()
            rows, cols = self.keep(k, s + 1), self.cols[k]
            total = self.own[rows, cols].astype(F32) + self.got[self.place(s), cols].astype(F32)
            self.own[rows, cols] = total.astype(BF16)

    def gather(self, k, s, rows):
        return remote(
            self.own.at[rows, self.cols[k]],
            self.own.at[rows, self.cols[k]],
            self.send.at[1, k, s],
            self.recv.at[1, k, s],
            peer(*self.orders[k][s]),
        )

    def gather_start(self, s):
        for k in range(2):
            if self.halved(s):
                self.gather(k, s, self.keep(k, s + 1)).start()

    def gather_finish(self, s):
        for k in range(2):
            if self.halved(s):
                self.gather(k, s, self.keep(k, s + 1)).wait_send()
                self.gather(k, s, self.away(k, s)).wait_recv()

    def moves(self, s, hbm, sems, out):
        copies = []
        for k in range(2):
            here = self.own.at[self.keep(k, s), self.cols[k]]
            there = hbm.at[self.keep(k, s), self.cols[k]]
            copies.append(pltpu.make_async_copy(*((here, there) if out else (there, here)), sems.at[k]))
        return copies


def run(copies, what):
    for copy in copies:
        getattr(copy, what)()


def own_half(ref):
    half = ref.shape[0] // 2
    return ref.at[pl.ds(pl.multiple_of(lax.axis_index("batch") % 2 * half, 16), half)]


def other_half(ref):
    half = ref.shape[0] // 2
    return ref.at[pl.ds(pl.multiple_of((1 - lax.axis_index("batch") % 2) * half, 16), half)]


def add_into(ref, other, step=64):
    for first in range(0, ref.shape[0], step):
        rows = slice(first, min(first + step, ref.shape[0]))
        ref[rows, :] = (ref[rows, :].astype(F32) + other[rows, :].astype(F32)).astype(BF16)


def carrying(body, counts, carry):
    def kernel(*refs):
        groups, first = [], 0
        for count in counts:
            groups.append(refs[first : first + count])
            first += count
        ins, c_ins, outs, c_outs, scr = groups
        c_scr = refs[first:]
        step = pl.program_id(0)
        points, last = carry(c_ins, c_outs, c_scr, outs)

        def hook(point):
            for (when, where), action in points:
                if where == point:
                    pl.when(step == when)(action)

        body(hook, *ins, *outs, *scr)
        for action in last:
            pl.when(step == pl.num_programs(0) - 1)(action)

    return kernel


def carry_mid(c_ins, c_outs, c_scr, outs):
    (g_last,) = c_ins
    (state_last,) = c_outs
    own, got, tmp, local, core, send, recv = c_scr
    flow = Flow(own.shape[0], own.shape[1], own, got, send, recv)
    load = pltpu.make_async_copy(own_half(g_last), own, local.at[0])
    copy = remote(other_half(g_last), tmp, core.at[0], core.at[1], peer("batch", 0))

    def start():
        load.start()
        signal_all()

    def enter():
        wait_all()
        copy.start()

    def first():
        load.wait()
        copy.wait()
        add_into(own, tmp)
        flow.scatter_start(0)

    def finish():
        flow.scatter_finish(0)
        dumps = flow.moves(1, state_last, local, True)
        run(dumps, "start")
        run(dumps, "wait")

    return [((0, -1), start), ((0, 0), enter), ((3, 0), first)], [finish]


def inner_stages(flow, done, first, until):
    stages = stage_count()

    def down(s):
        def action():
            flow.scatter_finish(s)
            if s + 1 < stages:
                flow.scatter_start(s + 1)
                return
            for k in range(2):
                rows = flow.keep(k, stages)
                done.own[rows, flow.cols[k]] = flow.own[rows, flow.cols[k]]
            done.gather_start(s)

        return action

    def back(s):
        def action():
            done.gather_finish(s)
            if s > until:
                done.gather_start(s - 1)

        return action

    return [down(s) for s in range(first, stages)] + [back(s) for s in range(stages - 1, until - 1, -1)]


def carry_conv(c_ins, c_outs, c_scr, outs):
    state_last, g_side = c_ins
    part_last, state_side = c_outs
    own_l, got_l, full_l, own_s, got_s, tmp, local, core, send_l, recv_l, send_s, recv_s = c_scr
    rows, width = own_l.shape
    last = Flow(rows, width, own_l, got_l, send_l, recv_l)
    done = Flow(rows, width, full_l, None, send_l, recv_l)
    side = Flow(rows, width, own_s, got_s, send_s, recv_s)
    loads = last.moves(1, state_last, local, False)
    load = pltpu.make_async_copy(own_half(g_side), own_s, local.at[2])
    copy = remote(other_half(g_side), tmp, core.at[0], core.at[1], peer("batch", 0))
    inner = inner_stages(last, done, 1, 2)

    def start():
        run(loads, "start")
        load.start()
        signal_all()

    def enter():
        wait_all()
        run(loads, "wait")
        last.scatter_start(1)
        copy.start()

    def first_side():
        load.wait()
        copy.wait()
        add_into(own_s, tmp)
        side.scatter_start(0)

    def next_side(s):
        def action():
            side.scatter_finish(s)
            side.scatter_start(s + 1)

        return action

    def finish():
        side.scatter_finish(1)
        dumps = done.moves(2, part_last, local, True)
        dumps += side.moves(2, state_side, local.at[pl.ds(2, 2)], True)
        run(dumps, "start")
        run(dumps, "wait")

    points = [((0, -1), start), ((0, 0), enter), ((1, 0), first_side)]
    places = [(1, 2), (3, 0), (4, 1), (5, 2)]
    points += [(places[min(k, 3)], act) for k, act in enumerate(inner[:-1])]
    points += [((4, 0), next_side(0))]
    return points, [inner[-1], finish]


class Halves:
    def __init__(self, array, own, tmp, sems, core):
        mine, wide = lax.axis_index("batch") % 2, own.shape[1]
        self.own, self.tmp, self.rows = own, tmp, array.shape[0]
        self.cols = pl.ds(pl.multiple_of(mine * wide, LANES), wide)
        away = pl.ds(pl.multiple_of((1 - mine) * wide, LANES), wide)
        rows = slice(0, self.rows)
        self.load = pltpu.make_async_copy(array.at[:, self.cols], own.at[rows], sems.at[0])
        self.mate = remote(
            array.at[:, away], tmp.at[rows], core.at[0], core.at[1], peer("batch", 0)
        )

    def clear(self):
        left = (self.own.shape[0] - self.rows, self.own.shape[1])
        if left[0]:
            self.own[self.rows :, :] = jnp.zeros(left, BF16)
            self.tmp[self.rows :, :] = jnp.zeros(left, BF16)

    def add(self):
        self.load.wait()
        self.mate.wait()
        add_into(self.own, self.tmp)


def ends(src, dst, sem, core):
    return [
        pltpu.make_async_copy(src, dst, sem),
        remote(src, dst, core.at[0], core.at[1], peer("batch", 0)),
    ]


def carry_first(c_ins, c_outs, c_scr, outs):
    part_last, state_side = c_ins
    half_last, part_side, state_near = c_outs
    own_l, own_s, got_s, full_s, local, send_l, recv_l, send_s, recv_s = c_scr[:9]
    own_h, got_h, tmp_h, core, send_h, recv_h = c_scr[9:]
    rows, width = own_l.shape
    last = Flow(rows, width, own_l, None, send_l, recv_l)
    side = Flow(rows, width, own_s, got_s, send_s, recv_s)
    done_s = Flow(rows, width, full_s, None, send_s, recv_s)
    head = Flow(own_h.shape[0], own_h.shape[1], own_h, got_h, send_h, recv_h)
    inner = inner_stages(side, done_s, 2, 3)
    loads = last.moves(2, part_last, local, False)
    loads += side.moves(2, state_side, local.at[pl.ds(2, 2)], False)
    load = pltpu.make_async_copy(own_half(outs[0]), own_h, local.at[4])
    copy = remote(other_half(outs[0]), tmp_h, core.at[0], core.at[1], peer("batch", 0))

    def start():
        run(loads, "start")
        signal(partners())

    def enter():
        wait_partners()
        run(loads, "wait")
        last.gather_start(1)
        side.scatter_start(2)

    def next_last():
        last.gather_finish(1)
        last.gather_start(0)

    def head_core():
        load.start()
        copy.start()

    def head_first():
        load.wait()
        copy.wait()
        add_into(own_h, tmp_h)
        head.scatter_start(0)

    def finish():
        last.gather_finish(0)
        head.scatter_finish(0)
        dumps = last.moves(0, half_last, local, True)
        dumps += done_s.moves(3, part_side, local.at[pl.ds(2, 2)], True)
        dumps += head.moves(1, state_near, local.at[pl.ds(4, 2)], True)
        run(dumps, "start")
        run(dumps, "wait")

    points = [((0, -1), start), ((0, 0), enter), ((3, 0), next_last)]
    points += [((min(4 + 4 * k, 8), 0), act) for k, act in enumerate(inner[:-1])]
    points += [((6, 0), head_core), ((8, 0), head_first)]
    return points, [inner[-1], finish]


def carry_image(c_ins, c_outs, c_scr, outs):
    half_last, part_side, g_mid, state_near, g_far = c_ins
    all_last, all_side, all_near, all_far, all_mid = c_outs
    own_l, own_s, own_m, got_m, tmp_m, full_m, tmp_h, local, core = c_scr[:9]
    send_s, recv_s, send_m, recv_m = c_scr[9:13]
    near, got_n, full_n, send_n, recv_n = c_scr[13:18]
    far, got_f, full_f, send_f, recv_f = c_scr[18:]

    def pair(own, got, full, send, recv):
        first = Flow(own.shape[0], own.shape[1], own, got, send, recv)
        return first, Flow(own.shape[0], own.shape[1], full, None, send, recv)

    side = Flow(own_s.shape[0], own_s.shape[1], own_s, None, send_s, recv_s)
    flow_n, done_n = pair(near, got_n, full_n, send_n, recv_n)
    flow_f, done_f = pair(far, got_f, full_f, send_f, recv_f)
    flow_m, done_m = pair(own_m, got_m, full_m, send_m, recv_m)
    halves = Halves(g_mid, own_m, tmp_m, local.at[pl.ds(5, 1)], core.at[pl.ds(6, 2)])
    load_l = pltpu.make_async_copy(half_last, own_l, local.at[0])
    load_f = pltpu.make_async_copy(own_half(g_far), far, local.at[9])
    copy = remote(other_half(g_far), tmp_h, core.at[0], core.at[1], peer("batch", 0))
    loads = side.moves(3, part_side, local.at[pl.ds(3, 2)], False)
    loads += flow_n.moves(1, state_near, local.at[pl.ds(7, 2)], False)
    few = slice(0, all_mid.shape[0])
    ends_last = ends(own_l, own_half(all_last), local.at[1], core.at[pl.ds(2, 2)])
    ends_side = ends(own_s, own_half(all_side), local.at[3], core.at[pl.ds(4, 2)])
    ends_n = ends(full_n, own_half(all_near), local.at[7], core.at[pl.ds(8, 2)])
    ends_f = ends(full_f, own_half(all_far), local.at[9], core.at[pl.ds(10, 2)])
    ends_m = ends(full_m.at[few], all_mid.at[:, halves.cols], local.at[5], core.at[pl.ds(12, 2)])

    def start():
        run(loads + [load_l, load_f, halves.load], "start")
        halves.clear()
        signal(partners())

    def enter():
        wait_partners()
        copy.start()
        halves.mate.start()
        run(loads, "wait")
        flow_n.scatter_start(1)
        side.gather_start(2)

    def first():
        load_f.wait()
        copy.wait()
        add_into(far, tmp_h)
        flow_f.scatter_start(0)
        halves.add()
        flow_m.scatter_start(0)
        load_l.wait()
        run(ends_last, "start")

    def side_next(s):
        def action():
            side.gather_finish(s)
            if s:
                side.gather_start(s - 1)
            else:
                run(ends_side, "start")

        return action

    def chain(flow, done, stage, end):
        actions = inner_stages(flow, done, stage, 0)
        return actions + [lambda: run(end, "start")]

    def both(one, two):
        def action():
            one()
            two()

        return action

    def finish():
        for end in (ends_last, ends_side, ends_n, ends_f, ends_m):
            run(end, "wait")

    chain_n = chain(flow_n, done_n, 1, ends_n)
    chain_f = chain(flow_f, done_f, 0, ends_f)
    chain_m = chain(flow_m, done_m, 0, ends_m)
    chain_f = [both(one, two) for one, two in zip(chain_f, chain_m)]
    points = [((0, -1), start), ((0, 0), enter), ((1, 0), first)]
    points += [((2 + 2 * k, 0), act) for k, act in enumerate(chain_n[:5])]
    points += [((3 + 2 * k, 0), act) for k, act in enumerate(chain_f[:5])]
    points += [((3, 0), side_next(2)), ((6, 0), side_next(1))]
    tail, rest_n, rest_f = [], chain_n[5:], chain_f[5:]
    for k in range(max(len(rest_n), len(rest_f))):
        tail += rest_n[k : k + 1] + rest_f[k : k + 1]
        if k == 1:
            tail.append(side_next(0))
    return points, tail + [finish]


def per_device(
    images,
    w_first,
    gain_first,
    shift_first,
    w_mid,
    gain_mid,
    shift_mid,
    w_last,
    gain_last,
    shift_last,
    w_side,
    gain_side,
    shift_side,
    cotangent,
):
    n, rows_in, cols_in, cin = images.shape
    mid = w_first.shape[1]
    wide = w_last.shape[1]
    gw = w_mid.shape[2]
    rows_out, cols_out = rows_in // 2, cols_in // 2
    px, q = rows_in * cols_in, rows_out * cols_out
    devices = lax.axis_size("batch") * lax.axis_size("height")
    cells_in = float(n * px * devices)
    cells_out = float(n * q * devices)
    size_h = lax.axis_size("height")
    per = 4
    steps = n // per
    rows = per * q

    anywhere = pl.BlockSpec(memory_space=pl.ANY)
    dma = pltpu.SemaphoreType.DMA
    halo_x = lax.ppermute(images[:, rows_in - 1], "height", [(i, i + 1) for i in range(size_h - 1)])
    taps = w_mid.reshape(9, gw, mid)
    size_p = per * cols_in

    eights, wide_eights = whole((8, mid)), whole((8, wide))
    def early(s):
        return jnp.minimum(s, steps - 1)

    def late(s):
        return jnp.maximum(s - steps, 0)

    def early_rows(count, cols):
        return pl.BlockSpec((count, cols), lambda s: (early(s), 0))

    def late_rows(count, cols):
        return pl.BlockSpec((count, cols), lambda s: (late(s), 0))

    xp, pre, side_pre, coef1, side_stat = call(
        functools.partial(
            first_body, per, px, q, functools.partial(first_totals, cells_in, mid)
        ),
        "first_product",
        (2 * steps,),
        [
            pl.BlockSpec((per, rows_in, cols_in, cin), lambda s: (early(s), 0, 0, 0)),
            whole((cin, mid)),
            whole((cin, wide)),
            whole((mid,)),
            whole((mid,)),
        ],
        [
            early_rows(per * px, cin),
            early_rows(per * px, mid),
            late_rows(rows, wide),
            eights,
            whole((2 * wide // LANES, LANES)),
        ],
        [
            shape((n * px, cin), BF16),
            shape((n * px, mid)),
            shape((n * q, wide)),
            shape((8, mid)),
            shape((2 * wide // LANES, LANES)),
        ],
        [pltpu.VMEM((16, mid), F32), pltpu.VMEM((16, wide), F32), pltpu.VMEM((px, px), BF16)]
        + [pltpu.VMEM((n * q, cin), BF16)]
        + exchange_scratch(2 * mid // LANES),
        flops=2 * n * (px * cin * (mid + px) + q * cin * wide),
        moved=n * px * cin * 8 + n * q * wide * 4 + cin * (mid + wide) * 2,
        ident=6,
    )(images, w_first, w_side, gain_first, shift_first)

    pre_planes = pre.reshape(n, 4, q, mid)
    planes_spec = pl.BlockSpec((per, 4, q, mid), lambda s: (s, 0, 0, 0))
    mid_pre, coef2, side_coef = call(
        functools.partial(conv_body, per, px, q, functools.partial(mid_totals, cells_out, mid, wide)),
        "grouped_conv",
        (steps,),
        [
            planes_spec,
            pl.BlockSpec((per, cols_in, cin), lambda s: (s, 0, 0)),
            whole((cin, mid)),
            eights,
            whole((9, gw, mid)),
            whole((mid,)),
            whole((mid,)),
            whole((2 * wide // LANES, LANES)),
        ],
        [rows_spec(rows, mid), eights, wide_eights],
        [shape((n * q, mid)), shape((8, mid)), shape((8, wide))],
        [
            pltpu.VMEM((per, q, mid), BF16),
            pltpu.VMEM((per, q, mid), BF16),
            pltpu.VMEM((per, q + 16, mid), BF16),
            pltpu.VMEM((per, q + 16, mid), BF16),
            pltpu.VMEM((9, CHUNK, mid), BF16),
            pltpu.VMEM((size_p, size_p), BF16),
            pltpu.VMEM((16, mid), F32),
        ]
        + exchange_scratch(2 * (mid + wide) // LANES),
        flops=2 * n * q * mid * CHUNK * 9 + 2 * n * cols_in * cin * mid,
        moved=n * px * mid * 4 + n * q * mid * 4,
        ident=0,
    )(pre_planes, halo_x, w_first, coef1, taps, gain_mid, shift_mid, side_stat)

    rim_spec = pl.BlockSpec((per, cols_out, mid), lambda s: (s, 0, 0))
    rim_shape = shape((n, cols_out, mid), BF16)
    mid_act, last_pre, coef3, rim_own = call(
        functools.partial(last_body, 2 * per, q, functools.partial(last_totals, cells_out, wide)),
        "last_product",
        (steps // 2,),
        [rows_spec(2 * rows, mid), eights, whole((mid, wide))] + [whole((wide,))] * 4 + [wide_eights],
        [rows_spec(2 * rows, mid), rows_spec(2 * rows, wide), wide_eights, pl.BlockSpec((2 * per, cols_out, mid), lambda s: (s, 0, 0))],
        [shape((n * q, mid), BF16), shape((n * q, wide)), shape((8, wide)), rim_shape],
        [pltpu.VMEM((16, wide), F32)] + exchange_scratch(2 * wide // LANES),
        flops=2 * n * q * mid * wide,
        moved=n * q * (mid * 6 + wide * 4),
        ident=7,
    )(mid_pre, coef2, w_last, gain_last, shift_last, gain_side, shift_side, side_coef)

    cot = cotangent.reshape(n * q, wide)
    stat_rows = 3 * wide // LANES
    output, stat = call(
        out_body,
        "output",
        (steps,),
        [rows_spec(rows, wide), rows_spec(rows, wide), rows_spec(rows, wide), wide_eights],
        [rows_spec(rows, wide), whole((stat_rows, LANES))],
        [shape((n * q, wide), BF16), shape((stat_rows, LANES))],
        [pltpu.VMEM((24, wide), F32)],
        flops=30 * n * q * wide,
        moved=n * q * wide * 12,
    )(last_pre, side_pre, cot, coef3)

    xp_planes = xp.reshape(n, 4, q, cin)
    half_l = mid // 2
    stages = stage_count()
    sems = dma((2, 2, stages))
    state = shape((half_l, wide), BF16)
    buf = pltpu.VMEM((half_l, wide), BF16)
    got = pltpu.VMEM((landing(half_l), wide), BF16)
    last_grad, side_grad, g_last, wide_grads, rim_normed = call(
        functools.partial(last_grad_body, functools.partial(out_totals, cells_out, wide)),
        "last_gradients",
        (steps,),
        [
            rows_spec(rows, wide),
            rows_spec(rows, wide),
            rows_spec(rows, wide),
            wide_eights,
            rows_spec(rows, mid),
            whole((stat_rows, LANES)),
            anywhere,
        ],
        [rows_spec(rows, wide), rows_spec(rows, wide), whole((mid, wide)), wide_eights, anywhere],
        [
            shape((n * q, wide), BF16),
            shape((n * q, wide), BF16),
            shape((mid, wide), BF16),
            shape((8, wide)),
            rim_shape,
        ],
        [pltpu.VMEM((mid, wide), F32), pltpu.VMEM((8, wide), F32), dma, dma]
        + exchange_scratch(stat_rows),
        flops=2 * n * q * mid * wide,
        moved=n * q * (wide * 14 + mid * 2) + mid * wide * 2,
        ident=3,
    )(last_pre, side_pre, cot, coef3, mid_act, stat, rim_own)
    rims = [pltpu.VMEM((n, cols_out, mid), BF16), dma((steps,)), dma((steps,))]
    inner_scratch = exchange_scratch(2 * mid // LANES)
    mid_up, coef5, mid_grads, rim_up, g_side, state_last = call(
        carrying(
            functools.partial(mid_back_body, per, q, functools.partial(inner_totals, cells_out, mid)),
            (6, 1, 5, 1, 5 + len(inner_scratch)),
            carry_mid,
        ),
        "mid_back",
        (2 * steps,),
        [
            early_rows(rows, wide),
            whole((mid, wide)),
            early_rows(rows, mid),
            eights,
            late_rows(rows, wide),
            pl.BlockSpec((per, 1, q, cin), lambda s: (late(s), 0, 0, 0)),
            anywhere,
        ],
        [early_rows(rows, mid), eights, eights, anywhere, whole((cin, wide)), anywhere],
        [
            shape((n * q, mid)),
            shape((8, mid)),
            shape((8, mid)),
            rim_shape,
            shape((cin, wide), BF16),
            state,
        ],
        [pltpu.VMEM((16, mid), F32), pltpu.VMEM((cin, wide), F32)]
        + rims
        + inner_scratch
        + [buf, got, buf, dma((2,)), dma((2,)), sems, sems],
        flops=2 * n * q * (mid + cin) * wide,
        moved=n * q * (wide * 4 + mid * 10) + mid * wide * 4,
        ident=9,
    )(last_grad, w_last, mid_pre, coef2, side_grad, xp_planes, g_last)

    first_up, g_mid, coef6, first_grads, part_last, state_side = call(
        carrying(
            functools.partial(
                conv_back_body, per, px, q, functools.partial(inner_totals, cells_in, mid)
            ),
            (9, 2, 4, 2, 5 + len(inner_scratch)),
            carry_conv,
        ),
        "grouped_conv_back",
        (steps,),
        [
            rows_spec(rows, mid),
            rows_spec(rows, mid),
            rim_spec,
            rim_spec,
            planes_spec,
            eights,
            eights,
            eights,
            whole((9, gw, mid)),
            anywhere,
            anywhere,
        ],
        [planes_spec, whole((9, gw, mid)), eights, eights, anywhere, anywhere],
        [
            shape((n, 4, q, mid), BF16),
            shape((9, gw, mid), BF16),
            shape((8, mid)),
            shape((8, mid)),
            state,
            state,
        ],
        [
            pltpu.VMEM((per, q + 16, mid), BF16),
            pltpu.VMEM((per, q + 16, mid), BF16),
            pltpu.VMEM((16, mid), F32),
            pltpu.VMEM((9, CHUNK, mid), F32),
            pltpu.VMEM((9, CHUNK, mid), BF16),
        ]
        + inner_scratch
        + [buf, got, buf, buf, got, buf, dma((4,)), dma((2,))]
        + [sems] * 4,
        flops=4 * n * q * mid * CHUNK * 9,
        moved=n * q * mid * 8 + n * px * mid * 6,
        vmem=60,
        ident=10,
    )(
        mid_up,
        mid_pre,
        rim_up,
        rim_normed,
        pre_planes,
        coef2,
        coef5,
        coef1,
        taps,
        state_last,
        g_side,
    )

    flat_up = first_up.reshape(n * px, mid)
    few = per // 2
    half_m = mid // 2
    half_h = cin // 2
    kept_h = shape((half_h, half_m), BF16)
    buf_h = pltpu.VMEM((half_h, half_m), BF16)
    got_h = pltpu.VMEM((landing(half_h), half_m), BF16)
    part_spec = pl.BlockSpec((per * px, half_m), lambda s: (lax.rem(s, steps), lax.div(s, steps)))
    rows_part = pl.BlockSpec((8, half_m), lambda s: (0, lax.div(s, steps)))
    g_near, g_far, half_last, part_side, state_near = call(
        carrying(first_back_body, (5, 2, 2, 3, 1), carry_first),
        "first_gradient",
        (2 * steps,),
        [
            part_spec,
            part_spec,
            rows_part,
            rows_part,
            pl.BlockSpec((per * px, cin), lambda s: (lax.rem(s, steps), 0)),
            anywhere,
            anywhere,
        ],
        [whole((cin, half_m)), whole((cin, half_m))] + [anywhere] * 3,
        [shape((cin, half_m), BF16), shape((cin, half_m), BF16), state, state, kept_h],
        [pltpu.VMEM((cin, half_m), F32), buf, buf, got, buf, dma((6,))]
        + [sems] * 4
        + [buf_h, got_h, buf_h, dma((2,)), sems, sems],
        flops=2 * n * px * mid * cin,
        moved=n * px * (mid * 6 + cin * 4),
        ident=11,
    )(flat_up, pre, coef1, coef6, xp, part_last, state_side)

    unit = 16 * (devices // 2)
    taps_rows = -(-9 * gw // unit) * unit
    buf_m = pltpu.VMEM((taps_rows, half_m), BF16)
    got_m = pltpu.VMEM((landing(taps_rows), half_m), BF16)
    planes, all_last, all_side, all_near, all_far, all_mid = call(
        carrying(functools.partial(image_back_body, few, px, q), (7, 5, 1, 5, 3), carry_image),
        "image_gradient",
        (n // few,),
        [
            rows_spec(few * px, mid),
            rows_spec(few * px, mid),
            eights,
            eights,
            whole((cin, mid)),
            rows_spec(few * q, wide),
            whole((cin, wide)),
        ]
        + [anywhere] * 5,
        [rows_spec(few * px, cin)] + [anywhere] * 5,
        [
            shape((n * px, cin), BF16),
            shape((mid, wide), BF16),
            shape((cin, wide), BF16),
            shape((cin, half_m), BF16),
            shape((cin, half_m), BF16),
            shape((9 * gw, mid), BF16),
        ],
        [
            pltpu.VMEM((few * px, mid), BF16),
            pltpu.VMEM((mid, cin), BF16),
            pltpu.VMEM((wide, cin), BF16),
        ]
        + [buf, buf, buf_m, got_m, buf_m, buf_m, buf_h]
        + [dma((10,)), dma((14,))]
        + [sems] * 4
        + [buf_h, got_h, buf_h, sems, sems] * 2,
        flops=2 * n * px * cin * mid + 2 * n * q * cin * wide,
        moved=n * px * (mid * 6 + cin * 2) + n * q * wide * 2,
        ident=12,
    )(
        flat_up,
        pre,
        coef1,
        coef6,
        w_first,
        side_grad,
        w_side,
        half_last,
        part_side,
        g_mid.reshape(9 * gw, mid),
        state_near,
        g_far,
    )
    three = 3
    cuts = n // three
    vectors = [mid] * 4 + [wide] * 4
    grad_images, grad_last, grad_side, grad_first, grad_mid, *grad_vectors = call(
        functools.partial(place_body, px),
        "image_places",
        (cuts,),
        [
            rows_spec(three * px, cin),
            rows_spec(mid // cuts, wide),
            rows_spec(cin // cuts, wide),
            rows_spec(cin // cuts, half_m),
            rows_spec(cin // cuts, half_m),
            whole((9 * gw, mid)),
            wide_eights,
            eights,
            eights,
        ],
        [
            pl.BlockSpec((three, rows_in, cols_in, cin), lambda s: (s, 0, 0, 0)),
            rows_spec(mid // cuts, wide),
            rows_spec(cin // cuts, wide),
            rows_spec(cin // cuts, mid),
            whole((9 * gw, mid)),
        ]
        + [whole((k,)) for k in vectors],
        [
            shape((n, rows_in, cols_in, cin), BF16),
            shape((mid, wide)),
            shape((cin, wide)),
            shape((cin, mid)),
            shape((9 * gw, mid)),
        ]
        + [shape((k,)) for k in vectors],
        [pltpu.VMEM((px, px), BF16)],
        flops=2 * n * px * cin * px,
        moved=n * px * cin * 4 + (mid + cin) * wide * 6 + cin * mid * 6,
    )(planes, all_last, all_side, all_near, all_far, all_mid, wide_grads, mid_grads, first_grads)

    return (
        output.reshape(n, rows_out, cols_out, wide),
        grad_images,
        grad_first,
        grad_vectors[0],
        grad_vectors[1],
        grad_mid.reshape(3, 3, gw, mid),
        grad_vectors[2],
        grad_vectors[3],
        grad_last,
        grad_vectors[4],
        grad_vectors[5],
        grad_side,
        grad_vectors[6],
        grad_vectors[7],
    )


def solution(mesh):
    split = P("batch", "height", None, None)
    in_specs = (split,) + (P(),) * 12 + (split,)
    out_specs = (split, split) + (P(),) * 12
    return jax.shard_map(
        per_device, mesh=mesh, in_specs=in_specs, out_specs=out_specs, check_vma=False
    )
```
